128 devices in a mesh: mem: 8 (over y, core), tile: 16 (over z, x).
Axes of the slice: x: 4, y: 4, z: 4, core: 2. Of those that a mesh axis runs over, the one named last changes fastest.
Arguments:
- noisy: bfloat16 [16, 128, 32, 256], P('mem', 'tile'), may hold values from -6 to 6
- timestep: int32 [16], P('mem'), may hold values from 500 to 999
- seams: int32 [128, 4, 3], P('tile'), may hold values from 0 to 127, as said below
- corner_list: int32 [128, 4, 2], P('tile'), may hold values from 0 to 127, as said below
- route: int32 [128, 1], replicated, may hold values from 0 to 15; in each aligned block of 8 rows (0 to 7, 8 to 15, ...) at most 2 rows name the same one
- target_block: int32 [128], replicated, may hold values from 0 to 3
- frac: float32 [128, 2], P('tile'), may hold values from 0.05 to 0.95
- w_time: float32 [128, 128], replicated, may hold values from -0.5 to 0.5
- w_lift: bfloat16 [8, 128], replicated, may hold values from -2 to 2
- w_fine: bfloat16 [9, 128, 128], replicated, may hold values from -0.1875 to 0.1875
- w_coarse: bfloat16 [9, 128, 128], replicated, may hold values from -0.1875 to 0.1875
- gain_fine: float32 [128], replicated, may hold values from 0.1 to 1.9
- gain_coarse: float32 [128], replicated, may hold values from 0.1 to 1.9
- gain_out: float32 [128], replicated, may hold values from 0.1 to 1.9
- w_out: bfloat16 [128, 8], replicated, may hold values from -0.5 to 0.5
Outputs:
- denoised: float32 [16, 128, 32, 256], P('mem', 'tile')
- ens_mean: float32 [64, 32, 256], P('tile')
- ens_spread: float32 [64, 32, 256], P('tile')
The draws below stay inside these ranges and needn't reach their ends.
Inputs may be any that keep to these rules, and one draw needn't show every extreme that they name: seams[t,k] = (neighbour sub-tile, its touching side 0..3, reversal flag 0 or 1), with sub-tiles numbered 8 to an index of tile in order. Every side is paired with exactly one side, symmetrically and with the same reversal flag at both ends: the east side of a sub-tile touches the west side of a sub-tile on the next index of tile (cyclically), and the north side touches the south side of a sub-tile on the same index. corner_list[t,k] = (sub-tile, its corner 0..3), following from seams: corners 0 and 1 are corners 3 and 2 of the north neighbour, corners 2 and 3 are corners 1 and 0 of the south neighbour, each pair swapped where that seam is reversed. `route`: of the sub-tiles of one index of tile, at most 2 go to one owner, and some index sends exactly 2 to some owner.
All inputs are finite; a program needn't handle non-finite values.
Results may differ from the reference program's by a relative error of at most 0.01.
Values may be sent and summed in bfloat16 or wider, within the bound.
A program may use at most 128 MiB of HBM per device.

```python
import math
import jax
import jax.numpy as jnp
import numpy as np
from jax import lax

C = 128
VARS = 8
SUB = 32
TILES_DEV = 8
STEPS = 1000
MEMBERS = 16
TILES = 128
BLK_DEV = 4
BLOCKS = 64
CAP = 2
N_TILE = 16


def local_perms(key, index_count):
    scores = jax.random.randint(key, (index_count, TILES_DEV), 0, 1 << 20, dtype=jnp.int32)
    scores = scores * TILES_DEV + jnp.arange(TILES_DEV, dtype=jnp.int32)[None, :]
    return jnp.argsort(scores, axis=1).astype(jnp.int32)


def side_pairing(key):
    index_count = TILES // TILES_DEV
    key_east, key_north, key_eflip, key_nflip = jax.random.split(key, 4)
    east_perm = local_perms(key_east, index_count)
    north_perm = local_perms(key_north, index_count)
    east_inv = jnp.argsort(east_perm, axis=1).astype(jnp.int32)
    north_inv = jnp.argsort(north_perm, axis=1).astype(jnp.int32)
    flip_east = jax.random.randint(key_eflip, (index_count, TILES_DEV), 0, 2, dtype=jnp.int32)
    flip_north = jax.random.randint(key_nflip, (index_count, TILES_DEV), 0, 2, dtype=jnp.int32)
    index_ids = jnp.arange(index_count, dtype=jnp.int32)[:, None]
    east_tile = (index_ids + 1) % index_count * TILES_DEV + east_perm
    prev_inv = jnp.roll(east_inv, 1, axis=0)
    west_tile = (index_ids - 1) % index_count * TILES_DEV + prev_inv
    west_flip = jnp.take_along_axis(jnp.roll(flip_east, 1, axis=0), prev_inv, axis=1)
    north_tile = index_ids * TILES_DEV + north_perm
    south_tile = index_ids * TILES_DEV + north_inv
    south_flip = jnp.take_along_axis(flip_north, north_inv, axis=1)
    tile_ids = jnp.stack([north_tile, east_tile, south_tile, west_tile], axis=-1).reshape(TILES, 4)
    flip_ids = jnp.stack([flip_north, flip_east, south_flip, west_flip], axis=-1).reshape(TILES, 4)
    return (tile_ids.astype(jnp.int32), flip_ids.astype(jnp.int32))


def draw_seams(key, part):
    tile_ids, flip_ids = side_pairing(key)
    side_ids = jnp.broadcast_to(jnp.array([2, 3, 0, 1], dtype=jnp.int32)[None, :], (TILES, 4))
    return jnp.stack([tile_ids, side_ids, flip_ids], axis=-1)


def draw_corner_list(key, part):
    tile_ids, flip_ids = side_pairing(key)
    north_tile, south_tile = (tile_ids[:, 0], tile_ids[:, 2])
    north_flip, south_flip = (flip_ids[:, 0], flip_ids[:, 2])
    corner_zero = jnp.where(north_flip == 1, 2, 3)
    corner_one = jnp.where(north_flip == 1, 3, 2)
    corner_two = jnp.where(south_flip == 1, 0, 1)
    corner_three = jnp.where(south_flip == 1, 1, 0)
    owners = jnp.stack([north_tile, north_tile, south_tile, south_tile], axis=1)
    which = jnp.stack([corner_zero, corner_one, corner_two, corner_three], axis=1)
    return jnp.stack([owners, which], axis=-1).astype(jnp.int32)


def plant(values, rng, low, high):
    longest = values.shape.index(max(values.shape))
    spots = []
    for shift in (0, 1):
        where = [jax.random.randint(jax.random.fold_in(rng, axis), (), 0, length) for axis, length in enumerate(values.shape)]
        where[longest] = (where[longest] + shift) % values.shape[longest]
        spots.append(tuple(where))
    return values.at[spots[0]].set(low).at[spots[1]].set(high)


def steps_of(stream_key, dims, pieces, low, top_value):
    def one(axis_at, parts):
        steps = jax.random.uniform(jax.random.fold_in(jax.random.fold_in(stream_key, 6), axis_at), (parts,), jnp.float32, low / len(pieces), top_value / len(pieces))
        return jnp.repeat(jnp.exp(steps), dims[axis_at] // parts).reshape((-1,) + (1,) * (len(dims) - axis_at - 1))

    level = one(*pieces[0])
    for cut in pieces[1:]:
        level = level * one(*cut)
    return level


def deal_out(key, own, number, rows, amount, top, bound, slope):
    ranking = jax.random.permutation(key, amount)
    crowded, usual = load_shares(amount, rows * top, bound, slope, True), load_shares(amount, rows * top, bound, slope, False)
    places = jnp.arange(amount)

    def named(sizes, turn):
        used = int((sizes > 0).sum())
        fixed = max(1, used // 4)
        passed = fixed + (places - fixed + turn * (used - fixed)) % max(1, amount - fixed)
        return jnp.zeros((amount,), jnp.int32).at[ranking[jnp.where(places < fixed, places, passed)]].set(jnp.asarray(sizes, jnp.int32))

    sizes = jnp.where(number % 4 == 0, named(crowded, number // 4), named(usual, number - number // 4 - 1))
    mixed = jax.random.permutation(jax.random.fold_in(own, 3), amount)
    source_of, receiver = mixed[0:amount // 2 * 2:2], mixed[1:amount // 2 * 2:2]
    room = jnp.minimum(sizes[source_of] - 1, bound - sizes[receiver]) // 2
    room = jnp.where((source_of == ranking[0]) | (receiver == ranking[0]) | (sizes[receiver] == 0), 0, jnp.maximum(room, 0))
    passed = jax.random.randint(jax.random.fold_in(own, 4), (amount // 2,), 0, 1 << 20) % (room + 1)
    sizes = sizes.at[source_of].add(-passed).at[receiver].add(passed)
    items = jnp.searchsorted(jnp.cumsum(sizes), jnp.arange(rows * top), side="right").astype(jnp.int32)
    table = items.reshape(top, rows).T
    table = table[jax.random.permutation(jax.random.fold_in(own, 1), rows)]
    turn = jax.random.randint(jax.random.fold_in(own, 2), (rows, 1), 0, top)
    return jnp.take_along_axis(table, (jnp.arange(top)[None, :] + turn) % top, axis=1)


def load_shares(count, total, bound, skew, full):
    weights = [(1 << 20) // math.isqrt(grade ** skew) + 1 for grade in range(1, count + 1)]
    largest = bound if full else min(bound, max(-(-total // count), total * weights[0] // sum(weights)))
    least = 1 if total - largest >= count - 1 else 0
    given, spare = [largest] + [least] * (count - 1), total - largest - least * (count - 1)
    while spare > 0:
        free = [i for i in range(1, count) if given[i] < largest] or [i for i in range(1, count) if given[i] < bound]
        pool, budget = sum([weights[i] for i in free]), spare
        for i in free:
            addition = min(bound - given[i], max(1, budget * weights[i] // pool), spare)
            given[i] = given[i] + addition
            spare = spare - addition
    return np.array(given)


def gaussian(own_key, extent, scale, most, shards=(), kind=jnp.bfloat16):
    values = jax.random.normal(own_key, extent, jnp.float32) * scale
    if len(shards) > 0:
        values = steps_of(own_key, extent, shards, -0.22, 0.18) * values
    return jnp.clip(values, min=-most, max=most).astype(kind)


def setup_inputs(seed: int = 0) -> dict:
    key_of = jax.random.split(jax.random.key(seed), 16)
    noisy = gaussian(key_of[0], (MEMBERS, TILES, SUB, SUB * VARS), 1.0, 6.0, ((0, 8), (1, 16)))
    timestep = plant(jax.random.randint(key_of[1], (MEMBERS,), STEPS // 2, STEPS), jax.random.fold_in(key_of[1], 1), STEPS // 2, STEPS - 1).astype(jnp.int32)
    seams = draw_seams(jax.random.fold_in(key_of[15], 71), 0)
    corner_list = draw_corner_list(jax.random.fold_in(key_of[15], 71), 0)
    route_keys = jax.random.split(jax.random.fold_in(key_of[4], 1), TILES // TILES_DEV)
    route_turns = jax.random.permutation(jax.random.fold_in(key_of[4], 3), TILES // TILES_DEV)
    route = jax.vmap(lambda own, number: deal_out(jax.random.fold_in(key_of[4], 2), own, number, TILES_DEV, N_TILE, 1, CAP, 2))(route_keys, route_turns).reshape((TILES, 1))
    target_block = plant(jax.random.randint(key_of[5], (TILES,), 0, BLK_DEV), jax.random.fold_in(key_of[5], 1), 0, BLK_DEV - 1).astype(jnp.int32)
    frac = jnp.clip(0.05 + 0.9 * jax.random.uniform(key_of[6], (TILES, 2), jnp.float32) ** steps_of(key_of[6], (TILES, 2), ((0, 16),), -0.2, 0.2), 0.05, 0.95)
    w_time = gaussian(key_of[7], (C, C), C ** -0.5, 0.5, (), jnp.float32)
    w_lift = gaussian(key_of[8], (VARS, C), VARS ** -0.5, 2.0)
    w_fine = gaussian(key_of[9], (9, C, C), (9 * C) ** -0.5, 0.1875)
    w_coarse = gaussian(key_of[10], (9, C, C), (9 * C) ** -0.5, 0.1875)
    gain_fine = jnp.clip(1.0 + 0.18 * jax.random.normal(key_of[11], (C,), jnp.float32), 0.1, 1.9)
    gain_coarse = jnp.clip(1.0 + 0.18 * jax.random.normal(key_of[12], (C,), jnp.float32), 0.1, 1.9)
    gain_out = jnp.clip(1.0 + 0.18 * jax.random.normal(key_of[13], (C,), jnp.float32), 0.1, 1.9)
    w_out = gaussian(key_of[14], (C, VARS), C ** -0.5, 0.5)
    return dict(noisy=noisy, timestep=timestep, seams=seams, corner_list=corner_list, route=route, target_block=target_block, frac=frac, w_time=w_time, w_lift=w_lift, w_fine=w_fine, w_coarse=w_coarse, gain_fine=gain_fine, gain_coarse=gain_coarse, gain_out=gain_out, w_out=w_out)


def precondition(timestep):
    fraction = timestep.astype(jnp.float32) / (STEPS - 1)
    high_root = 80.0 ** (1.0 / 7.0)
    low_root = 0.002 ** (1.0 / 7.0)
    sigma = (high_root + fraction * (low_root - high_root)) ** 7
    denominator = sigma * sigma + 1.0
    return (lax.rsqrt(denominator), 1.0 / denominator, sigma * lax.rsqrt(denominator))

def embed(timestep, w_time):
    half_width = w_time.shape[0] // 2
    frequency = jnp.exp(-math.log(10000.0) * jnp.arange(half_width, dtype=jnp.float32) / half_width)
    angles = timestep.astype(jnp.float32)[:, None] * frequency[None, :]
    features = jnp.concatenate([jnp.sin(angles), jnp.cos(angles)], axis=-1)
    return jax.nn.silu(jnp.dot(features, w_time, precision=lax.Precision.HIGHEST))

def rms_act(activation, gain):
    values = activation.astype(jnp.float32)
    normed = values * lax.rsqrt(lax.optimization_barrier(jnp.mean(values * values, axis=-1, keepdims=True)) + 1e-06) * gain
    return jax.nn.silu(normed).astype(jnp.bfloat16)

def rims_of(normed):
    edge_len = normed.shape[2]
    north_rim = normed[:, :, 0]
    east_rim = normed[:, :, :, edge_len - 1]
    south_rim = normed[:, :, edge_len - 1]
    west_rim = normed[:, :, :, 0]
    corners = jnp.stack([normed[:, :, 0, 0], normed[:, :, 0, edge_len - 1], normed[:, :, edge_len - 1, edge_len - 1], normed[:, :, edge_len - 1, 0]], axis=2)
    return jnp.concatenate([north_rim, east_rim, south_rim, west_rim, corners], axis=2)

def halo_rows(tile_refs, corner_refs, seams, corner_list, edge_len):
    width = 4 * edge_len + 4
    positions = jnp.arange(edge_len, dtype=jnp.int32)
    along_edge = jnp.where(seams[:, :, 2:3] == 1, edge_len - 1 - positions[None, None, :], positions[None, None, :])
    edge_rows = tile_refs[:, :, None] * width + seams[:, :, 1:2] * edge_len + along_edge
    corner_rows = corner_refs * width + 4 * edge_len + corner_list[:, :, 1]
    edge_rows = edge_rows.reshape(edge_rows.shape[0], 4 * edge_len)
    return jnp.concatenate([edge_rows, corner_rows], axis=1).astype(jnp.int32)

def assemble(normed, gathered):
    edge_len = normed.shape[2]
    north_rim = gathered[:, :, 0:edge_len]
    east_rim = gathered[:, :, edge_len:2 * edge_len]
    south_rim = gathered[:, :, 2 * edge_len:3 * edge_len]
    west_rim = gathered[:, :, 3 * edge_len:4 * edge_len]
    corners = gathered[:, :, 4 * edge_len:]
    middle = jnp.concatenate([west_rim[:, :, :, None], normed, east_rim[:, :, :, None]], axis=3)
    upper_row = jnp.concatenate([corners[:, :, 0:1], north_rim, corners[:, :, 1:2]], axis=2)[:, :, None]
    lower_row = jnp.concatenate([corners[:, :, 3:4], south_rim, corners[:, :, 2:3]], axis=2)[:, :, None]
    return jnp.concatenate([upper_row, middle, lower_row], axis=2)

def convolve(padded, weight):
    members, tile_total, edge_len = (padded.shape[0], padded.shape[1], padded.shape[2] - 2)
    channels = padded.shape[-1]
    summed = jnp.zeros((members * tile_total * edge_len * edge_len, weight.shape[2]), jnp.float32)
    for row_off in range(3):
        for col_off in range(3):
            slab_view = padded[:, :, row_off:row_off + edge_len, col_off:col_off + edge_len].reshape(-1, channels)
            summed = summed + jnp.dot(slab_view, weight[3 * row_off + col_off], preferred_element_type=jnp.float32)
    return summed.reshape(members, tile_total, edge_len, edge_len, weight.shape[2])

def level_step(activation, gain, weight, rows, window_fn):
    normed = rms_act(activation, gain)
    window = window_fn(rims_of(normed))
    members, tile_total = (normed.shape[0], normed.shape[1])
    flattened = window.reshape(members, -1, window.shape[-1])
    gathered = jnp.take(flattened, rows.reshape(-1), axis=1).reshape(members, tile_total, rows.shape[1], window.shape[-1])
    padded = assemble(normed, gathered)
    return (activation.astype(jnp.float32) + convolve(padded, weight)).astype(jnp.bfloat16)

def denoise(noisy, timestep, fine_rows, coarse_rows, weights, fine_fn, coarse_fn):
    w_time, w_lift, w_fine, w_coarse, gain_fine, gain_coarse, gain_out, w_out = weights
    members, tile_total, edge_len, packed = noisy.shape
    variables = packed // edge_len
    channels = w_lift.shape[1]
    scale_in, scale_skip, scale_out = precondition(timestep)
    temb = embed(timestep, w_time)
    scaled = (noisy.astype(jnp.float32) * scale_in[:, None, None, None]).astype(jnp.bfloat16)
    lifted = jnp.dot(scaled.reshape(-1, variables), w_lift, preferred_element_type=jnp.float32)
    lifted = lifted.reshape(members, tile_total, edge_len, edge_len, channels)
    started = (lifted + temb[:, None, None, None, :]).astype(jnp.bfloat16)
    fine_out = level_step(started, gain_fine, w_fine, fine_rows, fine_fn)
    half_len = edge_len // 2
    pooled = fine_out.astype(jnp.float32).reshape(members, tile_total, half_len, 2, half_len, 2, channels)
    pooled = (lax.optimization_barrier(jnp.sum(pooled, axis=(3, 5))) * 0.25).astype(jnp.bfloat16)
    coarse = level_step(pooled, gain_coarse, w_coarse, coarse_rows, coarse_fn)
    upsampled = jnp.repeat(jnp.repeat(coarse.astype(jnp.float32), 2, axis=2), 2, axis=3) + fine_out.astype(jnp.float32)
    final_act = rms_act(upsampled, gain_out)
    projected = jnp.dot(final_act.reshape(-1, channels), w_out, preferred_element_type=jnp.float32)
    projected = projected.reshape(members, tile_total, edge_len, packed)
    result = scale_skip[:, None, None, None] * noisy.astype(jnp.float32) + scale_out[:, None, None, None] * projected
    return result.astype(jnp.float32)

def remap(denoised, frac, variables):
    values = denoised.astype(jnp.float32)
    frac_rows = frac[:, 0][None, :, None, None]
    frac_cols = frac[:, 1][None, :, None, None]
    rows_next = jnp.concatenate([values[:, :, 1:], values[:, :, -1:]], axis=2)
    row_mixed = (1.0 - frac_rows) * values + frac_rows * rows_next
    cols_next = jnp.concatenate([row_mixed[..., variables:], row_mixed[..., -variables:]], axis=3)
    return (1.0 - frac_cols) * row_mixed + frac_cols * cols_next

def reference(noisy, timestep, seams, corner_list, route, target_block, frac, w_time, w_lift, w_fine, w_coarse, gain_fine, gain_coarse, gain_out, w_out):
    tile_refs = seams[:, :, 0].astype(jnp.int32)
    corner_refs = corner_list[:, :, 0].astype(jnp.int32)
    fine_rows = halo_rows(tile_refs, corner_refs, seams, corner_list, SUB)
    coarse_rows = halo_rows(tile_refs, corner_refs, seams, corner_list, SUB // 2)
    weights = (w_time, w_lift, w_fine, w_coarse, gain_fine, gain_coarse, gain_out, w_out)

    def keep_all(rim_cells):
        return rim_cells

    def one_member(pair):
        sample_one, step_one = pair
        return denoise(sample_one[None], step_one[None], fine_rows, coarse_rows, weights, keep_all, keep_all)[0]
    denoised = lax.map(one_member, (noisy, timestep))
    remapped = remap(denoised, frac, VARS).astype(jnp.float32)
    blocks = (route[:, 0].astype(jnp.int32) * BLK_DEV + target_block.astype(jnp.int32)).astype(jnp.int32)
    target = jax.ops.segment_sum(jnp.moveaxis(remapped, 1, 0), blocks, num_segments=BLOCKS)
    ens_mean = lax.optimization_barrier(jnp.sum(target, axis=1)) / MEMBERS
    deviation = target - ens_mean[:, None]
    ens_spread = jnp.sqrt(lax.optimization_barrier(jnp.sum(deviation * deviation, axis=1)) / (MEMBERS - 1) + 1e-06)
    return (denoised, ens_mean, ens_spread)
```

```python
import functools
import math

import jax
import jax.numpy as jnp
from jax import lax
from jax.experimental import pallas as pl
from jax.experimental.pallas import tpu as pltpu
from jax.sharding import PartitionSpec as P

STEPS = 1000
MESH = pl.DeviceIdType.MESH
F32 = jnp.float32
BF16 = jnp.bfloat16

B = 16
N = 32
H = N // 2
NT = 16
NM = 8
CH = 4
RC = N // CH


def dot(a, b):
    return jnp.dot(a, b, preferred_element_type=F32)


def twice(x):
    return jnp.concatenate([x, x], axis=-1)


def iota(shape, dim):
    return lax.broadcasted_iota(jnp.int32, shape, dim)


def act(x, ones, half_gain):
    mean = dot((x * x).astype(BF16), ones)
    h = x * lax.rsqrt(mean + 1e-06) * half_gain
    return (h + h * jnp.tanh(h)).astype(BF16)


def seam_perm(perm_ref, seam_ref, side, n, natural):
    tile = seam_ref[:, 3 * side : 3 * side + 1] % 8
    flag = seam_ref[:, 3 * side + 2 : 3 * side + 3]
    base = (iota((B, 1), 0) // 8) * 8 + tile
    lane = iota((B, n * B), 1)

    def row(r, _):
        along = jnp.where(flag == 1, n - 1 - r, r)
        source = base * n + along if natural else along * B + base
        perm_ref[pl.ds(pl.multiple_of(r * B, B), B), :] = jnp.where(
            source == lane, 1.0, 0.0
        ).astype(BF16)
        return 0

    lax.fori_loop(0, n, row, 0)


def conv_weights(out_ref, w_ref):
    zero = jnp.zeros((128, 128), BF16)
    for i in range(3):
        for j in range(4):
            left = w_ref[3 * i + j] if j < 3 else zero
            right = w_ref[3 * i + j - 1] if j > 0 else zero
            start = (4 * i + j) * 128
            out_ref[start : start + 128, :] = jnp.concatenate([left, right], axis=1)


def conv_pair(a_ref, w, pair, start, rows):
    parts = []
    for i in range(3):
        for j in range(4):
            parts.append(a_ref[2 * pair + j, pl.ds(start + i * B, rows), :])
    return dot(jnp.concatenate(parts, axis=1), w)


def kernel(
    noisy_ref,
    vec_ref,
    gain_ref,
    seam_ref,
    key_ref,
    blk_ref,
    wl_ref,
    wf_ref,
    wc_ref,
    wo_ref,
    den_ref,
    stat_ref,
    nx,
    sx,
    lift_w,
    out_w,
    fine_w,
    coarse_w,
    ones_ref,
    perm_a,
    perm_b,
    perm_c,
    slot_ref,
    sum_ref,
    halo,
    started,
    a1,
    fine,
    pooled,
    a2,
    halo2,
    coarse,
    d_ref,
    send,
    recv,
    tgt,
    mrecv,
    gat,
    h_send,
    h_recv,
    c_send,
    c_recv,
    a_send,
    a_recv,
    m_send,
    m_recv,
    g_send,
    g_recv,
):
    pos = lax.axis_index("tile")
    mem = lax.axis_index("mem")
    east = lax.rem(pos + 1, NT)
    west = lax.rem(pos + NT - 1, NT)

    barrier = pltpu.get_barrier_semaphore()

    def greet_tile(d, _):
        pl.semaphore_signal(
            barrier, inc=1, device_id={"tile": lax.rem(pos + d, NT)}, device_id_type=MESH
        )
        return 0

    def greet_mem(d, _):
        pl.semaphore_signal(
            barrier, inc=1, device_id={"mem": lax.rem(mem + d, NM)}, device_id_type=MESH
        )
        return 0

    lax.fori_loop(1, NT, greet_tile, 0)
    lax.fori_loop(1, NM, greet_mem, 0)
    pl.semaphore_wait(barrier, NT - 1 + NM - 1)

    to_west = pltpu.make_async_remote_copy(
        src_ref=noisy_ref.at[:, pl.ds(0, 128)],
        dst_ref=halo.at[0],
        send_sem=h_send.at[0],
        recv_sem=h_recv.at[0],
        device_id={"tile": west},
        device_id_type=MESH,
    )
    to_east = pltpu.make_async_remote_copy(
        src_ref=noisy_ref.at[:, pl.ds(128, 128)],
        dst_ref=halo.at[1],
        send_sem=h_send.at[1],
        recv_sem=h_recv.at[1],
        device_id={"tile": east},
        device_id_type=MESH,
    )
    to_west.start()
    to_east.start()

    c_in, c_skip, c_out = twice(vec_ref[0]), twice(vec_ref[1]), twice(vec_ref[2])
    temb, frac_p, frac_q = twice(vec_ref[3]), twice(vec_ref[4]), twice(vec_ref[5])
    gain_fine = twice(gain_ref[0:1]) * 0.5
    gain_coarse = gain_ref[1:2] * 0.5
    gain_out = twice(gain_ref[2:3]) * 0.5

    def lift_row(r, _):
        lane = iota((B, 512), 1)
        want = iota((B, 512), 0) * N + r
        perm_a[pl.ds(pl.multiple_of(r * B, B), B), :] = jnp.where(want == lane, 1.0, 0.0).astype(
            BF16
        )
        return 0

    lax.fori_loop(0, N, lift_row, 0)
    ones_ref[...] = jnp.where(
        iota((256, 256), 0) // 128 == iota((256, 256), 1) // 128, 1.0 / 128, 0.0
    ).astype(BF16)
    wl = wl_ref[...].astype(F32)
    wl_zero = jnp.zeros_like(wl)
    wl_pair = jnp.concatenate(
        [
            jnp.concatenate([wl, wl_zero], axis=1),
            jnp.concatenate([wl_zero, wl], axis=1),
        ],
        axis=0,
    ).astype(BF16)
    for q in range(8):
        lift_w[q] = jnp.zeros((128, 256), BF16)
        lift_w[q, q * B : (q + 1) * B, :] = wl_pair
        for j in range(2):
            place = jnp.where(
                iota((8, 128), 1) == iota((8, 128), 0) + (16 * q + 8 * j), 1.0, 0.0
            ).astype(BF16)
            out_w[q, j * 128 : (j + 1) * 128, :] = dot(wo_ref[...], place).astype(BF16)
    conv_weights(fine_w, wf_ref)
    conv_weights(coarse_w, wc_ref)

    natural = noisy_ref[...]
    for s in range(2):
        rows = slice(s * 256, (s + 1) * 256)
        moved = dot(perm_a[rows, :], natural)
        nx[rows, :] = moved.astype(BF16)
        sx[rows, :] = (moved.reshape(H, B, 256) * c_in).reshape(256, 256).astype(BF16)

    def lift(q, _):
        for half in range(2):
            pair = half * 8 + q
            for s in range(2):
                rows = slice(s * 256, (s + 1) * 256)
                up = dot(sx[rows, half * 128 : (half + 1) * 128], lift_w[q])
                first = (up.reshape(H, B, 256) + temb).reshape(256, 256).astype(BF16)
                started[2 * pair, rows, :] = first[:, :128]
                started[2 * pair + 1, rows, :] = first[:, 128:]
                normed = act(first.astype(F32), ones_ref[...], gain_fine)
                inner = slice(s * 256 + B, (s + 1) * 256 + B)
                a1[2 * pair + 1, inner, :] = normed[:, :128]
                a1[2 * pair + 2, inner, :] = normed[:, 128:]
        return 0

    lax.fori_loop(0, 8, lift, 0)

    def north_south(a_ref, perm, n, row_from, row_to):
        edge = a_ref[1 : n + 1, row_from * B : (row_from + 1) * B, :].reshape(n * B, 128)
        got = dot(perm[...], edge).astype(BF16).reshape(n, B, 128)
        rows = slice(row_to * B, (row_to + 1) * B)
        a_ref[1 : n + 1, rows, :] = got
        a_ref[0, rows, :] = got[0]
        a_ref[n + 1, rows, :] = got[n - 1]

    seam_perm(perm_a, seam_ref, 0, N, False)
    north_south(a1, perm_a, N, N, 0)
    seam_perm(perm_b, seam_ref, 2, N, False)
    north_south(a1, perm_b, N, 1, N + 1)
    seam_perm(perm_a, seam_ref, 1, N, True)
    seam_perm(perm_b, seam_ref, 3, N, True)
    to_west.wait()
    to_east.wait()
    for s in range(2):
        rows = slice(s * 256, (s + 1) * 256)
        sides = []
        for perm, side, w in (
            (perm_b, 1, lift_w[7, :, 128:256]),
            (perm_a, 0, lift_w[0, :, 0:128]),
        ):
            moved = dot(perm[rows, :], halo[side])
            scaled = (moved.reshape(H, B, 128) * vec_ref[0]).reshape(256, 128).astype(BF16)
            sides.append(dot(scaled, w))
        up = jnp.concatenate(sides, axis=1)
        first = (up.reshape(H, B, 256) + temb).reshape(256, 256).astype(BF16)
        normed = act(first.astype(F32), ones_ref[...], gain_fine)
        inner = slice(s * 256 + B, (s + 1) * 256 + B)
        a1[0, inner, :] = normed[:, :128]
        a1[N + 1, inner, :] = normed[:, 128:]

    def fine_pair(pair):
        for s in range(2):
            rows = slice(s * 256, (s + 1) * 256)
            got = conv_pair(a1, fine_w[...], pair, s * 256, 256)
            base = jnp.concatenate([started[2 * pair, rows, :], started[2 * pair + 1, rows, :]], axis=1)
            out = (base.astype(F32) + got).astype(BF16)
            fine[2 * pair, rows, :] = out[:, :128]
            fine[2 * pair + 1, rows, :] = out[:, 128:]
            wide = out.astype(F32).reshape(H // 2, 2, B, 256)
            tall = wide[:, 0] + wide[:, 1]
            mean = ((tall[:, :, :128] + tall[:, :, 128:]) * 0.25).reshape(128, 128).astype(BF16)
            half_rows = slice(s * 128, (s + 1) * 128)
            pooled[pair, half_rows, :] = mean
            normed = act(mean.astype(F32), ones_ref[0:128, 0:128], gain_coarse)
            a2[pair + 1, s * 128 + B : (s + 1) * 128 + B, :] = normed

    fine_pair(0)
    fine_pair(H - 1)
    c_west = pltpu.make_async_remote_copy(
        src_ref=a2.at[1, pl.ds(B, 256)],
        dst_ref=halo2.at[0],
        send_sem=c_send.at[0],
        recv_sem=c_recv.at[0],
        device_id={"tile": west},
        device_id_type=MESH,
    )
    c_east = pltpu.make_async_remote_copy(
        src_ref=a2.at[H, pl.ds(B, 256)],
        dst_ref=halo2.at[1],
        send_sem=c_send.at[1],
        recv_sem=c_recv.at[1],
        device_id={"tile": east},
        device_id_type=MESH,
    )
    c_west.start()
    c_east.start()

    def fine_loop(pair, _):
        fine_pair(pair)
        return 0

    lax.fori_loop(1, H - 1, fine_loop, 0)

    seam_perm(perm_c, seam_ref, 0, H, False)
    north_south(a2, perm_c, H, H, 0)
    seam_perm(perm_c, seam_ref, 2, H, False)
    north_south(a2, perm_c, H, 1, H + 1)
    c_west.wait()
    c_east.wait()
    seam_perm(perm_c, seam_ref, 1, H, False)
    a2[H + 1, B : B + 256, :] = dot(perm_c[...], halo2[0]).astype(BF16)
    seam_perm(perm_c, seam_ref, 3, H, False)
    a2[0, B : B + 256, :] = dot(perm_c[...], halo2[1]).astype(BF16)

    def coarse_loop(pair, _):
        got = conv_pair(a2, coarse_w[...], pair, 0, 256)
        base = jnp.concatenate([pooled[2 * pair], pooled[2 * pair + 1]], axis=1)
        out = (base.astype(F32) + got).astype(BF16)
        coarse[2 * pair] = out[:, :128]
        coarse[2 * pair + 1] = out[:, 128:]
        return 0

    lax.fori_loop(0, H // 2, coarse_loop, 0)

    i, j = iota((512, 128), 0), iota((512, 128), 1)
    slot_ref[...] = jnp.where(
        ((i >> 4) == key_ref[...]) & (((i >> 3) & 1) == ((j >> 3) & 1)) & ((i & 7) == (j >> 4)),
        1.0,
        0.0,
    ).astype(BF16)
    i, j = iota((64, 512), 0), iota((64, 512), 1)
    sum_ref[...] = jnp.where(
        ((i & 3) == blk_ref[...]) & (((i >> 2) & 1) == ((j >> 3) & 1)) & ((i >> 3) == (j & 7)),
        1.0,
        0.0,
    ).astype(BF16)

    rows_c = RC * B

    def a_copy(k, d):
        return pltpu.make_async_remote_copy(
            src_ref=send.at[k, d],
            dst_ref=recv.at[k, d],
            send_sem=a_send.at[k, d],
            recv_sem=a_recv.at[k, d],
            device_id={"tile": lax.rem(pos + d, NT)},
            device_id_type=MESH,
        )

    def m_copy(k, d):
        return pltpu.make_async_remote_copy(
            src_ref=tgt.at[k, lax.rem(mem + d, NM)],
            dst_ref=mrecv.at[k, d],
            send_sem=m_send.at[k, d],
            recv_sem=m_recv.at[k, d],
            device_id={"mem": lax.rem(mem + d, NM)},
            device_id_type=MESH,
        )

    def g_copy(k, d):
        return pltpu.make_async_remote_copy(
            src_ref=gat.at[k, mem],
            dst_ref=gat.at[k, mem],
            send_sem=g_send.at[k, d],
            recv_sem=g_recv.at[k, d],
            device_id={"mem": lax.rem(mem + d, NM)},
            device_id_type=MESH,
        )

    def each(count, what):
        def body(d, _):
            what(d)
            return 0

        lax.fori_loop(1, count, body, 0)

    def last_stage(k):
        start = k * rows_c

        def pair_step(q, sums):
            out = []
            for half in range(2):
                pair = half * 8 + q
                f = jnp.concatenate(
                    [fine[2 * pair, start : start + rows_c, :], fine[2 * pair + 1, start : start + rows_c, :]],
                    axis=1,
                ).astype(F32)
                c = coarse[pair, start // 2 : (start + rows_c) // 2, :].astype(F32)
                c = c.reshape(RC // 2, 1, B, 128)
                c = jnp.concatenate([c, c], axis=1).reshape(rows_c, 128)
                normed = act(f + twice(c), ones_ref[...], gain_out)
                out.append(sums[half] + dot(normed, out_w[q]))
            return tuple(out)

        zero = jnp.zeros((rows_c, 128), F32)
        left, right = lax.fori_loop(0, 8, pair_step, (zero, zero))
        proj = jnp.concatenate([left, right], axis=1).reshape(RC, B, 256)
        state = nx[start : start + rows_c, :].astype(F32).reshape(RC, B, 256)
        den = (c_skip * state + c_out * proj).reshape(rows_c, 256)
        d_ref[start : start + rows_c, :] = den
        den_ref[start : start + rows_c, :] = den
        if k == CH - 1:
            d_ref[N * B : (N + 1) * B, :] = den[rows_c - B :, :]
        below = d_ref[start + B : start + B + rows_c, :].reshape(RC, B, 256)
        mixed = (1.0 - frac_p) * den.reshape(RC, B, 256) + frac_p * below
        mixed = mixed.reshape(rows_c, 256)
        shifted = pltpu.roll(mixed, 248, 1)
        shifted = jnp.where(iota((rows_c, 256), 1) >= 248, mixed, shifted)
        out = (1.0 - frac_q) * mixed.reshape(RC, B, 256) + frac_q * shifted.reshape(RC, B, 256)
        blocks = dot(slot_ref[...], out.reshape(rows_c, 256).astype(BF16)).astype(BF16)
        blocks = blocks.reshape(NT, 32, 256)
        recv[k, 0] = blocks[0]
        send[k] = blocks
        each(NT, lambda d: a_copy(k, d).start())

    def sum_stage(k):
        each(NT, lambda d: a_copy(k, d).wait_recv())
        total = dot(sum_ref[...], recv[k].reshape(512, 256))
        tgt[k] = total.reshape(NM, 8, 256)
        mrecv[k, 0] = tgt[k, mem]
        each(NM, lambda d: m_copy(k, d).start())

    def stat_stage(k):
        each(NM, lambda d: m_copy(k, d).wait_recv())
        values = mrecv[k]
        total = jnp.sum(values, axis=0)
        mean = (total[0:4] + total[4:8]) * (1.0 / 16)
        dev = values - jnp.concatenate([mean, mean], axis=0)
        squares = jnp.sum(dev * dev, axis=0)
        spread = jnp.sqrt((squares[0:4] + squares[4:8]) / 15.0 + 1e-06)
        gat[k, mem] = jnp.concatenate([mean, spread], axis=0)
        each(NM, lambda d: g_copy(k, d).start())

    order = list(range(CH - 1, -1, -1))
    for step in range(CH + 2):
        if step < CH:
            last_stage(order[step])
        if 1 <= step < CH + 1:
            sum_stage(order[step - 1])
        if 2 <= step:
            stat_stage(order[step - 2])
    for k in order:
        each(NM, lambda d: g_copy(k, d).wait_recv())
    stat_ref[...] = gat[...]
    for k in order:
        each(NT, lambda d: a_copy(k, d).wait_send())
        each(NM, lambda d: m_copy(k, d).wait_send())
        each(NM, lambda d: g_copy(k, d).wait_send())


def precondition(timestep):
    fraction = timestep.astype(jnp.float32) / (STEPS - 1)
    high_root = 80.0 ** (1.0 / 7.0)
    low_root = 0.002 ** (1.0 / 7.0)
    sigma = (high_root + fraction * (low_root - high_root)) ** 7
    denominator = sigma * sigma + 1.0
    return (lax.rsqrt(denominator), 1.0 / denominator, sigma * lax.rsqrt(denominator))


def embed(timestep, w_time):
    half_width = w_time.shape[0] // 2
    frequency = jnp.exp(-math.log(10000.0) * jnp.arange(half_width, dtype=jnp.float32) / half_width)
    angles = timestep.astype(jnp.float32)[:, None] * frequency[None, :]
    features = jnp.concatenate([jnp.sin(angles), jnp.cos(angles)], axis=-1)
    return jax.nn.silu(jnp.dot(features, w_time, precision=lax.Precision.HIGHEST))


def on_device(
    noisy,
    timestep,
    seams,
    corner_list,
    route,
    target_block,
    frac,
    w_time,
    w_lift,
    w_fine,
    w_coarse,
    gain_fine,
    gain_coarse,
    gain_out,
    w_out,
):
    pos = lax.axis_index("tile")
    scales = precondition(timestep)
    temb = embed(timestep, w_time)

    def rows(x):
        return jnp.broadcast_to(jnp.repeat(x, 8)[:, None], (B, 128))

    def tiles(x):
        return jnp.broadcast_to(jnp.concatenate([x, x])[:, None], (B, 128))

    vec = jnp.stack(
        [rows(s) for s in scales]
        + [jnp.repeat(temb, 8, axis=0), tiles(frac[:, 0]), tiles(frac[:, 1])]
    )
    gains = jnp.stack([gain_fine, gain_coarse, gain_out])
    seam = seams.reshape(8, 12)
    seam = jnp.concatenate([seam, seam], axis=0)

    owners = route.reshape(NT, 8)
    same = owners[:, :, None] == owners[:, None, :]
    earlier = jnp.arange(8)[None, :, None] > jnp.arange(8)[None, None, :]
    rank = jnp.sum((same & earlier).astype(jnp.int32), axis=2)
    own_owner = lax.dynamic_index_in_dim(owners, pos, 0, False)
    own_rank = lax.dynamic_index_in_dim(rank, pos, 0, False)
    key = (own_owner - pos) % NT * 2 + own_rank
    key_lane = jnp.tile(key, 16)[None, :]
    blocks = target_block.reshape(NT, 8)
    mine = (owners == pos)[:, None, :] & (rank[:, None, :] == jnp.arange(2)[None, :, None])
    slot_block = jnp.max(jnp.where(mine, blocks[:, None, :], -1), axis=2)
    slot_block = jnp.take(slot_block, (pos - jnp.arange(NT)) % NT, axis=0)
    blk_lane = jnp.repeat(slot_block.reshape(32), 16)[None, :]

    vmem = pl.BlockSpec(memory_space=pltpu.VMEM)
    dma = pltpu.SemaphoreType.DMA
    den, stat = pl.pallas_call(
        kernel,
        out_shape=(
            jax.ShapeDtypeStruct((512, 256), F32),
            jax.ShapeDtypeStruct((CH, NM, 8, 256), F32),
        ),
        in_specs=[vmem] * 10,
        out_specs=(vmem, vmem),
        scratch_shapes=[
            pltpu.VMEM((512, 256), BF16),
            pltpu.VMEM((512, 256), BF16),
            pltpu.VMEM((8, 128, 256), BF16),
            pltpu.VMEM((8, 256, 128), BF16),
            pltpu.VMEM((1536, 256), BF16),
            pltpu.VMEM((1536, 256), BF16),
            pltpu.VMEM((256, 256), BF16),
            pltpu.VMEM((512, 512), BF16),
            pltpu.VMEM((512, 512), BF16),
            pltpu.VMEM((256, 256), BF16),
            pltpu.VMEM((512, 128), BF16),
            pltpu.VMEM((64, 512), BF16),
            pltpu.VMEM((2, 512, 128), BF16),
            pltpu.VMEM((N, 512, 128), BF16),
            pltpu.VMEM((N + 2, 544, 128), BF16),
            pltpu.VMEM((N, 512, 128), BF16),
            pltpu.VMEM((H, 256, 128), BF16),
            pltpu.VMEM((H + 2, 288, 128), BF16),
            pltpu.VMEM((2, 256, 128), BF16),
            pltpu.VMEM((H, 256, 128), BF16),
            pltpu.VMEM(((N + 1) * B, 256), F32),
            pltpu.VMEM((CH, NT, 32, 256), BF16),
            pltpu.VMEM((CH, NT, 32, 256), BF16),
            pltpu.VMEM((CH, NM, 8, 256), F32),
            pltpu.VMEM((CH, NM, 8, 256), F32),
            pltpu.VMEM((CH, NM, 8, 256), F32),
            dma((2,)),
            dma((2,)),
            dma((2,)),
            dma((2,)),
            dma((CH, NT)),
            dma((CH, NT)),
            dma((CH, NM)),
            dma((CH, NM)),
            dma((CH, NM)),
            dma((CH, NM)),
        ],
        compiler_params=pltpu.CompilerParams(
            collective_id=0, has_side_effects=True, vmem_limit_bytes=56 * 1024 * 1024
        ),
    )(
        noisy.reshape(512, 256),
        vec,
        gains,
        seam,
        key_lane,
        blk_lane,
        w_lift,
        w_fine,
        w_coarse,
        w_out,
    )
    denoised = den.reshape(N, B, 256).transpose(1, 0, 2).reshape(noisy.shape)
    stat = stat.reshape(N, 2, 4, 256)
    ens_mean = stat[:, 0].transpose(1, 0, 2)
    ens_spread = stat[:, 1].transpose(1, 0, 2)
    return (denoised, ens_mean, ens_spread)


def solution(mesh):
    placed = (
        P("mem", "tile", None, None),
        P("mem"),
        P("tile", None, None),
        P("tile", None, None),
        P(),
        P(),
        P("tile", None),
        P(),
        P(),
        P(),
        P(),
        P(),
        P(),
        P(),
        P(),
    )
    return jax.shard_map(
        on_device,
        mesh=mesh,
        in_specs=placed,
        out_specs=(P("mem", "tile", None, None), P("tile", None, None), P("tile", None, None)),
        check_vma=False,
    )
```

```python
import functools
import math

import jax
import jax.numpy as jnp
from jax import lax
from jax.experimental import pallas as pl
from jax.experimental.pallas import tpu as pltpu
from jax.sharding import PartitionSpec as P

STEPS = 1000
MESH = pl.DeviceIdType.MESH
F32 = jnp.float32
BF16 = jnp.bfloat16

B = 16
N = 32
H = N // 2
NT = 16
NM = 8
CH = 4
RC = N // CH


def dot(a, b):
    return jnp.dot(a, b, preferred_element_type=F32)


def twice(x):
    return jnp.concatenate([x, x], axis=-1)


def iota(shape, dim):
    return lax.broadcasted_iota(jnp.int32, shape, dim)


def act(x, ones, half_gain):
    mean = dot((x * x).astype(BF16), ones)
    h = x * lax.rsqrt(mean + 1e-06) * half_gain
    return (h + h * jnp.tanh(h)).astype(BF16)


def seam_perm(out_ref, seam_ref, side):
    tile = seam_ref[:, 3 * side : 3 * side + 1] & 7
    apart = iota((B, 256), 1) - ((iota((B, 256), 0) & 8) + tile)
    for c in range(256 // B):
        out_ref[side, c * B : (c + 1) * B, :] = jnp.where(apart == c * B, 1.0, 0.0).astype(BF16)


def from_side(perm, edge, n, flipped):
    if n * B > 256:
        edge = jnp.concatenate([edge[:256], edge[256:]], axis=1)
    got = dot(perm, edge)
    pieces = [
        got[c % H * B : (c % H + 1) * B, c // H * 128 : (c // H + 1) * 128] for c in range(n)
    ]
    return [jnp.where(flipped, pieces[n - 1 - c], pieces[c]) for c in range(n)]


def conv_weights(out_ref, w_ref):
    zero = jnp.zeros((128, 128), BF16)
    for i in range(3):
        for j in range(4):
            left = w_ref[3 * i + j] if j < 3 else zero
            right = w_ref[3 * i + j - 1] if j > 0 else zero
            start = (4 * i + j) * 128
            out_ref[start : start + 128, :] = jnp.concatenate([left, right], axis=1)


def conv_pair(a_ref, w, pair, start, rows):
    parts = []
    for i in range(3):
        for j in range(4):
            parts.append(a_ref[2 * pair + j, pl.ds(start + i * B, rows), :])
    return dot(jnp.concatenate(parts, axis=1), w)


def kernel(
    noisy_ref,
    vec_ref,
    gain_ref,
    seam_ref,
    key_ref,
    blk_ref,
    wl_ref,
    wf_ref,
    wc_ref,
    wo_ref,
    den_ref,
    stat_ref,
    nx,
    sx,
    lift_w,
    out_w,
    fine_w,
    coarse_w,
    ones_ref,
    to_rows,
    seam_w,
    slot_ref,
    sum_ref,
    halo,
    started,
    a1,
    fine,
    pooled,
    a2,
    halo2,
    coarse,
    g0,
    g1,
    act_s,
    edges,
    d_ref,
    send,
    recv,
    tgt,
    mrecv,
    gat,
    h_send,
    h_recv,
    c_send,
    c_recv,
    a_send,
    a_recv,
    m_send,
    m_recv,
    g_send,
    g_recv,
):
    pos = lax.axis_index("tile")
    mem = lax.axis_index("mem")
    east = lax.rem(pos + 1, NT)
    west = lax.rem(pos + NT - 1, NT)

    barrier = pltpu.get_barrier_semaphore()

    def greet_tile(d, _):
        pl.semaphore_signal(
            barrier, inc=1, device_id={"tile": lax.rem(pos + d, NT)}, device_id_type=MESH
        )
        return 0

    def greet_mem(d, _):
        pl.semaphore_signal(
            barrier, inc=1, device_id={"mem": lax.rem(mem + d, NM)}, device_id_type=MESH
        )
        return 0

    lax.fori_loop(1, NT, greet_tile, 0)
    lax.fori_loop(1, NM, greet_mem, 0)
    pl.semaphore_wait(barrier, NT - 1 + NM - 1)

    c_in, c_skip, c_out = twice(vec_ref[0]), twice(vec_ref[1]), twice(vec_ref[2])
    temb, frac_p, frac_q = twice(vec_ref[3]), twice(vec_ref[4]), twice(vec_ref[5])
    gain_fine = twice(gain_ref[0:1]) * 0.5
    gain_coarse = gain_ref[1:2] * 0.5
    gain_out = twice(gain_ref[2:3]) * 0.5

    def lift_row(r, _):
        lane = iota((B, 512), 1)
        want = iota((B, 512), 0) * N + r
        to_rows[pl.ds(pl.multiple_of(r * B, B), B), :] = jnp.where(want == lane, 1.0, 0.0).astype(
            BF16
        )
        return 0

    lax.fori_loop(0, N, lift_row, 0)
    ones_ref[...] = jnp.where(
        iota((256, 256), 0) // 128 == iota((256, 256), 1) // 128, 1.0 / 128, 0.0
    ).astype(BF16)
    wl = wl_ref[...].astype(F32)
    wl_zero = jnp.zeros_like(wl)
    wl_pair = jnp.concatenate(
        [
            jnp.concatenate([wl, wl_zero], axis=1),
            jnp.concatenate([wl_zero, wl], axis=1),
        ],
        axis=0,
    ).astype(BF16)
    for q in range(8):
        lift_w[q] = jnp.zeros((128, 256), BF16)
        lift_w[q, q * B : (q + 1) * B, :] = wl_pair
        for j in range(2):
            place = jnp.where(
                iota((8, 128), 1) == iota((8, 128), 0) + (16 * q + 8 * j), 1.0, 0.0
            ).astype(BF16)
            out_w[(2 * q + j) * 128 : (2 * q + j + 1) * 128, :] = dot(wo_ref[...], place).astype(BF16)
    for side in range(4):
        seam_perm(seam_w, seam_ref, side)
    flipped = [
        jnp.broadcast_to(seam_ref[:, 3 * side + 2 : 3 * side + 3], (B, 128)) == 1
        for side in range(4)
    ]
    conv_weights(fine_w, wf_ref)
    conv_weights(coarse_w, wc_ref)

    natural = noisy_ref[...]
    for s in range(2):
        rows = slice(s * 256, (s + 1) * 256)
        moved = dot(to_rows[rows, :], natural)
        nx[rows, :] = moved.astype(BF16)
        sx[rows, :] = (moved.reshape(H, B, 256) * c_in).reshape(256, 256).astype(BF16)

    to_west = pltpu.make_async_remote_copy(
        src_ref=nx.at[:, pl.ds(0, 128)],
        dst_ref=halo.at[0],
        send_sem=h_send.at[0],
        recv_sem=h_recv.at[0],
        device_id={"tile": west},
        device_id_type=MESH,
    )
    to_east = pltpu.make_async_remote_copy(
        src_ref=nx.at[:, pl.ds(128, 128)],
        dst_ref=halo.at[1],
        send_sem=h_send.at[1],
        recv_sem=h_recv.at[1],
        device_id={"tile": east},
        device_id_type=MESH,
    )
    to_west.start()
    to_east.start()

    def lift(step, _):
        for q in (2 * step, 2 * step + 1):
            for half in range(2):
                pair = half * 8 + q
                for s in range(2):
                    rows = slice(s * 256, (s + 1) * 256)
                    up = dot(sx[rows, half * 128 : (half + 1) * 128], lift_w[q])
                    first = (up.reshape(H, B, 256) + temb).reshape(256, 256).astype(BF16)
                    started[2 * pair, rows, :] = first[:, :128]
                    started[2 * pair + 1, rows, :] = first[:, 128:]
                    normed = act(first.astype(F32), ones_ref[...], gain_fine)
                    inner = slice(s * 256 + B, (s + 1) * 256 + B)
                    a1[2 * pair + 1, inner, :] = normed[:, :128]
                    a1[2 * pair + 2, inner, :] = normed[:, 128:]
        return 0

    lax.fori_loop(0, 4, lift, 0)

    def north_south(a_ref, side, n, row_from, row_to):
        edge = a_ref[1 : n + 1, row_from * B : (row_from + 1) * B, :].reshape(n * B, 128)
        got = from_side(seam_w[side], edge, n, flipped[side])
        rows = slice(row_to * B, (row_to + 1) * B)
        for c in range(n):
            a_ref[c + 1, rows, :] = got[c].astype(BF16)
        a_ref[0, rows, :] = got[0].astype(BF16)
        a_ref[n + 1, rows, :] = got[n - 1].astype(BF16)

    north_south(a1, 0, N, N, 0)
    north_south(a1, 2, N, 1, N + 1)
    to_west.wait()
    to_east.wait()
    sides = []
    for side, got, w in ((3, 1, lift_w[7, :, 128:256]), (1, 0, lift_w[0, :, 0:128])):
        moved = from_side(seam_w[side], halo[got], N, flipped[side])
        scaled = jnp.concatenate([(x * vec_ref[0]).astype(BF16) for x in moved], axis=0)
        sides.append(dot(scaled, w))
    up = jnp.concatenate(sides, axis=1)
    first = (up.reshape(N, B, 256) + temb).reshape(512, 256).astype(BF16)
    normed = act(first.astype(F32), ones_ref[...], gain_fine)
    a1[0, B : B + 512, :] = normed[:, :128]
    a1[N + 1, B : B + 512, :] = normed[:, 128:]

    def fine_conv(pair, buf):
        for s in range(2):
            buf[s * 256 : (s + 1) * 256, :] = conv_pair(a1, fine_w[...], pair, s * 256, 256)

    def fine_post(pair, buf):
        for s in range(2):
            rows = slice(s * 256, (s + 1) * 256)
            base = jnp.concatenate([started[2 * pair, rows, :], started[2 * pair + 1, rows, :]], axis=1)
            out = (base.astype(F32) + buf[rows, :]).astype(BF16)
            fine[2 * pair, rows, :] = out[:, :128]
            fine[2 * pair + 1, rows, :] = out[:, 128:]
            wide = out.astype(F32).reshape(H // 2, 2, B, 256)
            tall = wide[:, 0] + wide[:, 1]
            mean = ((tall[:, :, :128] + tall[:, :, 128:]) * 0.25).reshape(128, 128).astype(BF16)
            pooled[pair, s * 128 : (s + 1) * 128, :] = mean
            normed = act(mean.astype(F32), ones_ref[0:128, 0:128], gain_coarse)
            a2[pair + 1, s * 128 + B : (s + 1) * 128 + B, :] = normed

    def nth(i):
        return jnp.where(i == 0, 0, jnp.where(i == 1, H - 1, i - 1))

    def fine_step(q, _):
        fine_conv(nth(2 * q), g0)
        fine_post(nth(jnp.maximum(2 * q - 1, 0)), g1)
        fine_conv(nth(2 * q + 1), g1)
        fine_post(nth(2 * q), g0)
        return 0

    g1[...] = jnp.zeros((512, 256), F32)
    lax.fori_loop(0, 2, fine_step, 0)
    edges[0] = a2[1, B : B + 256, :]
    edges[1] = a2[H, B : B + 256, :]
    c_west = pltpu.make_async_remote_copy(
        src_ref=edges.at[0],
        dst_ref=halo2.at[0],
        send_sem=c_send.at[0],
        recv_sem=c_recv.at[0],
        device_id={"tile": west},
        device_id_type=MESH,
    )
    c_east = pltpu.make_async_remote_copy(
        src_ref=edges.at[1],
        dst_ref=halo2.at[1],
        send_sem=c_send.at[1],
        recv_sem=c_recv.at[1],
        device_id={"tile": east},
        device_id_type=MESH,
    )
    c_west.start()
    c_east.start()

    lax.fori_loop(2, 8, fine_step, 0)
    fine_post(H - 2, g1)

    north_south(a2, 0, H, H, 0)
    north_south(a2, 2, H, 1, H + 1)
    c_west.wait()
    c_east.wait()
    for side, got, column in ((1, 0, H + 1), (3, 1, 0)):
        moved = from_side(seam_w[side], halo2[got], H, flipped[side])
        for r in range(H):
            a2[column, (r + 1) * B : (r + 2) * B, :] = moved[r].astype(BF16)

    def coarse_loop(q, _):
        for pair in (2 * q, 2 * q + 1):
            got = conv_pair(a2, coarse_w[...], pair, 0, 256)
            base = jnp.concatenate([pooled[2 * pair], pooled[2 * pair + 1]], axis=1)
            out = (base.astype(F32) + got).astype(BF16)
            coarse[2 * pair] = out[:, :128]
            coarse[2 * pair + 1] = out[:, 128:]
        return 0

    lax.fori_loop(0, H // 4, coarse_loop, 0)

    i, j = iota((512, 128), 0), iota((512, 128), 1)
    slot_ref[...] = jnp.where(
        ((i >> 4) == key_ref[...]) & (((i >> 3) & 1) == ((j >> 3) & 1)) & ((i & 7) == (j >> 4)),
        1.0,
        0.0,
    ).astype(BF16)
    i, j = iota((64, 512), 0), iota((64, 512), 1)
    sum_ref[...] = jnp.where(
        ((i & 3) == blk_ref[...]) & (((i >> 2) & 1) == ((j >> 3) & 1)) & ((i >> 3) == (j & 7)),
        1.0,
        0.0,
    ).astype(BF16)

    rows_c = RC * B

    def a_copy(k, d):
        return pltpu.make_async_remote_copy(
            src_ref=send.at[k, d],
            dst_ref=recv.at[k, d],
            send_sem=a_send.at[k, d],
            recv_sem=a_recv.at[k, d],
            device_id={"tile": lax.rem(pos + d, NT)},
            device_id_type=MESH,
        )

    def m_copy(k, d):
        return pltpu.make_async_remote_copy(
            src_ref=tgt.at[k, lax.rem(mem + d, NM)],
            dst_ref=mrecv.at[k, d],
            send_sem=m_send.at[k, d],
            recv_sem=m_recv.at[k, d],
            device_id={"mem": lax.rem(mem + d, NM)},
            device_id_type=MESH,
        )

    def g_copy(k, d):
        return pltpu.make_async_remote_copy(
            src_ref=gat.at[k, mem],
            dst_ref=gat.at[k, mem],
            send_sem=g_send.at[k, d],
            recv_sem=g_recv.at[k, d],
            device_id={"mem": lax.rem(mem + d, NM)},
            device_id_type=MESH,
        )

    def each(count, what):
        def body(d, _):
            what(d)
            return 0

        lax.fori_loop(1, count, body, 0)

    def last_stage(k):
        start = k * rows_c

        for pair in range(H):
            f = jnp.concatenate(
                [fine[2 * pair, start : start + rows_c, :], fine[2 * pair + 1, start : start + rows_c, :]],
                axis=1,
            ).astype(F32)
            c = coarse[pair, start // 2 : (start + rows_c) // 2, :].astype(F32)
            c = c.reshape(RC // 2, 1, B, 128)
            c = jnp.concatenate([c, c], axis=1).reshape(rows_c, 128)
            act_s[:, pair * 256 : (pair + 1) * 256] = act(f + twice(c), ones_ref[...], gain_out)
        left = dot(act_s[:, :2048], out_w[...])
        right = dot(act_s[:, 2048:], out_w[...])
        proj = jnp.concatenate([left, right], axis=1).reshape(RC, B, 256)
        state = nx[start : start + rows_c, :].astype(F32).reshape(RC, B, 256)
        den = (c_skip * state + c_out * proj).reshape(rows_c, 256)
        d_ref[start : start + rows_c, :] = den
        den_ref[start : start + rows_c, :] = den
        if k == CH - 1:
            d_ref[N * B : (N + 1) * B, :] = den[rows_c - B :, :]
        below = d_ref[start + B : start + B + rows_c, :].reshape(RC, B, 256)
        mixed = (1.0 - frac_p) * den.reshape(RC, B, 256) + frac_p * below
        mixed = mixed.reshape(rows_c, 256)
        shifted = pltpu.roll(mixed, 248, 1)
        shifted = jnp.where(iota((rows_c, 256), 1) >= 248, mixed, shifted)
        out = (1.0 - frac_q) * mixed.reshape(RC, B, 256) + frac_q * shifted.reshape(RC, B, 256)
        blocks = dot(slot_ref[...], out.reshape(rows_c, 256).astype(BF16)).astype(BF16)
        blocks = blocks.reshape(NT, 32, 256)
        recv[k, 0] = blocks[0]
        send[k] = blocks
        each(NT, lambda d: a_copy(k, d).start())

    def sum_stage(k):
        each(NT, lambda d: a_copy(k, d).wait_recv())
        total = dot(sum_ref[...], recv[k].reshape(512, 256))
        tgt[k] = total.reshape(NM, 8, 256)
        mrecv[k, 0] = tgt[k, mem]
        each(NM, lambda d: m_copy(k, d).start())

    def stat_stage(k):
        each(NM, lambda d: m_copy(k, d).wait_recv())
        values = mrecv[k]
        total = jnp.sum(values, axis=0)
        mean = (total[0:4] + total[4:8]) * (1.0 / 16)
        dev = values - jnp.concatenate([mean, mean], axis=0)
        squares = jnp.sum(dev * dev, axis=0)
        spread = jnp.sqrt((squares[0:4] + squares[4:8]) / 15.0 + 1e-06)
        gat[k, mem] = jnp.concatenate([mean, spread], axis=0)
        each(NM, lambda d: g_copy(k, d).start())

    order = list(range(CH - 1, -1, -1))
    for step in range(CH + 2):
        if step < CH:
            last_stage(order[step])
        if 1 <= step < CH + 1:
            sum_stage(order[step - 1])
        if 2 <= step:
            stat_stage(order[step - 2])
    for k in order:
        each(NM, lambda d: g_copy(k, d).wait_recv())
    stat_ref[...] = gat[...]
    for k in order:
        each(NT, lambda d: a_copy(k, d).wait_send())
        each(NM, lambda d: m_copy(k, d).wait_send())
        each(NM, lambda d: g_copy(k, d).wait_send())


def precondition(timestep):
    fraction = timestep.astype(jnp.float32) / (STEPS - 1)
    high_root = 80.0 ** (1.0 / 7.0)
    low_root = 0.002 ** (1.0 / 7.0)
    sigma = (high_root + fraction * (low_root - high_root)) ** 7
    denominator = sigma * sigma + 1.0
    return (lax.rsqrt(denominator), 1.0 / denominator, sigma * lax.rsqrt(denominator))


def embed(timestep, w_time):
    half_width = w_time.shape[0] // 2
    frequency = jnp.exp(-math.log(10000.0) * jnp.arange(half_width, dtype=jnp.float32) / half_width)
    angles = timestep.astype(jnp.float32)[:, None] * frequency[None, :]
    features = jnp.concatenate([jnp.sin(angles), jnp.cos(angles)], axis=-1)
    return jax.nn.silu(jnp.dot(features, w_time, precision=lax.Precision.HIGHEST))


def on_device(
    noisy,
    timestep,
    seams,
    corner_list,
    route,
    target_block,
    frac,
    w_time,
    w_lift,
    w_fine,
    w_coarse,
    gain_fine,
    gain_coarse,
    gain_out,
    w_out,
):
    pos = lax.axis_index("tile")
    scales = precondition(timestep)
    temb = embed(timestep, w_time)

    def rows(x):
        return jnp.broadcast_to(jnp.repeat(x, 8)[:, None], (B, 128))

    def tiles(x):
        return jnp.broadcast_to(jnp.concatenate([x, x])[:, None], (B, 128))

    vec = jnp.stack(
        [rows(s) for s in scales]
        + [jnp.repeat(temb, 8, axis=0), tiles(frac[:, 0]), tiles(frac[:, 1])]
    )
    gains = jnp.stack([gain_fine, gain_coarse, gain_out])
    seam = seams.reshape(8, 12)
    seam = jnp.concatenate([seam, seam], axis=0)

    owners = route.reshape(NT, 8)
    same = owners[:, :, None] == owners[:, None, :]
    earlier = jnp.arange(8)[None, :, None] > jnp.arange(8)[None, None, :]
    rank = jnp.sum((same & earlier).astype(jnp.int32), axis=2)
    own_owner = lax.dynamic_index_in_dim(owners, pos, 0, False)
    own_rank = lax.dynamic_index_in_dim(rank, pos, 0, False)
    key = (own_owner - pos) % NT * 2 + own_rank
    key_lane = jnp.tile(key, 16)[None, :]
    blocks = target_block.reshape(NT, 8)
    mine = (owners == pos)[:, None, :] & (rank[:, None, :] == jnp.arange(2)[None, :, None])
    slot_block = jnp.max(jnp.where(mine, blocks[:, None, :], -1), axis=2)
    slot_block = jnp.take(slot_block, (pos - jnp.arange(NT)) % NT, axis=0)
    blk_lane = jnp.repeat(slot_block.reshape(32), 16)[None, :]

    vmem = pl.BlockSpec(memory_space=pltpu.VMEM)
    dma = pltpu.SemaphoreType.DMA
    den, stat = pl.pallas_call(
        kernel,
        out_shape=(
            jax.ShapeDtypeStruct((512, 256), F32),
            jax.ShapeDtypeStruct((CH, NM, 8, 256), F32),
        ),
        in_specs=[vmem] * 10,
        out_specs=(vmem, vmem),
        scratch_shapes=[
            pltpu.VMEM((512, 256), BF16),
            pltpu.VMEM((512, 256), BF16),
            pltpu.VMEM((8, 128, 256), BF16),
            pltpu.VMEM((2048, 128), BF16),
            pltpu.VMEM((1536, 256), BF16),
            pltpu.VMEM((1536, 256), BF16),
            pltpu.VMEM((256, 256), BF16),
            pltpu.VMEM((512, 512), BF16),
            pltpu.VMEM((4, 256, 256), BF16),
            pltpu.VMEM((512, 128), BF16),
            pltpu.VMEM((64, 512), BF16),
            pltpu.VMEM((2, 512, 128), BF16),
            pltpu.VMEM((N, 512, 128), BF16),
            pltpu.VMEM((N + 2, 544, 128), BF16),
            pltpu.VMEM((N, 512, 128), BF16),
            pltpu.VMEM((H, 256, 128), BF16),
            pltpu.VMEM((H + 2, 288, 128), BF16),
            pltpu.VMEM((2, 256, 128), BF16),
            pltpu.VMEM((H, 256, 128), BF16),
            pltpu.VMEM((512, 256), F32),
            pltpu.VMEM((512, 256), F32),
            pltpu.VMEM((RC * B, 4096), BF16),
            pltpu.VMEM((2, 256, 128), BF16),
            pltpu.VMEM(((N + 1) * B, 256), F32),
            pltpu.VMEM((CH, NT, 32, 256), BF16),
            pltpu.VMEM((CH, NT, 32, 256), BF16),
            pltpu.VMEM((CH, NM, 8, 256), F32),
            pltpu.VMEM((CH, NM, 8, 256), F32),
            pltpu.VMEM((CH, NM, 8, 256), F32),
            dma((2,)),
            dma((2,)),
            dma((2,)),
            dma((2,)),
            dma((CH, NT)),
            dma((CH, NT)),
            dma((CH, NM)),
            dma((CH, NM)),
            dma((CH, NM)),
            dma((CH, NM)),
        ],
        compiler_params=pltpu.CompilerParams(
            collective_id=0, has_side_effects=True, vmem_limit_bytes=36 * 1024 * 1024
        ),
    )(
        noisy.reshape(512, 256),
        vec,
        gains,
        seam,
        key_lane,
        blk_lane,
        w_lift,
        w_fine,
        w_coarse,
        w_out,
    )
    denoised = den.reshape(N, B, 256).transpose(1, 0, 2).reshape(noisy.shape)
    stat = stat.reshape(N, 2, 4, 256)
    ens_mean = stat[:, 0].transpose(1, 0, 2)
    ens_spread = stat[:, 1].transpose(1, 0, 2)
    return (denoised, ens_mean, ens_spread)


def solution(mesh):
    placed = (
        P("mem", "tile", None, None),
        P("mem"),
        P("tile", None, None),
        P("tile", None, None),
        P(),
        P(),
        P("tile", None),
        P(),
        P(),
        P(),
        P(),
        P(),
        P(),
        P(),
        P(),
    )
    return jax.shard_map(
        on_device,
        mesh=mesh,
        in_specs=placed,
        out_specs=(P("mem", "tile", None, None), P("tile", None, None), P("tile", None, None)),
        check_vma=False,
    )
```

```python
import functools
import math

import jax
import jax.numpy as jnp
from jax import lax
from jax.experimental import pallas as pl
from jax.experimental.pallas import tpu as pltpu
from jax.sharding import PartitionSpec as P

STEPS = 1000
MESH = pl.DeviceIdType.MESH
F32 = jnp.float32
BF16 = jnp.bfloat16

B = 16
N = 32
H = N // 2
NT = 16
NM = 8
DUMMY = H + 1
FIRST = 10
EARLY = 4
CHUNK = 128


def dot(a, b):
    return jnp.dot(a, b, preferred_element_type=F32)


def twice(x):
    return jnp.concatenate([x, x], axis=-1)


def iota(shape, dim):
    return lax.broadcasted_iota(jnp.int32, shape, dim)


def onehot(where):
    return jnp.where(where, 1.0, 0.0).astype(BF16)


def act(x, ones, half_gain):
    mean = dot((x * x).astype(BF16), ones)
    h = x * lax.rsqrt(mean + 1e-06) * half_gain
    return (h + h * jnp.tanh(h)).astype(BF16)


def column(row):
    spread = jnp.broadcast_to(row.astype(F32), (B, 8))
    own = iota((B, 8), 1) == (iota((B, 8), 0) & 7)
    return jnp.sum(jnp.where(own, spread, 0.0), axis=1, keepdims=True)


def from_side(perm, edge, n, flipped):
    rows = edge.shape[0]
    if rows > 256:
        edge = jnp.concatenate([edge[:256], edge[256:]], axis=1)
        got = dot(perm[...], edge)
        pieces = [
            got[c % H * B : (c % H + 1) * B, c // H * 128 : (c // H + 1) * 128] for c in range(n)
        ]
    else:
        got = dot(perm[:rows, :rows], edge)
        pieces = [got[c * B : (c + 1) * B] for c in range(n)]
    if edge.shape[1] > 128 and rows <= 256:
        flipped = twice(flipped)
    return [
        jnp.where(flipped > 0.5, pieces[n - 1 - c], pieces[c]) for c in range(n)
    ]


def conv_weights(out_ref, w_ref):
    zero = jnp.zeros((128, 128), BF16)
    for i in range(3):
        for j in range(4):
            left = w_ref[3 * i + j] if j < 3 else zero
            right = w_ref[3 * i + j - 1] if j > 0 else zero
            start = (4 * i + j) * 128
            out_ref[start : start + 128, :] = jnp.concatenate([left, right], axis=1)


def conv_pair(a_ref, w_ref, pair, rows):
    parts = []
    for i in range(3):
        for j in range(4):
            parts.append(a_ref[2 * pair + j, i * B : i * B + rows, :])
    return dot(jnp.concatenate(parts, axis=1), w_ref[...])


def each(count, what):
    def body(d, _):
        what(d)
        return 0

    lax.fori_loop(1, count, body, 0)


def kernel(
    noisy_ref,
    step_ref,
    seam_ref,
    route_ref,
    block_ref,
    frac_ref,
    wt_ref,
    wl_ref,
    wf_hbm,
    wc_hbm,
    gf_ref,
    gc_ref,
    go_ref,
    wo_ref,
    den_ref,
    stat_ref,
    wf_ref,
    wc_ref,
    nx,
    sx,
    lift_w,
    out_w,
    fine_w,
    coarse_w,
    ones_ref,
    seam_w,
    slot_ref,
    sum_ref,
    halo,
    started0,
    started1,
    a10,
    a11,
    fine0,
    fine1,
    pooled0,
    pooled1,
    a20,
    a21,
    coarse0,
    coarse1,
    halo2,
    edges,
    g0,
    g1,
    act_s,
    d_ref,
    send,
    recv,
    tgt,
    mrecv,
    gat,
    w_sem,
    h_send,
    h_recv,
    c_send,
    c_recv,
    a_send,
    a_recv,
    m_send,
    m_recv,
    g_send,
    g_recv,
):
    pos = lax.axis_index("tile")
    mem = lax.axis_index("mem")
    started, a1, fine = (started0, started1), (a10, a11), (fine0, fine1)
    pooled, a2, coarse = (pooled0, pooled1), (a20, a21), (coarse0, coarse1)

    def along_tile(d):
        return {"tile": lax.rem(pos + d, NT)}

    def along_mem(d):
        return {"mem": lax.rem(mem + d, NM)}

    barrier = pltpu.get_barrier_semaphore()

    def greet(where):
        pl.semaphore_signal(barrier, inc=1, device_id=where, device_id_type=MESH)

    each(NT, lambda d: greet(along_tile(d)))
    each(NM, lambda d: greet(along_mem(d)))

    load_fine = pltpu.make_async_copy(wf_hbm, wf_ref, w_sem.at[0])
    load_coarse = pltpu.make_async_copy(wc_hbm, wc_ref, w_sem.at[1])
    load_fine.start()
    load_coarse.start()

    ones_ref[...] = jnp.where(
        iota((256, 256), 0) // 128 == iota((256, 256), 1) // 128, 1.0 / 128, 0.0
    ).astype(BF16)
    wl = wl_ref[...].astype(F32)
    wl_zero = jnp.zeros_like(wl)
    wl_pair = jnp.concatenate(
        [
            jnp.concatenate([wl, wl_zero], axis=1),
            jnp.concatenate([wl_zero, wl], axis=1),
        ],
        axis=0,
    ).astype(BF16)
    for q in range(8):
        lift_w[q] = jnp.zeros((128, 256), BF16)
        lift_w[q, q * B : (q + 1) * B, :] = wl_pair

    level = jnp.where(iota((8, 128), 0) < 4, step_ref[0], step_ref[1]).astype(F32)
    fraction = level / (STEPS - 1)
    high_root = 80.0 ** (1.0 / 7.0)
    low_root = 0.002 ** (1.0 / 7.0)
    root = high_root + fraction * (low_root - high_root)
    square = root * root
    sigma = square * square * square * root
    denominator = sigma * sigma + 1.0
    scales = (lax.rsqrt(denominator), 1.0 / denominator, sigma * lax.rsqrt(denominator))
    c_in, c_skip, c_out = [[twice(x[0:1]), twice(x[4:5])] for x in scales]
    lane = iota((8, 128), 1)
    frequency = jnp.exp((lane & 63).astype(F32) * (-math.log(10000.0) / 64))
    angles = level * frequency
    features = jnp.where(lane < 64, jnp.sin(angles), jnp.cos(angles))
    embedded = jnp.dot(
        features, wt_ref[...], preferred_element_type=F32, precision=lax.Precision.HIGHEST
    )
    embedded = embedded / (1.0 + jnp.exp(-embedded))
    temb = [twice(embedded[0:1]), twice(embedded[4:5])]
    gain_fine = twice(gf_ref[...]) * 0.5
    gain_coarse = gc_ref[...] * 0.5
    gain_out = twice(go_ref[...]) * 0.5

    i = iota((256, 256), 0)
    to_rows = onehot(((i & 7) * N + ((i >> 3) & 1) * H + (i >> 4)) == iota((256, 256), 1))
    for m in range(2):
        moved = dot(to_rows, noisy_ref[m * 256 : (m + 1) * 256, :])
        nx[m * 256 : (m + 1) * 256, :] = moved.astype(BF16)
        sx[m * 256 : (m + 1) * 256, :] = (moved * c_in[m]).astype(BF16)

    def lift(m):
        def body(step, _):
            for q in (2 * step, 2 * step + 1):
                for half in range(2):
                    pair = half * 8 + q
                    cells = sx[m * 256 : (m + 1) * 256, half * 128 : (half + 1) * 128]
                    first = (dot(cells, lift_w[q]) + temb[m]).astype(BF16)
                    started[m][2 * pair] = first[:, :128]
                    started[m][2 * pair + 1] = first[:, 128:]
                    normed = act(first.astype(F32), ones_ref[...], gain_fine)
                    a1[m][2 * pair + 1, B : B + 256, :] = normed[:, :128]
                    a1[m][2 * pair + 2, B : B + 256, :] = normed[:, 128:]
            return 0

        lax.fori_loop(0, 4, body, 0)

    lift(0)

    half = iota((B, 1), 0) >> 3
    own = iota((B, 1), 0) & 7
    flipped = []
    for side in range(4):
        tile = column(seam_ref[0, side : side + 1, :] & 7).astype(jnp.int32)
        flag = column(seam_ref[2, side : side + 1, :]).astype(jnp.int32)
        if side == 0:
            source = jnp.where(half == 0, 8 + tile, own)
            flag = jnp.where(half == 0, flag, 0)
        elif side == 2:
            source = jnp.where(half == 0, 8 + own, tile)
            flag = jnp.where(half == 0, 0, flag)
        else:
            source = ((half + flag) & 1) * 8 + tile
        flipped.append(jnp.broadcast_to(flag.astype(F32), (B, 128)))
        apart = iota((B, 256), 1) - source
        for c in range(256 // B):
            seam_w[side, c * B : (c + 1) * B, :] = onehot(apart == c * B)

    def north_south(a_ref, cols, rows):
        for side, row_from, row_to in ((0, rows, 0), (2, 1, rows + 1)):
            edge = a_ref[1 : cols + 1, row_from * B : (row_from + 1) * B, :]
            got = from_side(seam_w.at[side], edge.reshape(cols * B, 128), cols, flipped[side])
            for c in range(cols):
                a_ref[c + 1, row_to * B : (row_to + 1) * B, :] = got[c].astype(BF16)

    def corners(a_ref, cols, rows):
        for col, inner in ((0, 1), (cols + 1, cols)):
            north = a_ref[inner, 0:B, :].astype(F32)
            south = a_ref[inner, (rows + 1) * B : (rows + 2) * B, :].astype(F32)
            last = a_ref[col, rows * B : (rows + 1) * B, :].astype(F32)
            first = a_ref[col, B : 2 * B, :].astype(F32)
            a_ref[col, 0:B, :] = jnp.concatenate([north[:8], last[:8]], axis=0).astype(BF16)
            a_ref[col, (rows + 1) * B : (rows + 2) * B, :] = jnp.concatenate(
                [first[8:], south[8:]], axis=0
            ).astype(BF16)

    north_south(a10, N, H)
    load_fine.wait()
    conv_weights(fine_w, wf_ref)
    lift(1)

    pl.semaphore_wait(barrier, NT - 1 + NM - 1)

    def h_copy(side):
        return pltpu.make_async_remote_copy(
            src_ref=nx.at[:, pl.ds(side * 128, 128)],
            dst_ref=halo.at[side],
            send_sem=h_send.at[side],
            recv_sem=h_recv.at[side],
            device_id=along_tile(1 if side else NT - 1),
            device_id_type=MESH,
        )

    def c_copy(m, side):
        return pltpu.make_async_remote_copy(
            src_ref=edges.at[m, side],
            dst_ref=halo2.at[m, side],
            send_sem=c_send.at[m, side],
            recv_sem=c_recv.at[m, side],
            device_id=along_tile(1 if side else NT - 1),
            device_id_type=MESH,
        )

    for side in range(2):
        h_copy(side).start()

    def fine_post(m, pair, buf):
        base = jnp.concatenate([started[m][2 * pair], started[m][2 * pair + 1]], axis=1)
        out = (base.astype(F32) + buf[...]).astype(BF16)
        fine[m][2 * pair] = out[:, :128]
        fine[m][2 * pair + 1] = out[:, 128:]
        wide = out.astype(F32).reshape(H // 2, 2, B, 256)
        tall = wide[:, 0] + wide[:, 1]
        mean = ((tall[:, :, :128] + tall[:, :, 128:]) * 0.25).reshape(128, 128).astype(BF16)
        pooled[m][pair] = mean
        a2[m][pair + 1, B : B + 128, :] = act(mean.astype(F32), ones_ref[0:128, 0:128], gain_coarse)

    def fine_pairs(m, count, nth):
        def body(q, _):
            g0[...] = conv_pair(a1[m], fine_w, nth(2 * q), 256)
            fine_post(m, jnp.where(q == 0, DUMMY, nth(2 * q - 1)), g1)
            g1[...] = conv_pair(a1[m], fine_w, nth(2 * q + 1), 256)
            fine_post(m, nth(2 * q), g0)
            return 0

        lax.fori_loop(0, count // 2, body, 0)
        fine_post(m, nth(count - 1), g1)

    def ends(i):
        return i * (H - 1)

    def send_edges(m):
        edges[m, 0] = a2[m][1, B : B + 128, :]
        edges[m, 1] = a2[m][H, B : B + 128, :]
        for side in range(2):
            c_copy(m, side).start()

    g1[...] = jnp.zeros((256, 256), F32)
    fine_pairs(0, H - 2, lambda i: i + 1)

    north_south(a11, N, H)
    for side in range(2):
        h_copy(side).wait()
    sides = []
    for side, got, w in ((3, 1, lift_w[7, :, 128:256]), (1, 0, lift_w[0, :, 0:128])):
        both = jnp.concatenate([halo[got, 0:256, :], halo[got, 256:512, :]], axis=1)
        moved = jnp.concatenate(from_side(seam_w.at[side], both, H, flipped[side]), axis=0)
        sides.append(
            [
                dot((moved[:, m * 128 : (m + 1) * 128] * c_in[m][:, :128]).astype(BF16), w)
                for m in range(2)
            ]
        )
    for m in range(2):
        first = (jnp.concatenate([sides[0][m], sides[1][m]], axis=1) + temb[m]).astype(BF16)
        normed = act(first.astype(F32), ones_ref[...], gain_fine)
        a1[m][0, B : B + 256, :] = normed[:, :128]
        a1[m][N + 1, B : B + 256, :] = normed[:, 128:]
        corners(a1[m], N, H)

    fine_pairs(0, 2, ends)
    send_edges(0)
    fine_pairs(1, 2, ends)
    send_edges(1)
    load_coarse.wait()
    conv_weights(coarse_w, wc_ref)
    for q in range(8):
        for j in range(2):
            place = onehot(iota((8, 128), 1) == iota((8, 128), 0) + (16 * q + 8 * j))
            out_w[(2 * q + j) * 128 : (2 * q + j + 1) * 128, :] = lax.dot_general(
                wo_ref[...], place, (((0,), (0,)), ((), ())), preferred_element_type=F32
            ).astype(BF16)
    frac_p, frac_q = [
        jnp.broadcast_to(column(frac_ref[k : k + 1, :]), (B, 256)) for k in range(2)
    ]

    route = jnp.broadcast_to(route_ref[...], (8, 128))
    rank = jnp.zeros((8, 128), jnp.int32)
    for s in range(1, 8):
        again = (pltpu.roll(route, s, 1) == route) & ((lane & 7) >= s)
        rank = rank + jnp.where(again, 1, 0)
    key = ((route - pos) & (NT - 1)) * 2 + rank
    pick = onehot(iota((128, 128), 0) == pos * 8 + (iota((128, 128), 1) & 7))
    key = dot(key.astype(F32).astype(BF16), pick)[0:1, :]
    i, j = iota((512, 128), 0), iota((512, 128), 1)
    slot_ref[...] = onehot(
        ((i >> 4).astype(F32) == key) & (((i >> 3) & 1) == ((j >> 3) & 1)) & ((i & 7) == (j >> 4))
    )
    slot = jnp.where(route == pos, ((pos - (lane >> 3)) & (NT - 1)) * 2 + rank, -1).astype(F32)
    diagonal = iota((128, 128), 0) == iota((128, 128), 1)
    slot = jnp.sum(jnp.where(diagonal, slot[0:1, :], 0.0), axis=1, keepdims=True)
    pick = onehot(slot == (iota((128, 512), 1) >> 4).astype(F32))
    block = jnp.broadcast_to(block_ref[...], (8, 128)).astype(F32) + 1.0
    block = dot(block.astype(BF16), pick)[0:1, :]
    i, j = iota((64, 512), 0), iota((64, 512), 1)
    sum_ref[...] = onehot(
        (((i & 3) + 1).astype(F32) == block)
        & (((i >> 2) & 1) == ((j >> 3) & 1))
        & ((i >> 3) == (j & 7))
    )

    def a_copy(k, d):
        return pltpu.make_async_remote_copy(
            src_ref=send.at[k, d],
            dst_ref=recv.at[k, d],
            send_sem=a_send.at[k, d],
            recv_sem=a_recv.at[k, d],
            device_id=along_tile(d),
            device_id_type=MESH,
        )

    def m_copy(m, d):
        return pltpu.make_async_remote_copy(
            src_ref=tgt.at[m, lax.rem(mem + d, NM)],
            dst_ref=mrecv.at[m, d],
            send_sem=m_send.at[m, d],
            recv_sem=m_recv.at[m, d],
            device_id=along_mem(d),
            device_id_type=MESH,
        )

    def g_copy(d):
        return pltpu.make_async_remote_copy(
            src_ref=gat.at[mem],
            dst_ref=gat.at[mem],
            send_sem=g_send.at[d],
            recv_sem=g_recv.at[d],
            device_id=along_mem(d),
            device_id_type=MESH,
        )

    def coarse_level(m):
        north_south(a2[m], H, H // 2)
        for side in range(2):
            c_copy(m, side).wait()
        for side, got, col in ((1, 0, H + 1), (3, 1, 0)):
            moved = from_side(seam_w.at[side], halo2[m, got], H // 2, flipped[side])
            for r in range(H // 2):
                a2[m][col, (r + 1) * B : (r + 2) * B, :] = moved[r].astype(BF16)
        corners(a2[m], H, H // 2)

        def body(q, _):
            for pair in (4 * q, 4 * q + 1, 4 * q + 2, 4 * q + 3):
                got = conv_pair(a2[m], coarse_w, pair, 128)
                base = jnp.concatenate([pooled[m][2 * pair], pooled[m][2 * pair + 1]], axis=1)
                out = (base.astype(F32) + got).astype(BF16)
                coarse[m][2 * pair] = out[:, :128]
                coarse[m][2 * pair + 1] = out[:, 128:]
            return 0

        lax.fori_loop(0, 2, body, 0)

    def state(m, row, count):
        start, rows = row * B, count * B
        for pair in range(H):
            f = jnp.concatenate(
                [
                    fine[m][2 * pair, start : start + rows, :],
                    fine[m][2 * pair + 1, start : start + rows, :],
                ],
                axis=1,
            ).astype(F32)
            c = coarse[m][pair, start // 2 : (start + rows) // 2, :].astype(F32)
            c = c.reshape(count // 2, 1, B, 128)
            c = jnp.concatenate([c, c], axis=1).reshape(rows, 128)
            act_s[:rows, pair * 256 : (pair + 1) * 256] = act(f + twice(c), ones_ref[...], gain_out)
        left = dot(act_s[:rows, :2048], out_w[...])
        right = dot(act_s[:rows, 2048:], out_w[...])
        proj = jnp.concatenate([left, right], axis=1)
        cells = slice(m * 256 + start, m * 256 + start + rows)
        den = c_skip[m] * nx[cells, :].astype(F32) + c_out[m] * proj
        d_ref[start : start + rows, :] = den
        den_ref[cells, :] = den

    def route_rows(m, k):
        start = k * CHUNK
        den = d_ref[start : start + CHUNK, :].reshape(8, B, 256)
        below = d_ref[start + B : start + B + CHUNK, :].reshape(8, B, 256)
        mixed = ((1.0 - frac_p) * den + frac_p * below).reshape(CHUNK, 256)
        shifted = pltpu.roll(mixed, 248, 1)
        shifted = jnp.where(iota((CHUNK, 256), 1) >= 248, mixed, shifted)
        out = (1.0 - frac_q) * mixed.reshape(8, B, 256) + frac_q * shifted.reshape(8, B, 256)
        blocks = dot(slot_ref[...], out.reshape(CHUNK, 256).astype(BF16)).astype(BF16)
        blocks = blocks.reshape(NT, 32, 256)
        recv[2 * m + k, 0] = blocks[0]
        send[2 * m + k] = blocks
        each(NT, lambda d: a_copy(2 * m + k, d).start())

    def last_stage(m):
        state(m, 0, FIRST)
        route_rows(m, 0)
        state(m, FIRST, H - FIRST)
        d_ref[H * B :, :] = jnp.concatenate([d_ref[8:16, :], d_ref[H * B - 8 : H * B, :]], axis=0)
        route_rows(m, 1)

    def sum_stage(m):
        for k in range(2):
            each(NT, lambda d: a_copy(2 * m + k, d).wait_recv())
            total = dot(sum_ref[...], recv[2 * m + k].reshape(512, 256))
            tgt[m, :, k] = total.reshape(NM, 8, 256)
        mrecv[m, 0] = tgt[m, mem]
        each(NM, lambda d: m_copy(m, d).start())

    fine_pairs(1, EARLY, lambda i: i + 1)
    coarse_level(0)
    last_stage(0)
    fine_pairs(1, H - 2 - EARLY, lambda i: i + 1 + EARLY)
    coarse_level(1)
    last_stage(1)
    sum_stage(0)
    sum_stage(1)

    for m in range(2):
        each(NM, lambda d: m_copy(m, d).wait_recv())
    total = jnp.zeros((2, 8, 256), F32)
    for m in range(2):
        for d in range(NM):
            total = total + mrecv[m, d]
    mean = total * (1.0 / 16)
    squares = jnp.zeros((2, 8, 256), F32)
    for m in range(2):
        for d in range(NM):
            dev = mrecv[m, d] - mean
            squares = squares + dev * dev
    gat[mem, 0] = mean
    gat[mem, 1] = jnp.sqrt(squares / 15.0 + 1e-06)
    each(NM, lambda d: g_copy(d).start())
    each(NM, lambda d: g_copy(d).wait_recv())
    stat_ref[...] = gat[...]
    for k in range(4):
        each(NT, lambda d: a_copy(k, d).wait_send())
    for m in range(2):
        each(NM, lambda d: m_copy(m, d).wait_send())
    each(NM, lambda d: g_copy(d).wait_send())


def on_device(
    noisy,
    timestep,
    seams,
    corner_list,
    route,
    target_block,
    frac,
    w_time,
    w_lift,
    w_fine,
    w_coarse,
    gain_fine,
    gain_coarse,
    gain_out,
    w_out,
):
    vmem = pl.BlockSpec(memory_space=pltpu.VMEM)
    smem = pl.BlockSpec(memory_space=pltpu.SMEM)
    hbm = pl.BlockSpec(memory_space=pltpu.HBM)
    dma = pltpu.SemaphoreType.DMA
    den, stat = pl.pallas_call(
        kernel,
        out_shape=(
            jax.ShapeDtypeStruct((512, 256), F32),
            jax.ShapeDtypeStruct((NM, 2, 2, 8, 256), F32),
        ),
        in_specs=[vmem, smem] + [vmem] * 6 + [hbm] * 2 + [vmem] * 4,
        out_specs=(vmem, vmem),
        scratch_shapes=[
            pltpu.VMEM((9, 128, 128), BF16),
            pltpu.VMEM((9, 128, 128), BF16),
            pltpu.VMEM((512, 256), BF16),
            pltpu.VMEM((512, 256), BF16),
            pltpu.VMEM((8, 128, 256), BF16),
            pltpu.VMEM((2048, 128), BF16),
            pltpu.VMEM((1536, 256), BF16),
            pltpu.VMEM((1536, 256), BF16),
            pltpu.VMEM((256, 256), BF16),
            pltpu.VMEM((4, 256, 256), BF16),
            pltpu.VMEM((512, 128), BF16),
            pltpu.VMEM((64, 512), BF16),
            pltpu.VMEM((2, 512, 128), BF16),
        ]
        + [pltpu.VMEM((2 * DUMMY + 2, 256, 128), BF16)] * 2
        + [pltpu.VMEM((N + 2, 288, 128), BF16)] * 2
        + [pltpu.VMEM((2 * DUMMY + 2, 256, 128), BF16)] * 2
        + [pltpu.VMEM((DUMMY + 1, 128, 128), BF16)] * 2
        + [pltpu.VMEM((DUMMY + 2, 160, 128), BF16)] * 2
        + [pltpu.VMEM((H, 128, 128), BF16)] * 2
        + [
            pltpu.VMEM((2, 2, 128, 128), BF16),
            pltpu.VMEM((2, 2, 128, 128), BF16),
            pltpu.VMEM((256, 256), F32),
            pltpu.VMEM((256, 256), F32),
            pltpu.VMEM((FIRST * B, 4096), BF16),
            pltpu.VMEM(((H + 1) * B, 256), F32),
            pltpu.VMEM((4, NT, 32, 256), BF16),
            pltpu.VMEM((4, NT, 32, 256), BF16),
            pltpu.VMEM((2, NM, 2, 8, 256), F32),
            pltpu.VMEM((2, NM, 2, 8, 256), F32),
            pltpu.VMEM((NM, 2, 2, 8, 256), F32),
            dma((2,)),
            dma((2,)),
            dma((2,)),
            dma((2, 2)),
            dma((2, 2)),
            dma((4, NT)),
            dma((4, NT)),
            dma((2, NM)),
            dma((2, NM)),
            dma((NM,)),
            dma((NM,)),
        ],
        compiler_params=pltpu.CompilerParams(
            collective_id=0, has_side_effects=True, vmem_limit_bytes=36 * 1024 * 1024
        ),
    )(
        noisy.reshape(512, 256),
        timestep,
        seams.transpose(2, 1, 0),
        route.reshape(1, 128),
        target_block.reshape(1, 128),
        frac.T,
        w_time,
        w_lift,
        w_fine,
        w_coarse,
        gain_fine.reshape(1, 128),
        gain_coarse.reshape(1, 128),
        gain_out.reshape(1, 128),
        w_out.T,
    )
    denoised = den.reshape(2, H, 2, 8, 256).transpose(0, 3, 2, 1, 4).reshape(noisy.shape)
    stat = stat.reshape(NM, 2, 2, 2, 4, 256).transpose(1, 4, 3, 2, 0, 5).reshape(2, 4, N, 256)
    return (denoised, stat[0], stat[1])


def solution(mesh):
    placed = (
        P("mem", "tile", None, None),
        P("mem"),
        P("tile", None, None),
        P("tile", None, None),
        P(),
        P(),
        P("tile", None),
        P(),
        P(),
        P(),
        P(),
        P(),
        P(),
        P(),
        P(),
    )
    return jax.shard_map(
        on_device,
        mesh=mesh,
        in_specs=placed,
        out_specs=(P("mem", "tile", None, None), P("tile", None, None), P("tile", None, None)),
        check_vma=False,
    )
```

```python
import functools
import math

import jax
import jax.numpy as jnp
from jax import lax
from jax.experimental import pallas as pl
from jax.experimental.pallas import tpu as pltpu
from jax.sharding import PartitionSpec as P

STEPS = 1000
MESH = pl.DeviceIdType.MESH
F32 = jnp.float32
BF16 = jnp.bfloat16

B = 16
N = 32
H = N // 2
NT = 16
NM = 8
NY = NM // 2
FIRST = 10
CHUNK = 128


def dot(a, b):
    return jnp.dot(a, b, preferred_element_type=F32)


def twice(x):
    return jnp.concatenate([x, x], axis=-1)


def iota(shape, dim):
    return lax.broadcasted_iota(jnp.int32, shape, dim)


def onehot(where):
    return jnp.where(where, 1.0, 0.0).astype(BF16)


def act(x, ones, half_gain):
    short = x.astype(BF16)
    mean = dot(short * short, ones)
    h = x.astype(F32) * lax.rsqrt(mean + 1e-06) * half_gain
    return (h + h * jnp.tanh(h)).astype(BF16)


def column(row):
    spread = jnp.broadcast_to(row.astype(F32), (B, 8))
    own = iota((B, 8), 1) == (iota((B, 8), 0) & 7)
    return jnp.sum(jnp.where(own, spread, 0.0), axis=1, keepdims=True)


def from_side(perm, edge, n, flipped):
    rows = edge.shape[0]
    if rows > 256:
        edge = jnp.concatenate([edge[:256], edge[256:]], axis=1)
        got = dot(perm[...], edge)
        pieces = [
            got[c % H * B : (c % H + 1) * B, c // H * 128 : (c // H + 1) * 128] for c in range(n)
        ]
    else:
        got = dot(perm[:rows, :rows], edge)
        pieces = [got[c * B : (c + 1) * B] for c in range(n)]
    if edge.shape[1] > 128 and rows <= 256:
        flipped = twice(flipped)
    return [
        jnp.where(flipped > 0.5, pieces[n - 1 - c], pieces[c]) for c in range(n)
    ]


def conv_weights(out_ref, w_ref):
    zero = jnp.zeros((128, 128), BF16)
    for i in range(3):
        for j in range(4):
            left = w_ref[3 * i + j] if j < 3 else zero
            right = w_ref[3 * i + j - 1] if j > 0 else zero
            start = (4 * i + j) * 128
            out_ref[start : start + 128, :] = jnp.concatenate([left, right], axis=1)


def conv_pair(a_ref, w_ref, pair, rows):
    parts = []
    for i in range(3):
        for j in range(4):
            parts.append(a_ref[2 * pair + j, i * B : i * B + rows, :])
    return dot(jnp.concatenate(parts, axis=1), w_ref[...])


def each(count, what):
    def body(d, _):
        what(d)
        return 0

    lax.fori_loop(1, count, body, 0)


def kernel(
    noisy_ref,
    step_ref,
    seam_ref,
    route_ref,
    block_ref,
    frac_ref,
    wt_ref,
    wl_ref,
    wf_hbm,
    wc_hbm,
    gf_ref,
    gc_ref,
    go_ref,
    wo_ref,
    den_hbm,
    stat_hbm,
    wf_ref,
    wc_ref,
    nx,
    sx,
    lift_w,
    out_w,
    fine_w,
    coarse_w,
    ones_ref,
    seam_w,
    slot_ref,
    sum_ref,
    halo,
    started0,
    started1,
    a10,
    a11,
    fine0,
    fine1,
    pooled0,
    pooled1,
    a20,
    a21,
    coarse0,
    coarse1,
    halo2,
    edges,
    g0,
    g1,
    act_s,
    d_ref0,
    d_ref1,
    by_row,
    den_ref,
    stat_ref,
    send,
    recv,
    target,
    other,
    w_sem,
    o_sem,
    h_send,
    h_recv,
    c_send,
    c_recv,
    a_send,
    a_recv,
    m_send,
    m_recv,
    x_send,
    x_recv,
):
    pos = lax.axis_index("tile")
    mem = lax.axis_index("mem")
    started, a1, fine = (started0, started1), (a10, a11), (fine0, fine1)
    pooled, a2, coarse = (pooled0, pooled1), (a20, a21), (coarse0, coarse1)
    d_ref = (d_ref0, d_ref1)

    def along_tile(d):
        return {"tile": lax.rem(pos + d, NT)}

    def along_y(d):
        return {"mem": lax.rem(mem + 2 * d, NM)}

    other_core = {"mem": mem + 1 - 2 * lax.rem(mem, 2)}

    barrier = pltpu.get_barrier_semaphore()

    def greet(where):
        pl.semaphore_signal(barrier, inc=1, device_id=where, device_id_type=MESH)

    each(NT, lambda d: greet(along_tile(d)))
    each(NY, lambda d: greet(along_y(d)))
    greet(other_core)

    load_fine = pltpu.make_async_copy(wf_hbm, wf_ref, w_sem.at[0])
    load_coarse = pltpu.make_async_copy(wc_hbm, wc_ref, w_sem.at[1])
    load_fine.start()
    load_coarse.start()

    ones_ref[...] = jnp.where(
        iota((256, 256), 0) // 128 == iota((256, 256), 1) // 128, 1.0 / 128, 0.0
    ).astype(BF16)
    wl = wl_ref[...].astype(F32)
    wl_zero = jnp.zeros_like(wl)
    wl_pair = jnp.concatenate(
        [
            jnp.concatenate([wl, wl_zero], axis=1),
            jnp.concatenate([wl_zero, wl], axis=1),
        ],
        axis=0,
    ).astype(BF16)
    for q in range(8):
        lift_w[q] = jnp.zeros((128, 256), BF16)
        lift_w[q, q * B : (q + 1) * B, :] = wl_pair

    level = jnp.where(iota((8, 128), 0) < 4, step_ref[0], step_ref[1]).astype(F32)
    fraction = level / (STEPS - 1)
    high_root = 80.0 ** (1.0 / 7.0)
    low_root = 0.002 ** (1.0 / 7.0)
    root = high_root + fraction * (low_root - high_root)
    square = root * root
    sigma = square * square * square * root
    denominator = sigma * sigma + 1.0
    scales = (lax.rsqrt(denominator), 1.0 / denominator, sigma * lax.rsqrt(denominator))
    c_in, c_skip, c_out = [[twice(x[0:1]), twice(x[4:5])] for x in scales]
    lane = iota((8, 128), 1)
    frequency = jnp.exp((lane & 63).astype(F32) * (-math.log(10000.0) / 64))
    angles = level * frequency
    features = jnp.where(lane < 64, jnp.sin(angles), jnp.cos(angles))
    embedded = jnp.dot(
        features, wt_ref[...], preferred_element_type=F32, precision=lax.Precision.HIGHEST
    )
    embedded = embedded / (1.0 + jnp.exp(-embedded))
    temb = [twice(embedded[0:1]), twice(embedded[4:5])]
    gain_fine = twice(gf_ref[...]) * 0.5
    gain_coarse = gc_ref[...] * 0.5
    gain_out = twice(go_ref[...]) * 0.5

    i = iota((256, 256), 0)
    to_rows = onehot(((i & 7) * N + ((i >> 3) & 1) * H + (i >> 4)) == iota((256, 256), 1))
    for m in range(2):
        moved = dot(to_rows, noisy_ref[m * 256 : (m + 1) * 256, :])
        nx[m * 256 : (m + 1) * 256, :] = moved.astype(BF16)
        sx[m * 256 : (m + 1) * 256, :] = (moved * c_in[m]).astype(BF16)

    def lift(m):
        for q in range(8):
            for half in range(2):
                pair = half * 8 + q
                cells = sx[m * 256 : (m + 1) * 256, half * 128 : (half + 1) * 128]
                first = (dot(cells, lift_w[q]) + temb[m]).astype(BF16)
                started[m][2 * pair] = first[:, :128]
                started[m][2 * pair + 1] = first[:, 128:]
                normed = act(first, ones_ref[...], gain_fine)
                a1[m][2 * pair + 1, B : B + 256, :] = normed[:, :128]
                a1[m][2 * pair + 2, B : B + 256, :] = normed[:, 128:]

    lift(0)

    pl.semaphore_wait(barrier, NT - 1 + NY)

    def h_copy(side):
        return pltpu.make_async_remote_copy(
            src_ref=nx.at[:, pl.ds(side * 128, 128)],
            dst_ref=halo.at[side],
            send_sem=h_send.at[side],
            recv_sem=h_recv.at[side],
            device_id=along_tile(1 if side else NT - 1),
            device_id_type=MESH,
        )

    def c_copy(m, side):
        return pltpu.make_async_remote_copy(
            src_ref=edges.at[m, side],
            dst_ref=halo2.at[m, side],
            send_sem=c_send.at[m, side],
            recv_sem=c_recv.at[m, side],
            device_id=along_tile(1 if side else NT - 1),
            device_id_type=MESH,
        )

    for side in range(2):
        h_copy(side).start()

    half = iota((B, 1), 0) >> 3
    own = iota((B, 1), 0) & 7
    flipped = []
    for side in range(4):
        tile = column(seam_ref[0, side : side + 1, :] & 7).astype(jnp.int32)
        flag = column(seam_ref[2, side : side + 1, :]).astype(jnp.int32)
        if side == 0:
            source = jnp.where(half == 0, 8 + tile, own)
            flag = jnp.where(half == 0, flag, 0)
        elif side == 2:
            source = jnp.where(half == 0, 8 + own, tile)
            flag = jnp.where(half == 0, 0, flag)
        else:
            source = ((half + flag) & 1) * 8 + tile
        flipped.append(jnp.broadcast_to(flag.astype(F32), (B, 128)))
        apart = iota((B, 256), 1) - source
        for c in range(256 // B):
            seam_w[side, c * B : (c + 1) * B, :] = onehot(apart == c * B)

    def north_south(a_ref, cols, rows):
        for side, row_from, row_to in ((0, rows, 0), (2, 1, rows + 1)):
            edge = a_ref[1 : cols + 1, row_from * B : (row_from + 1) * B, :]
            got = from_side(seam_w.at[side], edge.reshape(cols * B, 128), cols, flipped[side])
            for c in range(cols):
                a_ref[c + 1, row_to * B : (row_to + 1) * B, :] = got[c].astype(BF16)

    def corners(a_ref, cols, rows):
        for col, inner in ((0, 1), (cols + 1, cols)):
            north = a_ref[inner, 0:B, :].astype(F32)
            south = a_ref[inner, (rows + 1) * B : (rows + 2) * B, :].astype(F32)
            last = a_ref[col, rows * B : (rows + 1) * B, :].astype(F32)
            first = a_ref[col, B : 2 * B, :].astype(F32)
            a_ref[col, 0:B, :] = jnp.concatenate([north[:8], last[:8]], axis=0).astype(BF16)
            a_ref[col, (rows + 1) * B : (rows + 2) * B, :] = jnp.concatenate(
                [first[8:], south[8:]], axis=0
            ).astype(BF16)

    north_south(a10, N, H)
    load_fine.wait()
    conv_weights(fine_w, wf_ref)
    lift(1)
    north_south(a11, N, H)

    load_coarse.wait()
    conv_weights(coarse_w, wc_ref)
    for q in range(8):
        for j in range(2):
            place = onehot(iota((8, 128), 1) == iota((8, 128), 0) + (16 * q + 8 * j))
            out_w[(2 * q + j) * 128 : (2 * q + j + 1) * 128, :] = lax.dot_general(
                wo_ref[...], place, (((0,), (0,)), ((), ())), preferred_element_type=F32
            ).astype(BF16)
    frac_p, frac_q = [
        jnp.broadcast_to(column(frac_ref[k : k + 1, :]), (B, 256)) for k in range(2)
    ]

    route = jnp.broadcast_to(route_ref[...], (8, 128))
    rank = jnp.zeros((8, 128), jnp.int32)
    for s in range(1, 8):
        again = (pltpu.roll(route, s, 1) == route) & ((lane & 7) >= s)
        rank = rank + jnp.where(again, 1, 0)
    key = ((route - pos) & (NT - 1)) * 2 + rank
    pick = onehot(iota((128, 128), 0) == pos * 8 + (iota((128, 128), 1) & 7))
    key = dot(key.astype(F32).astype(BF16), pick)[0:1, :]
    i, j = iota((512, 128), 0), iota((512, 128), 1)
    slot_ref[...] = onehot(
        ((i >> 4).astype(F32) == key) & (((i >> 3) & 1) == ((j >> 3) & 1)) & ((i & 7) == (j >> 4))
    )
    slot = jnp.where(route == pos, ((pos - (lane >> 3)) & (NT - 1)) * 2 + rank, -1).astype(F32)
    diagonal = iota((128, 128), 0) == iota((128, 128), 1)
    slot = jnp.sum(jnp.where(diagonal, slot[0:1, :], 0.0), axis=1, keepdims=True)
    pick = onehot(slot == (iota((128, 512), 1) >> 4).astype(F32))
    block = jnp.broadcast_to(block_ref[...], (8, 128)).astype(F32) + 1.0
    block = dot(block.astype(BF16), pick)[0:1, :]
    i, j = iota((64, 512), 0), iota((64, 512), 1)
    sum_ref[...] = onehot(
        (((i >> 4) + 1).astype(F32) == block)
        & (((i >> 3) & 1) == ((j >> 3) & 1))
        & ((i & 7) == (j & 7))
    )

    def fine_post(m, pair, buf):
        base = jnp.concatenate([started[m][2 * pair], started[m][2 * pair + 1]], axis=1)
        out = (base.astype(F32) + buf[...]).astype(BF16)
        fine[m][2 * pair] = out[:, :128]
        fine[m][2 * pair + 1] = out[:, 128:]
        wide = out.astype(F32).reshape(H // 2, 2, B, 256)
        tall = wide[:, 0] + wide[:, 1]
        mean = ((tall[:, :, :128] + tall[:, :, 128:]) * 0.25).reshape(128, 128).astype(BF16)
        pooled[m][pair] = mean
        a2[m][pair + 1, B : B + 128, :] = act(mean, ones_ref[0:128, 0:128], gain_coarse)

    bufs = (g0, g1)
    waiting = []

    def finish():
        if waiting:
            m, pair, slot = waiting.pop()
            fine_post(m, pair, bufs[slot])

    def fine_next(m, pair):
        slot = 1 - waiting[0][2] if waiting else 0
        bufs[slot][...] = conv_pair(a1[m], fine_w, pair, 256)
        finish()
        waiting.append((m, pair, slot))

    def fine_run(count):
        m, first, slot = waiting.pop()

        def body(q, _):
            for u in range(4):
                here, there = (slot + u) % 2, (slot + u + 1) % 2
                pair = first + 4 * q + u
                bufs[there][...] = conv_pair(a1[m], fine_w, pair + 1, 256)
                fine_post(m, pair, bufs[here])
            return 0

        lax.fori_loop(0, count // 4, body, 0)
        waiting.append((m, first + count, slot))

    def send_edges(m):
        edges[m, 0] = a2[m][1, B : B + 128, :]
        edges[m, 1] = a2[m][H, B : B + 128, :]
        for side in range(2):
            c_copy(m, side).start()

    fine_next(0, 1)
    fine_run(4)
    finish()

    for side in range(2):
        h_copy(side).wait()
    sides = []
    for side, got, w in ((3, 1, lift_w[7, :, 128:256]), (1, 0, lift_w[0, :, 0:128])):
        both = jnp.concatenate([halo[got, 0:256, :], halo[got, 256:512, :]], axis=1)
        moved = jnp.concatenate(from_side(seam_w.at[side], both, H, flipped[side]), axis=0)
        sides.append(
            [
                dot((moved[:, m * 128 : (m + 1) * 128] * c_in[m][:, :128]).astype(BF16), w)
                for m in range(2)
            ]
        )
    for m in range(2):
        first = (jnp.concatenate([sides[0][m], sides[1][m]], axis=1) + temb[m]).astype(BF16)
        normed = act(first, ones_ref[...], gain_fine)
        a1[m][0, B : B + 256, :] = normed[:, :128]
        a1[m][N + 1, B : B + 256, :] = normed[:, 128:]
        corners(a1[m], N, H)

    def a_copy(k, d):
        return pltpu.make_async_remote_copy(
            src_ref=send.at[k, d],
            dst_ref=recv.at[k, d],
            send_sem=a_send.at[k, d],
            recv_sem=a_recv.at[k, d],
            device_id=along_tile(d),
            device_id_type=MESH,
        )

    def y_copy(m, k, d):
        return pltpu.make_async_remote_copy(
            src_ref=target.at[m, k, 0],
            dst_ref=target.at[m, k, d],
            send_sem=m_send.at[2 * m + k, d],
            recv_sem=m_recv.at[2 * m + k, d],
            device_id=along_y(d),
            device_id_type=MESH,
        )

    def x_copy(m, k):
        return pltpu.make_async_remote_copy(
            src_ref=target.at[m, k],
            dst_ref=other.at[m, k],
            send_sem=x_send.at[2 * m + k],
            recv_sem=x_recv.at[2 * m + k],
            device_id=other_core,
            device_id_type=MESH,
        )

    def coarse_level(m):
        north_south(a2[m], H, H // 2)
        for side in range(2):
            c_copy(m, side).wait()
        for side, got, col in ((1, 0, H + 1), (3, 1, 0)):
            moved = from_side(seam_w.at[side], halo2[m, got], H // 2, flipped[side])
            for r in range(H // 2):
                a2[m][col, (r + 1) * B : (r + 2) * B, :] = moved[r].astype(BF16)
        corners(a2[m], H, H // 2)

        def body(q, _):
            for pair in (4 * q, 4 * q + 1, 4 * q + 2, 4 * q + 3):
                got = conv_pair(a2[m], coarse_w, pair, 128)
                base = jnp.concatenate([pooled[m][2 * pair], pooled[m][2 * pair + 1]], axis=1)
                out = (base.astype(F32) + got).astype(BF16)
                coarse[m][2 * pair] = out[:, :128]
                coarse[m][2 * pair + 1] = out[:, 128:]
            return 0

        lax.fori_loop(0, 2, body, 0)

    def state(m, row, count):
        start, rows = row * B, count * B
        for pair in range(H):
            f = jnp.concatenate(
                [
                    fine[m][2 * pair, start : start + rows, :],
                    fine[m][2 * pair + 1, start : start + rows, :],
                ],
                axis=1,
            ).astype(F32)
            c = coarse[m][pair, start // 2 : (start + rows) // 2, :].astype(F32)
            c = c.reshape(count // 2, 1, B, 128)
            c = jnp.concatenate([c, c], axis=1).reshape(rows, 128)
            act_s[:rows, pair * 256 : (pair + 1) * 256] = act(f + twice(c), ones_ref[...], gain_out)
        left = dot(act_s[:rows, :2048], out_w[...])
        right = dot(act_s[:rows, 2048:], out_w[...])
        proj = jnp.concatenate([left, right], axis=1)
        cells = slice(m * 256 + start, m * 256 + start + rows)
        den = c_skip[m] * nx[cells, :].astype(F32) + c_out[m] * proj
        d_ref[m][start : start + rows, :] = den
        by_row[2 * m, start : start + rows, :] = den[:, :128]
        by_row[2 * m + 1, start : start + rows, :] = den[:, 128:]

    def route_rows(m, k):
        start = k * CHUNK
        den = d_ref[m][start : start + CHUNK, :].reshape(8, B, 256)
        below = d_ref[m][start + B : start + B + CHUNK, :].reshape(8, B, 256)
        mixed = ((1.0 - frac_p) * den + frac_p * below).reshape(CHUNK, 256)
        shifted = pltpu.roll(mixed, 248, 1)
        shifted = jnp.where(iota((CHUNK, 256), 1) >= 248, mixed, shifted)
        out = (1.0 - frac_q) * mixed.reshape(8, B, 256) + frac_q * shifted.reshape(8, B, 256)
        blocks = dot(slot_ref[...], out.reshape(CHUNK, 256).astype(BF16)).astype(BF16)
        blocks = blocks.reshape(NT, 32, 256)
        recv[2 * m + k, 0] = blocks[0]
        send[2 * m + k] = blocks
        each(NT, lambda d: a_copy(2 * m + k, d).start())

    def last_stage(m):
        state(m, 0, FIRST)
        route_rows(m, 0)
        state(m, FIRST, H - FIRST)
        d_ref[m][H * B :, :] = jnp.concatenate(
            [d_ref[m][8:16, :], d_ref[m][H * B - 8 : H * B, :]], axis=0
        )
        route_rows(m, 1)

    def sum_stage(m, k):
        each(NT, lambda d: a_copy(2 * m + k, d).wait_recv())
        total = dot(sum_ref[...], recv[2 * m + k].reshape(512, 256))
        target[m, k, 0] = total.astype(BF16)
        each(NY, lambda d: y_copy(m, k, d).start())

    def pass_stage(m, k):
        each(NY, lambda d: y_copy(m, k, d).wait_recv())
        x_copy(m, k).start()

    def stat_stage(k):
        for m in range(2):
            x_copy(m, k).wait_recv()
        for q in range(4):
            rows = slice(q * B, (q + 1) * B)
            values = [
                held[m, k, d, rows, :].astype(F32)
                for held in (target, other)
                for m in range(2)
                for d in range(NY)
            ]
            mean = functools.reduce(lambda a, b: a + b, values) * (1.0 / 16)
            squares = functools.reduce(lambda a, b: a + b, [(v - mean) * (v - mean) for v in values])
            spread = jnp.sqrt(squares / 15.0 + 1e-06)
            for half in range(2):
                row = half * H + k * 8
                stat_ref[0, q, row : row + 8, :] = mean[half * 8 : half * 8 + 8]
                stat_ref[1, q, row : row + 8, :] = spread[half * 8 : half * 8 + 8]

    fine_next(0, 0)
    fine_next(0, H - 1)
    fine_next(0, 6)
    send_edges(0)
    fine_run(8)
    fine_next(1, 0)
    fine_next(1, H - 1)
    fine_next(1, 1)
    send_edges(1)
    fine_run(8)
    finish()
    coarse_level(0)
    last_stage(0)
    fine_next(1, 10)
    fine_run(4)
    finish()
    coarse_level(1)
    last_stage(1)

    for m in range(2):
        for b in range(B):
            start = m * 256 + (b % 8) * N + (b // 8) * H
            for side in range(2):
                den_ref[start : start + H, side * 128 : (side + 1) * 128] = by_row[
                    2 * m + side, pl.ds(b, H, stride=B), :
                ]
    store_den = pltpu.make_async_copy(den_ref, den_hbm, o_sem.at[0])
    store_den.start()

    for m in range(2):
        for k in range(2):
            sum_stage(m, k)
    for m in range(2):
        for k in range(2):
            pass_stage(m, k)
    for k in range(2):
        stat_stage(k)
    store_stat = pltpu.make_async_copy(stat_ref, stat_hbm, o_sem.at[1])
    store_stat.start()
    for k in range(4):
        each(NT, lambda d: a_copy(k, d).wait_send())
    for m in range(2):
        for k in range(2):
            each(NY, lambda d: y_copy(m, k, d).wait_send())
            x_copy(m, k).wait_send()
    store_den.wait()
    store_stat.wait()


def on_device(
    noisy,
    timestep,
    seams,
    corner_list,
    route,
    target_block,
    frac,
    w_time,
    w_lift,
    w_fine,
    w_coarse,
    gain_fine,
    gain_coarse,
    gain_out,
    w_out,
):
    vmem = pl.BlockSpec(memory_space=pltpu.VMEM)
    smem = pl.BlockSpec(memory_space=pltpu.SMEM)
    hbm = pl.BlockSpec(memory_space=pltpu.HBM)
    dma = pltpu.SemaphoreType.DMA
    den, stat = pl.pallas_call(
        kernel,
        out_shape=(
            jax.ShapeDtypeStruct((512, 256), F32),
            jax.ShapeDtypeStruct((2, 4, N, 256), F32),
        ),
        in_specs=[vmem, smem] + [vmem] * 6 + [hbm] * 2 + [vmem] * 4,
        out_specs=(hbm, hbm),
        scratch_shapes=[
            pltpu.VMEM((9, 128, 128), BF16),
            pltpu.VMEM((9, 128, 128), BF16),
            pltpu.VMEM((512, 256), BF16),
            pltpu.VMEM((512, 256), BF16),
            pltpu.VMEM((8, 128, 256), BF16),
            pltpu.VMEM((2048, 128), BF16),
            pltpu.VMEM((1536, 256), BF16),
            pltpu.VMEM((1536, 256), BF16),
            pltpu.VMEM((256, 256), BF16),
            pltpu.VMEM((4, 256, 256), BF16),
            pltpu.VMEM((512, 128), BF16),
            pltpu.VMEM((64, 512), BF16),
            pltpu.VMEM((2, 512, 128), BF16),
        ]
        + [pltpu.VMEM((N, 256, 128), BF16)] * 2
        + [pltpu.VMEM((N + 2, 288, 128), BF16)] * 2
        + [pltpu.VMEM((N, 256, 128), BF16)] * 2
        + [pltpu.VMEM((H, 128, 128), BF16)] * 2
        + [pltpu.VMEM((H + 2, 160, 128), BF16)] * 2
        + [pltpu.VMEM((H, 128, 128), BF16)] * 2
        + [
            pltpu.VMEM((2, 2, 128, 128), BF16),
            pltpu.VMEM((2, 2, 128, 128), BF16),
            pltpu.VMEM((256, 256), F32),
            pltpu.VMEM((256, 256), F32),
            pltpu.VMEM((FIRST * B, 4096), BF16),
            pltpu.VMEM(((H + 1) * B, 256), F32),
            pltpu.VMEM(((H + 1) * B, 256), F32),
            pltpu.VMEM((4, 256, 128), F32),
            pltpu.VMEM((512, 256), F32),
            pltpu.VMEM((2, 4, N, 256), F32),
            pltpu.VMEM((4, NT, 32, 256), BF16),
            pltpu.VMEM((4, NT, 32, 256), BF16),
            pltpu.VMEM((2, 2, NY, 64, 256), BF16),
            pltpu.VMEM((2, 2, NY, 64, 256), BF16),
            dma((2,)),
            dma((2,)),
            dma((2,)),
            dma((2,)),
            dma((2, 2)),
            dma((2, 2)),
            dma((4, NT)),
            dma((4, NT)),
            dma((4, NY)),
            dma((4, NY)),
            dma((4,)),
            dma((4,)),
        ],
        compiler_params=pltpu.CompilerParams(
            collective_id=0, has_side_effects=True, vmem_limit_bytes=56 * 1024 * 1024
        ),
    )(
        noisy.reshape(512, 256),
        timestep,
        seams.transpose(2, 1, 0),
        route.reshape(1, 128),
        target_block.reshape(1, 128),
        frac.T,
        w_time,
        w_lift,
        w_fine,
        w_coarse,
        gain_fine.reshape(1, 128),
        gain_coarse.reshape(1, 128),
        gain_out.reshape(1, 128),
        w_out.T,
    )
    return (den.reshape(noisy.shape), stat[0], stat[1])


def solution(mesh):
    placed = (
        P("mem", "tile", None, None),
        P("mem"),
        P("tile", None, None),
        P("tile", None, None),
        P(),
        P(),
        P("tile", None),
        P(),
        P(),
        P(),
        P(),
        P(),
        P(),
        P(),
        P(),
    )
    return jax.shard_map(
        on_device,
        mesh=mesh,
        in_specs=placed,
        out_specs=(P("mem", "tile", None, None), P("tile", None, None), P("tile", None, None)),
        check_vma=False,
    )
```

```python
import functools
import math

import jax
import jax.numpy as jnp
from jax import lax
from jax.experimental import pallas as pl
from jax.experimental.pallas import tpu as pltpu
from jax.sharding import PartitionSpec as P

STEPS = 1000
MESH = pl.DeviceIdType.MESH
F32 = jnp.float32
BF16 = jnp.bfloat16

B = 16
N = 32
H = N // 2
NT = 16
NM = 8
NY = NM // 2
FAR = sorted(range(1, NT), key=lambda e: -min(e // 4, 4 - e // 4) - min(e % 4, 4 - e % 4))
FIRST = 10
EARLY = 5
CHUNK = 128


def dot(a, b):
    return jnp.dot(a, b, preferred_element_type=F32)


def twice(x):
    return jnp.concatenate([x, x], axis=-1)


def iota(shape, dim):
    return lax.broadcasted_iota(jnp.int32, shape, dim)


def onehot(where):
    return jnp.where(where, 1.0, 0.0).astype(BF16)


def act(x, ones, half_gain):
    short = x.astype(BF16)
    mean = dot(short * short, ones)
    h = x.astype(F32) * lax.rsqrt(mean + 1e-06) * half_gain
    return (h + h * jnp.tanh(h)).astype(BF16)


def column(row):
    spread = jnp.broadcast_to(row.astype(F32), (B, 8))
    own = iota((B, 8), 1) == (iota((B, 8), 0) & 7)
    return jnp.sum(jnp.where(own, spread, 0.0), axis=1, keepdims=True)


def from_side(perm, edge, n, flipped):
    rows = edge.shape[0]
    if rows > 256:
        edge = jnp.concatenate([edge[:256], edge[256:]], axis=1)
        got = dot(perm[...], edge)
        pieces = [
            got[c % H * B : (c % H + 1) * B, c // H * 128 : (c // H + 1) * 128] for c in range(n)
        ]
    else:
        got = dot(perm[:rows, :rows], edge)
        pieces = [got[c * B : (c + 1) * B] for c in range(n)]
    if edge.shape[1] > 128 and rows <= 256:
        flipped = twice(flipped)
    return [
        jnp.where(flipped > 0.5, pieces[n - 1 - c], pieces[c]) for c in range(n)
    ]


def conv_weights(out_ref, w_ref):
    zero = jnp.zeros((128, 128), BF16)
    for i in range(3):
        for j in range(4):
            left = w_ref[3 * i + j] if j < 3 else zero
            right = w_ref[3 * i + j - 1] if j > 0 else zero
            start = (4 * i + j) * 128
            out_ref[start : start + 128, :] = jnp.concatenate([left, right], axis=1)


def conv_pair(a_ref, w_ref, pair, rows):
    parts = []
    for i in range(3):
        for j in range(4):
            parts.append(a_ref[2 * pair + j, i * B : i * B + rows, :])
    return dot(jnp.concatenate(parts, axis=1), w_ref[...])


def each(count, what):
    def body(d, _):
        what(d)
        return 0

    lax.fori_loop(1, count, body, 0)


def kernel(
    noisy_hbm,
    step_hbm,
    seam_hbm,
    route_hbm,
    block_hbm,
    frac_hbm,
    wt_hbm,
    wl_hbm,
    wf_hbm,
    wc_hbm,
    gf_hbm,
    gc_hbm,
    go_hbm,
    wo_hbm,
    den_hbm,
    mean_hbm,
    spread_hbm,
    noisy_ref,
    step_ref,
    seam_ref,
    route_ref,
    block_ref,
    frac_ref,
    wt_ref,
    wl_ref,
    wf_ref,
    wc_ref,
    gf_ref,
    gc_ref,
    go_ref,
    wo_ref,
    nx,
    sx,
    lift_w,
    out_w,
    fine_w,
    coarse_w,
    ones_ref,
    seam_w,
    slot_ref,
    sum_ref,
    halo,
    started0,
    started1,
    a10,
    a11,
    fine0,
    fine1,
    pooled0,
    pooled1,
    a20,
    a21,
    coarse0,
    coarse1,
    halo2,
    edges,
    g0,
    g1,
    act_s,
    d_ref0,
    d_ref1,
    by_row,
    den_ref,
    mean_ref,
    spread_ref,
    send,
    recv,
    target,
    other,
    w_sem,
    o_sem,
    h_send,
    h_recv,
    c_send,
    c_recv,
    a_send,
    a_recv,
    m_send,
    m_recv,
    x_send,
    x_recv,
):
    pos = lax.axis_index("tile")
    mem = lax.axis_index("mem")
    started, a1, fine = (started0, started1), (a10, a11), (fine0, fine1)
    pooled, a2, coarse = (pooled0, pooled1), (a20, a21), (coarse0, coarse1)
    d_ref = (d_ref0, d_ref1)

    def along_tile(d):
        return {"tile": lax.rem(pos + d, NT)}

    def torus(e):
        return {"tile": lax.rem(pos // 4 + e // 4, 4) * 4 + lax.rem(lax.rem(pos, 4) + e % 4, 4)}

    def along_y(d):
        return {"mem": lax.rem(mem + 2 * d, NM)}

    other_core = {"mem": mem + 1 - 2 * lax.rem(mem, 2)}

    barrier = pltpu.get_barrier_semaphore()

    def greet(where):
        pl.semaphore_signal(barrier, inc=1, device_id=where, device_id_type=MESH)

    each(NT, lambda d: greet(along_tile(d)))
    each(NY, lambda d: greet(along_y(d)))
    greet(other_core)

    inputs = (
        (noisy_hbm, noisy_ref),
        (step_hbm, step_ref),
        (wt_hbm, wt_ref),
        (wl_hbm, wl_ref),
        (gf_hbm, gf_ref),
        (seam_hbm, seam_ref),
        (wf_hbm, wf_ref),
        (gc_hbm, gc_ref),
        (go_hbm, go_ref),
        (route_hbm, route_ref),
        (block_hbm, block_ref),
        (frac_hbm, frac_ref),
        (wo_hbm, wo_ref),
        (wc_hbm, wc_ref),
    )
    loads = [pltpu.make_async_copy(a, b, w_sem.at[i]) for i, (a, b) in enumerate(inputs)]
    for load in loads:
        load.start()

    ones_ref[...] = jnp.where(
        iota((256, 256), 0) // 128 == iota((256, 256), 1) // 128, 1.0 / 128, 0.0
    ).astype(BF16)
    for load in loads[:6]:
        load.wait()
    wl = wl_ref[...].astype(F32)
    wl_zero = jnp.zeros_like(wl)
    wl_pair = jnp.concatenate(
        [
            jnp.concatenate([wl, wl_zero], axis=1),
            jnp.concatenate([wl_zero, wl], axis=1),
        ],
        axis=0,
    ).astype(BF16)
    for q in range(8):
        lift_w[q] = jnp.zeros((128, 256), BF16)
        lift_w[q, q * B : (q + 1) * B, :] = wl_pair

    level = jnp.where(iota((8, 128), 0) < 4, step_ref[0:1, 0:1], step_ref[0:1, 1:2]).astype(F32)
    fraction = level / (STEPS - 1)
    high_root = 80.0 ** (1.0 / 7.0)
    low_root = 0.002 ** (1.0 / 7.0)
    root = high_root + fraction * (low_root - high_root)
    square = root * root
    sigma = square * square * square * root
    denominator = sigma * sigma + 1.0
    scales = (lax.rsqrt(denominator), 1.0 / denominator, sigma * lax.rsqrt(denominator))
    c_in, c_skip, c_out = [[twice(x[0:1]), twice(x[4:5])] for x in scales]
    lane = iota((8, 128), 1)
    frequency = jnp.exp((lane & 63).astype(F32) * (-math.log(10000.0) / 64))
    angles = level * frequency
    features = jnp.where(lane < 64, jnp.sin(angles), jnp.cos(angles))
    embedded = jnp.dot(
        features, wt_ref[...], preferred_element_type=F32, precision=lax.Precision.HIGHEST
    )
    embedded = embedded / (1.0 + jnp.exp(-embedded))
    temb = [twice(embedded[0:1]), twice(embedded[4:5])]
    gain_fine = twice(gf_ref[...]) * 0.5

    i = iota((256, 256), 0)
    to_rows = onehot(((i & 7) * N + ((i >> 3) & 1) * H + (i >> 4)) == iota((256, 256), 1))
    for m in range(2):
        moved = dot(to_rows, noisy_ref[m * 256 : (m + 1) * 256, :])
        nx[m * 256 : (m + 1) * 256, :] = moved.astype(BF16)
        sx[m * 256 : (m + 1) * 256, :] = (moved * c_in[m]).astype(BF16)

    def lift(m):
        for q in range(8):
            for half in range(2):
                pair = half * 8 + q
                cells = sx[m * 256 : (m + 1) * 256, half * 128 : (half + 1) * 128]
                first = (dot(cells, lift_w[q]) + temb[m]).astype(BF16)
                started[m][2 * pair] = first[:, :128]
                started[m][2 * pair + 1] = first[:, 128:]
                normed = act(first, ones_ref[...], gain_fine)
                a1[m][2 * pair + 1, B : B + 256, :] = normed[:, :128]
                a1[m][2 * pair + 2, B : B + 256, :] = normed[:, 128:]

    lift(0)

    pl.semaphore_wait(barrier, NT - 1 + NY)

    def h_copy(side):
        return pltpu.make_async_remote_copy(
            src_ref=nx.at[:, pl.ds(side * 128, 128)],
            dst_ref=halo.at[side],
            send_sem=h_send.at[side],
            recv_sem=h_recv.at[side],
            device_id=along_tile(1 if side else NT - 1),
            device_id_type=MESH,
        )

    def c_copy(m, side):
        return pltpu.make_async_remote_copy(
            src_ref=edges.at[m, side],
            dst_ref=halo2.at[m, side],
            send_sem=c_send.at[m, side],
            recv_sem=c_recv.at[m, side],
            device_id=along_tile(1 if side else NT - 1),
            device_id_type=MESH,
        )

    for side in range(2):
        h_copy(side).start()

    half = iota((B, 1), 0) >> 3
    own = iota((B, 1), 0) & 7
    flipped = []
    for side in range(4):
        tile = column(seam_ref[0, side : side + 1, :] & 7).astype(jnp.int32)
        flag = column(seam_ref[2, side : side + 1, :]).astype(jnp.int32)
        if side == 0:
            source = jnp.where(half == 0, 8 + tile, own)
            flag = jnp.where(half == 0, flag, 0)
        elif side == 2:
            source = jnp.where(half == 0, 8 + own, tile)
            flag = jnp.where(half == 0, 0, flag)
        else:
            source = ((half + flag) & 1) * 8 + tile
        flipped.append(jnp.broadcast_to(flag.astype(F32), (B, 128)))
        apart = iota((B, 256), 1) - source
        for c in range(256 // B):
            seam_w[side, c * B : (c + 1) * B, :] = onehot(apart == c * B)

    def north_south(a_ref, cols, rows):
        for side, row_from, row_to in ((0, rows, 0), (2, 1, rows + 1)):
            edge = a_ref[1 : cols + 1, row_from * B : (row_from + 1) * B, :]
            got = from_side(seam_w.at[side], edge.reshape(cols * B, 128), cols, flipped[side])
            for c in range(cols):
                a_ref[c + 1, row_to * B : (row_to + 1) * B, :] = got[c].astype(BF16)

    def corners(a_ref, cols, rows):
        for col, inner in ((0, 1), (cols + 1, cols)):
            north = a_ref[inner, 0:B, :].astype(F32)
            south = a_ref[inner, (rows + 1) * B : (rows + 2) * B, :].astype(F32)
            last = a_ref[col, rows * B : (rows + 1) * B, :].astype(F32)
            first = a_ref[col, B : 2 * B, :].astype(F32)
            a_ref[col, 0:B, :] = jnp.concatenate([north[:8], last[:8]], axis=0).astype(BF16)
            a_ref[col, (rows + 1) * B : (rows + 2) * B, :] = jnp.concatenate(
                [first[8:], south[8:]], axis=0
            ).astype(BF16)

    north_south(a10, N, H)
    loads[6].wait()
    conv_weights(fine_w, wf_ref)

    for load in loads[7:]:
        load.wait()
    gain_coarse = gc_ref[...] * 0.5
    gain_out = twice(go_ref[...]) * 0.5
    conv_weights(coarse_w, wc_ref)
    for q in range(8):
        for j in range(2):
            place = onehot(iota((8, 128), 1) == iota((8, 128), 0) + (16 * q + 8 * j))
            out_w[(2 * q + j) * 128 : (2 * q + j + 1) * 128, :] = lax.dot_general(
                wo_ref[...], place, (((0,), (0,)), ((), ())), preferred_element_type=F32
            ).astype(BF16)
    frac_p, frac_q = [
        jnp.broadcast_to(column(frac_ref[k : k + 1, :]), (B, 256)) for k in range(2)
    ]

    route = jnp.broadcast_to(route_ref[...], (8, 128))
    rank = jnp.zeros((8, 128), jnp.int32)
    for s in range(1, 8):
        again = (pltpu.roll(route, s, 1) == route) & ((lane & 7) >= s)
        rank = rank + jnp.where(again, 1, 0)
    def offset(to, start):
        return (((to >> 2) - (start >> 2)) & 3) * 4 + ((to - start) & 3)

    key = offset(route, pos) * 2 + rank
    pick = onehot(iota((128, 128), 0) == pos * 8 + (iota((128, 128), 1) & 7))
    key = dot(key.astype(F32).astype(BF16), pick)[0:1, :]
    i, j = iota((512, 128), 0), iota((512, 128), 1)
    slot_ref[...] = onehot(
        ((i >> 4).astype(F32) == key) & (((i >> 3) & 1) == ((j >> 3) & 1)) & ((i & 7) == (j >> 4))
    )
    slot = jnp.where(route == pos, offset(pos, lane >> 3) * 2 + rank, -1).astype(F32)
    diagonal = iota((128, 128), 0) == iota((128, 128), 1)
    slot = jnp.sum(jnp.where(diagonal, slot[0:1, :], 0.0), axis=1, keepdims=True)
    pick = onehot(slot == (iota((128, 512), 1) >> 4).astype(F32))
    block = jnp.broadcast_to(block_ref[...], (8, 128)).astype(F32) + 1.0
    block = dot(block.astype(BF16), pick)[0:1, :]
    i, j = iota((64, 512), 0), iota((64, 512), 1)
    sum_ref[...] = onehot(
        (((i >> 4) + 1).astype(F32) == block)
        & (((i >> 3) & 1) == ((j >> 3) & 1))
        & ((i & 7) == (j & 7))
    )

    def fine_post(m, pair, buf):
        base = jnp.concatenate([started[m][2 * pair], started[m][2 * pair + 1]], axis=1)
        out = (base.astype(F32) + buf[...]).astype(BF16)
        fine[m][2 * pair] = out[:, :128]
        fine[m][2 * pair + 1] = out[:, 128:]
        wide = out.astype(F32).reshape(H // 2, 2, B, 256)
        tall = wide[:, 0] + wide[:, 1]
        mean = ((tall[:, :, :128] + tall[:, :, 128:]) * 0.25).reshape(128, 128).astype(BF16)
        pooled[m][pair] = mean
        a2[m][pair + 1, B : B + 128, :] = act(mean, ones_ref[0:128, 0:128], gain_coarse)

    bufs = (g0, g1)
    waiting = []

    def finish():
        if waiting:
            m, pair, slot = waiting.pop()
            fine_post(m, pair, bufs[slot])

    def fine_next(m, pair):
        slot = 1 - waiting[0][2] if waiting else 0
        bufs[slot][...] = conv_pair(a1[m], fine_w, pair, 256)
        finish()
        waiting.append((m, pair, slot))

    def fine_run(count):
        for _ in range(count):
            m, pair, _ = waiting[0]
            fine_next(m, pair + 1)

    def send_edges(m):
        edges[m, 0] = a2[m][1, B : B + 128, :]
        edges[m, 1] = a2[m][H, B : B + 128, :]
        for side in range(2):
            c_copy(m, side).start()

    fine_next(0, 1)
    fine_run(H - 3)
    finish()

    for side in range(2):
        h_copy(side).wait()
    sides = []
    for side, got, w in ((3, 1, lift_w[7, :, 128:256]), (1, 0, lift_w[0, :, 0:128])):
        both = jnp.concatenate([halo[got, 0:256, :], halo[got, 256:512, :]], axis=1)
        moved = jnp.concatenate(from_side(seam_w.at[side], both, H, flipped[side]), axis=0)
        sides.append(
            [
                dot((moved[:, m * 128 : (m + 1) * 128] * c_in[m][:, :128]).astype(BF16), w)
                for m in range(2)
            ]
        )
    def east_west(m):
        first = (jnp.concatenate([sides[0][m], sides[1][m]], axis=1) + temb[m]).astype(BF16)
        normed = act(first, ones_ref[...], gain_fine)
        a1[m][0, B : B + 256, :] = normed[:, :128]
        a1[m][N + 1, B : B + 256, :] = normed[:, 128:]
        corners(a1[m], N, H)

    def a_copy(k, d):
        return pltpu.make_async_remote_copy(
            src_ref=send.at[k, d],
            dst_ref=recv.at[k, d],
            send_sem=a_send.at[k, d],
            recv_sem=a_recv.at[k, d],
            device_id=torus(d),
            device_id_type=MESH,
        )

    def y_copy(m, k, d):
        return pltpu.make_async_remote_copy(
            src_ref=target.at[m, k, 0],
            dst_ref=target.at[m, k, d],
            send_sem=m_send.at[2 * m + k, d],
            recv_sem=m_recv.at[2 * m + k, d],
            device_id=along_y(d),
            device_id_type=MESH,
        )

    def x_copy(m, k):
        return pltpu.make_async_remote_copy(
            src_ref=target.at[m, k],
            dst_ref=other.at[m, k],
            send_sem=x_send.at[2 * m + k],
            recv_sem=x_recv.at[2 * m + k],
            device_id=other_core,
            device_id_type=MESH,
        )

    def coarse_level(m):
        north_south(a2[m], H, H // 2)
        for side in range(2):
            c_copy(m, side).wait()
        for side, got, col in ((1, 0, H + 1), (3, 1, 0)):
            moved = from_side(seam_w.at[side], halo2[m, got], H // 2, flipped[side])
            for r in range(H // 2):
                a2[m][col, (r + 1) * B : (r + 2) * B, :] = moved[r].astype(BF16)
        corners(a2[m], H, H // 2)

        def body(q, _):
            for pair in (4 * q, 4 * q + 1, 4 * q + 2, 4 * q + 3):
                got = conv_pair(a2[m], coarse_w, pair, 128)
                base = jnp.concatenate([pooled[m][2 * pair], pooled[m][2 * pair + 1]], axis=1)
                out = (base.astype(F32) + got).astype(BF16)
                coarse[m][2 * pair] = out[:, :128]
                coarse[m][2 * pair + 1] = out[:, 128:]
            return 0

        lax.fori_loop(0, 2, body, 0)

    def state(m, row, count):
        start, rows = row * B, count * B
        for pair in range(H):
            f = jnp.concatenate(
                [
                    fine[m][2 * pair, start : start + rows, :],
                    fine[m][2 * pair + 1, start : start + rows, :],
                ],
                axis=1,
            ).astype(F32)
            c = coarse[m][pair, start // 2 : (start + rows) // 2, :].astype(F32)
            c = c.reshape(count // 2, 1, B, 128)
            c = jnp.concatenate([c, c], axis=1).reshape(rows, 128)
            act_s[:rows, pair * 256 : (pair + 1) * 256] = act(f + twice(c), ones_ref[...], gain_out)
        left = dot(act_s[:rows, :2048], out_w[...])
        right = dot(act_s[:rows, 2048:], out_w[...])
        proj = jnp.concatenate([left, right], axis=1)
        cells = slice(m * 256 + start, m * 256 + start + rows)
        den = c_skip[m] * nx[cells, :].astype(F32) + c_out[m] * proj
        d_ref[m][start : start + rows, :] = den
        by_row[2 * m, start : start + rows, :] = den[:, :128]
        by_row[2 * m + 1, start : start + rows, :] = den[:, 128:]

    def route_rows(m, k):
        start = k * CHUNK
        den = d_ref[m][start : start + CHUNK, :].reshape(8, B, 256)
        below = d_ref[m][start + B : start + B + CHUNK, :].reshape(8, B, 256)
        mixed = ((1.0 - frac_p) * den + frac_p * below).reshape(CHUNK, 256)
        shifted = pltpu.roll(mixed, 248, 1)
        shifted = jnp.where(iota((CHUNK, 256), 1) >= 248, mixed, shifted)
        out = (1.0 - frac_q) * mixed.reshape(8, B, 256) + frac_q * shifted.reshape(8, B, 256)
        blocks = dot(slot_ref[...], out.reshape(CHUNK, 256).astype(BF16)).astype(BF16)
        blocks = blocks.reshape(NT, 32, 256)
        recv[2 * m + k, 0] = blocks[0]
        send[2 * m + k] = blocks
        for d in FAR:
            a_copy(2 * m + k, d).start()

    def last_stage(m):
        state(m, 0, FIRST)
        route_rows(m, 0)
        state(m, FIRST, H - FIRST)
        d_ref[m][H * B :, :] = jnp.concatenate(
            [d_ref[m][8:16, :], d_ref[m][H * B - 8 : H * B, :]], axis=0
        )
        route_rows(m, 1)

    def sum_stage(m, k):
        each(NT, lambda d: a_copy(2 * m + k, d).wait_recv())
        total = dot(sum_ref[...], recv[2 * m + k].reshape(512, 256))
        target[m, k, 0] = total.astype(BF16)
        each(NY, lambda d: y_copy(m, k, d).start())

    def pass_stage(m, k):
        each(NY, lambda d: y_copy(m, k, d).wait_recv())
        x_copy(m, k).start()

    def stat_stage(k):
        for m in range(2):
            x_copy(m, k).wait_recv()
        for q in range(4):
            rows = slice(q * B, (q + 1) * B)
            values = [
                held[m, k, d, rows, :].astype(F32)
                for held in (target, other)
                for m in range(2)
                for d in range(NY)
            ]
            mean = functools.reduce(lambda a, b: a + b, values) * (1.0 / 16)
            squares = functools.reduce(lambda a, b: a + b, [(v - mean) * (v - mean) for v in values])
            spread = jnp.sqrt(squares / 15.0 + 1e-06)
            for half in range(2):
                row = half * H + k * 8
                mean_ref[q, row : row + 8, :] = mean[half * 8 : half * 8 + 8]
                spread_ref[q, row : row + 8, :] = spread[half * 8 : half * 8 + 8]

    east_west(0)
    fine_next(0, 0)
    fine_next(0, H - 1)
    finish()
    send_edges(0)
    lift(1)
    north_south(a11, N, H)
    east_west(1)
    fine_next(1, 0)
    fine_next(1, H - 1)
    fine_next(1, 1)
    send_edges(1)
    fine_run(EARLY - 1)
    finish()
    coarse_level(0)
    last_stage(0)
    fine_next(1, EARLY + 1)
    fine_run(H - 3 - EARLY)
    finish()
    coarse_level(1)
    last_stage(1)

    for m in range(2):
        for b in range(B):
            start = m * 256 + (b % 8) * N + (b // 8) * H
            for side in range(2):
                den_ref[start : start + H, side * 128 : (side + 1) * 128] = by_row[
                    2 * m + side, pl.ds(b, H, stride=B), :
                ]
    store_den = pltpu.make_async_copy(den_ref, den_hbm, o_sem.at[0])
    store_den.start()

    for m in range(2):
        for k in range(2):
            sum_stage(m, k)
    for m in range(2):
        for k in range(2):
            pass_stage(m, k)
    for k in range(2):
        stat_stage(k)
    store_mean = pltpu.make_async_copy(mean_ref, mean_hbm, o_sem.at[1])
    store_spread = pltpu.make_async_copy(spread_ref, spread_hbm, o_sem.at[2])
    store_mean.start()
    store_spread.start()
    for k in range(4):
        each(NT, lambda d: a_copy(k, d).wait_send())
    for m in range(2):
        for k in range(2):
            each(NY, lambda d: y_copy(m, k, d).wait_send())
            x_copy(m, k).wait_send()
    store_den.wait()
    store_mean.wait()
    store_spread.wait()


def on_device(
    noisy,
    timestep,
    seams,
    corner_list,
    route,
    target_block,
    frac,
    w_time,
    w_lift,
    w_fine,
    w_coarse,
    gain_fine,
    gain_coarse,
    gain_out,
    w_out,
):
    hbm = pl.BlockSpec(memory_space=pltpu.HBM)
    dma = pltpu.SemaphoreType.DMA
    den, mean, spread = pl.pallas_call(
        kernel,
        out_shape=(
            jax.ShapeDtypeStruct((512, 256), F32),
            jax.ShapeDtypeStruct((4, N, 256), F32),
            jax.ShapeDtypeStruct((4, N, 256), F32),
        ),
        in_specs=[hbm] * 14,
        out_specs=(hbm, hbm, hbm),
        scratch_shapes=[
            pltpu.VMEM((512, 256), BF16),
            pltpu.VMEM((1, 2), jnp.int32),
            pltpu.VMEM((3, 4, 8), jnp.int32),
            pltpu.VMEM((1, 128), jnp.int32),
            pltpu.VMEM((1, 128), jnp.int32),
            pltpu.VMEM((2, 8), F32),
            pltpu.VMEM((128, 128), F32),
            pltpu.VMEM((8, 128), BF16),
            pltpu.VMEM((9, 128, 128), BF16),
            pltpu.VMEM((9, 128, 128), BF16),
            pltpu.VMEM((1, 128), F32),
            pltpu.VMEM((1, 128), F32),
            pltpu.VMEM((1, 128), F32),
            pltpu.VMEM((8, 128), BF16),
            pltpu.VMEM((512, 256), BF16),
            pltpu.VMEM((512, 256), BF16),
            pltpu.VMEM((8, 128, 256), BF16),
            pltpu.VMEM((2048, 128), BF16),
            pltpu.VMEM((1536, 256), BF16),
            pltpu.VMEM((1536, 256), BF16),
            pltpu.VMEM((256, 256), BF16),
            pltpu.VMEM((4, 256, 256), BF16),
            pltpu.VMEM((512, 128), BF16),
            pltpu.VMEM((64, 512), BF16),
            pltpu.VMEM((2, 512, 128), BF16),
        ]
        + [pltpu.VMEM((N, 256, 128), BF16)] * 2
        + [pltpu.VMEM((N + 2, 288, 128), BF16)] * 2
        + [pltpu.VMEM((N, 256, 128), BF16)] * 2
        + [pltpu.VMEM((H, 128, 128), BF16)] * 2
        + [pltpu.VMEM((H + 2, 160, 128), BF16)] * 2
        + [pltpu.VMEM((H, 128, 128), BF16)] * 2
        + [
            pltpu.VMEM((2, 2, 128, 128), BF16),
            pltpu.VMEM((2, 2, 128, 128), BF16),
            pltpu.VMEM((256, 256), F32),
            pltpu.VMEM((256, 256), F32),
            pltpu.VMEM((FIRST * B, 4096), BF16),
            pltpu.VMEM(((H + 1) * B, 256), F32),
            pltpu.VMEM(((H + 1) * B, 256), F32),
            pltpu.VMEM((4, 256, 128), F32),
            pltpu.VMEM((512, 256), F32),
            pltpu.VMEM((4, N, 256), F32),
            pltpu.VMEM((4, N, 256), F32),
            pltpu.VMEM((4, NT, 32, 256), BF16),
            pltpu.VMEM((4, NT, 32, 256), BF16),
            pltpu.VMEM((2, 2, NY, 64, 256), BF16),
            pltpu.VMEM((2, 2, NY, 64, 256), BF16),
            dma((14,)),
            dma((3,)),
            dma((2,)),
            dma((2,)),
            dma((2, 2)),
            dma((2, 2)),
            dma((4, NT)),
            dma((4, NT)),
            dma((4, NY)),
            dma((4, NY)),
            dma((4,)),
            dma((4,)),
        ],
        compiler_params=pltpu.CompilerParams(
            collective_id=0, has_side_effects=True, vmem_limit_bytes=56 * 1024 * 1024
        ),
    )(
        noisy.reshape(512, 256),
        timestep.reshape(1, 2),
        seams.transpose(2, 1, 0),
        route.reshape(1, 128),
        target_block.reshape(1, 128),
        frac.T,
        w_time,
        w_lift,
        w_fine,
        w_coarse,
        gain_fine.reshape(1, 128),
        gain_coarse.reshape(1, 128),
        gain_out.reshape(1, 128),
        w_out.T,
    )
    return (den.reshape(noisy.shape), mean, spread)


def solution(mesh):
    placed = (
        P("mem", "tile", None, None),
        P("mem"),
        P("tile", None, None),
        P("tile", None, None),
        P(),
        P(),
        P("tile", None),
        P(),
        P(),
        P(),
        P(),
        P(),
        P(),
        P(),
        P(),
    )
    return jax.shard_map(
        on_device,
        mesh=mesh,
        in_specs=placed,
        out_specs=(P("mem", "tile", None, None), P("tile", None, None), P("tile", None, None)),
        check_vma=False,
    )
```

```python
import functools
import math

import jax
import jax.numpy as jnp
from jax import lax
from jax.experimental import pallas as pl
from jax.experimental.pallas import tpu as pltpu
from jax.sharding import PartitionSpec as P

STEPS = 1000
MESH = pl.DeviceIdType.MESH
F32 = jnp.float32
BF16 = jnp.bfloat16

B = 16
N = 32
H = N // 2
NT = 16
NM = 8
NY = NM // 2
FAR = sorted(range(1, NT), key=lambda e: -min(e // 4, 4 - e // 4) - min(e % 4, 4 - e % 4))
FIRST = 10
EARLY = 9
CHUNK = 128


def dot(a, b):
    return jnp.dot(a, b, preferred_element_type=F32)


def twice(x):
    return jnp.concatenate([x, x], axis=-1)


def iota(shape, dim):
    return lax.broadcasted_iota(jnp.int32, shape, dim)


def onehot(where):
    return jnp.where(where, 1.0, 0.0).astype(BF16)


def act(x, ones, half_gain):
    short = x.astype(BF16)
    mean = dot(short * short, ones)
    h = x.astype(F32) * lax.rsqrt(mean + 1e-06) * half_gain
    return (h + h * jnp.tanh(h)).astype(BF16)


def column(row):
    spread = jnp.broadcast_to(row.astype(F32), (B, 8))
    own = iota((B, 8), 1) == (iota((B, 8), 0) & 7)
    return jnp.sum(jnp.where(own, spread, 0.0), axis=1, keepdims=True)


def from_side(perm, edge, n, flipped):
    rows = edge.shape[0]
    if rows > 256:
        edge = jnp.concatenate([edge[:256], edge[256:]], axis=1)
        got = dot(perm[...], edge)
        pieces = [
            got[c % H * B : (c % H + 1) * B, c // H * 128 : (c // H + 1) * 128] for c in range(n)
        ]
    else:
        got = dot(perm[:rows, :rows], edge)
        pieces = [got[c * B : (c + 1) * B] for c in range(n)]
    if edge.shape[1] > 128 and rows <= 256:
        flipped = twice(flipped)
    return [
        jnp.where(flipped > 0.5, pieces[n - 1 - c], pieces[c]) for c in range(n)
    ]


def conv_weights(out_ref, w_ref):
    zero = jnp.zeros((128, 128), BF16)
    for i in range(3):
        for j in range(4):
            left = w_ref[3 * i + j] if j < 3 else zero
            right = w_ref[3 * i + j - 1] if j > 0 else zero
            start = (4 * i + j) * 128
            out_ref[start : start + 128, :] = jnp.concatenate([left, right], axis=1)


def conv_pair(a_ref, w_ref, pair, rows):
    parts = []
    for i in range(3):
        for j in range(4):
            parts.append(a_ref[2 * pair + j, i * B : i * B + rows, :])
    return dot(jnp.concatenate(parts, axis=1), w_ref[...])


def each(count, what):
    def body(d, _):
        what(d)
        return 0

    lax.fori_loop(1, count, body, 0)


def kernel(
    noisy_hbm,
    step_hbm,
    seam_hbm,
    route_hbm,
    block_hbm,
    frac_hbm,
    wt_hbm,
    wl_hbm,
    wf_hbm,
    wc_hbm,
    gf_hbm,
    gc_hbm,
    go_hbm,
    wo_hbm,
    den_hbm,
    stat_hbm,
    noisy_ref,
    step_ref,
    seam_ref,
    route_ref,
    block_ref,
    frac_ref,
    wt_ref,
    wl_ref,
    wf_ref,
    wc_ref,
    gf_ref,
    gc_ref,
    go_ref,
    wo_ref,
    nx,
    sx,
    lift_w,
    out_w,
    fine_w,
    coarse_w,
    ones_ref,
    seam_w,
    slot_ref,
    sum_ref,
    halo,
    started0,
    started1,
    a10,
    a11,
    fine0,
    fine1,
    pooled0,
    pooled1,
    a20,
    a21,
    coarse0,
    coarse1,
    halo2,
    edges,
    g0,
    g1,
    act_s,
    d_ref0,
    d_ref1,
    by_row,
    den_ref,
    mean_ref,
    spread_ref,
    send,
    recv,
    target,
    other,
    w_sem,
    o_sem,
    h_send,
    h_recv,
    c_send,
    c_recv,
    a_send,
    a_recv,
    m_send,
    m_recv,
    x_send,
    x_recv,
):
    pos = lax.axis_index("tile")
    mem = lax.axis_index("mem")
    started, a1, fine = (started0, started1), (a10, a11), (fine0, fine1)
    pooled, a2, coarse = (pooled0, pooled1), (a20, a21), (coarse0, coarse1)
    d_ref = (d_ref0, d_ref1)

    def along_tile(d):
        return {"tile": lax.rem(pos + d, NT)}

    def torus(e):
        return {"tile": lax.rem(pos // 4 + e // 4, 4) * 4 + lax.rem(lax.rem(pos, 4) + e % 4, 4)}

    def along_y(d):
        return {"mem": lax.rem(mem + 2 * d, NM)}

    def across(d):
        there = lax.rem(mem + 2 * d, NM)
        return {"mem": there + 1 - 2 * lax.rem(there, 2)}

    other_core = {"mem": mem + 1 - 2 * lax.rem(mem, 2)}

    barrier = pltpu.get_barrier_semaphore()

    def greet(where):
        pl.semaphore_signal(barrier, inc=1, device_id=where, device_id_type=MESH)

    each(NT, lambda d: greet(along_tile(d)))
    each(NY, lambda d: greet(along_y(d)))
    each(NY, lambda d: greet(across(d)))
    greet(other_core)

    inputs = (
        (noisy_hbm, noisy_ref),
        (step_hbm, step_ref),
        (wt_hbm, wt_ref),
        (wl_hbm, wl_ref),
        (gf_hbm, gf_ref),
        (seam_hbm, seam_ref),
        (wf_hbm, wf_ref),
        (gc_hbm, gc_ref),
        (go_hbm, go_ref),
        (route_hbm, route_ref),
        (block_hbm, block_ref),
        (frac_hbm, frac_ref),
        (wo_hbm, wo_ref),
        (wc_hbm, wc_ref),
    )
    loads = [pltpu.make_async_copy(a, b, w_sem.at[i]) for i, (a, b) in enumerate(inputs)]
    for load in loads:
        load.start()

    ones_ref[...] = jnp.where(
        iota((256, 256), 0) // 128 == iota((256, 256), 1) // 128, 1.0 / 128, 0.0
    ).astype(BF16)
    i = iota((256, 256), 0)
    to_rows = onehot(((i & 7) * N + ((i >> 3) & 1) * H + (i >> 4)) == iota((256, 256), 1))
    lift_w[...] = jnp.zeros((8, 128, 256), BF16)
    for load in loads[:6]:
        load.wait()
    wl = wl_ref[...].astype(F32)
    wl_zero = jnp.zeros_like(wl)
    wl_pair = jnp.concatenate(
        [
            jnp.concatenate([wl, wl_zero], axis=1),
            jnp.concatenate([wl_zero, wl], axis=1),
        ],
        axis=0,
    ).astype(BF16)
    for q in range(8):
        lift_w[q, q * B : (q + 1) * B, :] = wl_pair

    level = jnp.where(iota((8, 128), 0) < 4, step_ref[0:1, 0:1], step_ref[0:1, 1:2]).astype(F32)
    fraction = level / (STEPS - 1)
    high_root = 80.0 ** (1.0 / 7.0)
    low_root = 0.002 ** (1.0 / 7.0)
    root = high_root + fraction * (low_root - high_root)
    square = root * root
    sigma = square * square * square * root
    denominator = sigma * sigma + 1.0
    scales = (lax.rsqrt(denominator), 1.0 / denominator, sigma * lax.rsqrt(denominator))
    c_in, c_skip, c_out = [[twice(x[0:1]), twice(x[4:5])] for x in scales]
    lane = iota((8, 128), 1)
    frequency = jnp.exp((lane & 63).astype(F32) * (-math.log(10000.0) / 64))
    angles = level * frequency
    features = jnp.where(lane < 64, jnp.sin(angles), jnp.cos(angles))
    embedded = jnp.dot(
        features, wt_ref[...], preferred_element_type=F32, precision=lax.Precision.HIGHEST
    )
    embedded = embedded / (1.0 + jnp.exp(-embedded))
    temb = [twice(embedded[0:1]), twice(embedded[4:5])]
    gain_fine = twice(gf_ref[...]) * 0.5

    for m in range(2):
        moved = dot(to_rows, noisy_ref[m * 256 : (m + 1) * 256, :])
        nx[m * 256 : (m + 1) * 256, :] = moved.astype(BF16)
        sx[m * 256 : (m + 1) * 256, :] = (moved * c_in[m]).astype(BF16)

    def lift(m):
        for q in range(8):
            for half in range(2):
                pair = half * 8 + q
                cells = sx[m * 256 : (m + 1) * 256, half * 128 : (half + 1) * 128]
                first = (dot(cells, lift_w[q]) + temb[m]).astype(BF16)
                started[m][2 * pair] = first[:, :128]
                started[m][2 * pair + 1] = first[:, 128:]
                normed = act(first, ones_ref[...], gain_fine)
                a1[m][2 * pair + 1, B : B + 256, :] = normed[:, :128]
                a1[m][2 * pair + 2, B : B + 256, :] = normed[:, 128:]

    lift(0)

    pl.semaphore_wait(barrier, NT - 1 + NM - 1)

    def h_copy(side):
        return pltpu.make_async_remote_copy(
            src_ref=nx.at[:, pl.ds(side * 128, 128)],
            dst_ref=halo.at[side],
            send_sem=h_send.at[side],
            recv_sem=h_recv.at[side],
            device_id=along_tile(1 if side else NT - 1),
            device_id_type=MESH,
        )

    def c_copy(m, side):
        return pltpu.make_async_remote_copy(
            src_ref=edges.at[m, side],
            dst_ref=halo2.at[m, side],
            send_sem=c_send.at[m, side],
            recv_sem=c_recv.at[m, side],
            device_id=along_tile(1 if side else NT - 1),
            device_id_type=MESH,
        )

    for side in range(2):
        h_copy(side).start()

    half = iota((B, 1), 0) >> 3
    own = iota((B, 1), 0) & 7
    flipped = []
    for side in range(4):
        tile = column(seam_ref[0, side : side + 1, :] & 7).astype(jnp.int32)
        flag = column(seam_ref[2, side : side + 1, :]).astype(jnp.int32)
        if side == 0:
            source = jnp.where(half == 0, 8 + tile, own)
            flag = jnp.where(half == 0, flag, 0)
        elif side == 2:
            source = jnp.where(half == 0, 8 + own, tile)
            flag = jnp.where(half == 0, 0, flag)
        else:
            source = ((half + flag) & 1) * 8 + tile
        flipped.append(jnp.broadcast_to(flag.astype(F32), (B, 128)))
        apart = iota((B, 256), 1) - source
        for c in range(256 // B):
            seam_w[side, c * B : (c + 1) * B, :] = onehot(apart == c * B)

    def north_south(a_ref, cols, rows):
        for side, row_from, row_to in ((0, rows, 0), (2, 1, rows + 1)):
            edge = a_ref[1 : cols + 1, row_from * B : (row_from + 1) * B, :]
            got = from_side(seam_w.at[side], edge.reshape(cols * B, 128), cols, flipped[side])
            for c in range(cols):
                a_ref[c + 1, row_to * B : (row_to + 1) * B, :] = got[c].astype(BF16)

    def corners(a_ref, cols, rows):
        for col, inner in ((0, 1), (cols + 1, cols)):
            north = a_ref[inner, 0:B, :].astype(F32)
            south = a_ref[inner, (rows + 1) * B : (rows + 2) * B, :].astype(F32)
            last = a_ref[col, rows * B : (rows + 1) * B, :].astype(F32)
            first = a_ref[col, B : 2 * B, :].astype(F32)
            a_ref[col, 0:B, :] = jnp.concatenate([north[:8], last[:8]], axis=0).astype(BF16)
            a_ref[col, (rows + 1) * B : (rows + 2) * B, :] = jnp.concatenate(
                [first[8:], south[8:]], axis=0
            ).astype(BF16)

    north_south(a10, N, H)
    loads[6].wait()
    conv_weights(fine_w, wf_ref)

    for load in loads[7:]:
        load.wait()
    gain_coarse = gc_ref[...] * 0.5
    gain_out = twice(go_ref[...]) * 0.5
    conv_weights(coarse_w, wc_ref)
    for q in range(8):
        for j in range(2):
            place = onehot(iota((8, 128), 1) == iota((8, 128), 0) + (16 * q + 8 * j))
            out_w[(2 * q + j) * 128 : (2 * q + j + 1) * 128, :] = lax.dot_general(
                wo_ref[...], place, (((0,), (0,)), ((), ())), preferred_element_type=F32
            ).astype(BF16)
    frac_p, frac_q = [
        jnp.broadcast_to(column(frac_ref[k : k + 1, :]), (B, 256)) for k in range(2)
    ]

    route = jnp.broadcast_to(route_ref[...], (8, 128))
    rank = jnp.zeros((8, 128), jnp.int32)
    for s in range(1, 8):
        again = (pltpu.roll(route, s, 1) == route) & ((lane & 7) >= s)
        rank = rank + jnp.where(again, 1, 0)
    def offset(to, start):
        return (((to >> 2) - (start >> 2)) & 3) * 4 + ((to - start) & 3)

    key = offset(route, pos) * 2 + rank
    pick = onehot(iota((128, 128), 0) == pos * 8 + (iota((128, 128), 1) & 7))
    key = dot(key.astype(F32).astype(BF16), pick)[0:1, :]
    i, j = iota((512, 128), 0), iota((512, 128), 1)
    slot_ref[...] = onehot(
        ((i >> 4).astype(F32) == key) & (((i >> 3) & 1) == ((j >> 3) & 1)) & ((i & 7) == (j >> 4))
    )
    slot = jnp.where(route == pos, offset(pos, lane >> 3) * 2 + rank, -1).astype(F32)
    diagonal = iota((128, 128), 0) == iota((128, 128), 1)
    slot = jnp.sum(jnp.where(diagonal, slot[0:1, :], 0.0), axis=1, keepdims=True)
    pick = onehot(slot == (iota((128, 512), 1) >> 4).astype(F32))
    block = jnp.broadcast_to(block_ref[...], (8, 128)).astype(F32) + 1.0
    block = dot(block.astype(BF16), pick)[0:1, :]
    i, j = iota((64, 512), 0), iota((64, 512), 1)
    sum_ref[...] = onehot(
        (((i >> 4) + 1).astype(F32) == block)
        & (((i >> 3) & 1) == ((j >> 3) & 1))
        & ((i & 7) == (j & 7))
    )

    def fine_post(m, pair, buf):
        base = jnp.concatenate([started[m][2 * pair], started[m][2 * pair + 1]], axis=1)
        out = (base.astype(F32) + buf[...]).astype(BF16)
        fine[m][2 * pair] = out[:, :128]
        fine[m][2 * pair + 1] = out[:, 128:]
        wide = out.astype(F32).reshape(H // 2, 2, B, 256)
        tall = wide[:, 0] + wide[:, 1]
        mean = ((tall[:, :, :128] + tall[:, :, 128:]) * 0.25).reshape(128, 128).astype(BF16)
        pooled[m][pair] = mean
        a2[m][pair + 1, B : B + 128, :] = act(mean, ones_ref[0:128, 0:128], gain_coarse)

    bufs = (g0, g1)
    waiting = []

    def finish():
        if waiting:
            m, pair, slot = waiting.pop()
            fine_post(m, pair, bufs[slot])

    def fine_next(m, pair):
        slot = 1 - waiting[0][2] if waiting else 0
        bufs[slot][...] = conv_pair(a1[m], fine_w, pair, 256)
        finish()
        waiting.append((m, pair, slot))

    def fine_run(count):
        for _ in range(count):
            m, pair, _ = waiting[0]
            fine_next(m, pair + 1)

    def send_edges(m):
        edges[m, 0] = a2[m][1, B : B + 128, :]
        edges[m, 1] = a2[m][H, B : B + 128, :]
        for side in range(2):
            c_copy(m, side).start()

    fine_next(0, 1)
    fine_run(H - 3)
    finish()

    for side in range(2):
        h_copy(side).wait()
    sides = []
    for side, got, w in ((3, 1, lift_w[7, :, 128:256]), (1, 0, lift_w[0, :, 0:128])):
        both = jnp.concatenate([halo[got, 0:256, :], halo[got, 256:512, :]], axis=1)
        moved = jnp.concatenate(from_side(seam_w.at[side], both, H, flipped[side]), axis=0)
        sides.append(
            [
                dot((moved[:, m * 128 : (m + 1) * 128] * c_in[m][:, :128]).astype(BF16), w)
                for m in range(2)
            ]
        )
    def east_west(m):
        first = (jnp.concatenate([sides[0][m], sides[1][m]], axis=1) + temb[m]).astype(BF16)
        normed = act(first, ones_ref[...], gain_fine)
        a1[m][0, B : B + 256, :] = normed[:, :128]
        a1[m][N + 1, B : B + 256, :] = normed[:, 128:]
        corners(a1[m], N, H)

    def a_copy(k, d):
        return pltpu.make_async_remote_copy(
            src_ref=send.at[k, d],
            dst_ref=recv.at[k, d],
            send_sem=a_send.at[k, d],
            recv_sem=a_recv.at[k, d],
            device_id=torus(d),
            device_id_type=MESH,
        )

    def y_copy(m, k, d):
        return pltpu.make_async_remote_copy(
            src_ref=target.at[m, k, 0],
            dst_ref=target.at[m, k, d],
            send_sem=m_send.at[2 * m + k, d],
            recv_sem=m_recv.at[2 * m + k, d],
            device_id=along_y(d),
            device_id_type=MESH,
        )

    def x_copy(m, k, d):
        last = m == 1 and k == 1 and d > 0
        return pltpu.make_async_remote_copy(
            src_ref=target.at[m, k, 0 if last else d],
            dst_ref=other.at[m, k, d],
            send_sem=x_send.at[2 * m + k, d],
            recv_sem=x_recv.at[2 * m + k, d],
            device_id=across(d) if last else other_core,
            device_id_type=MESH,
        )

    def coarse_level(m):
        north_south(a2[m], H, H // 2)
        for side in range(2):
            c_copy(m, side).wait()
        for side, got, col in ((1, 0, H + 1), (3, 1, 0)):
            moved = from_side(seam_w.at[side], halo2[m, got], H // 2, flipped[side])
            for r in range(H // 2):
                a2[m][col, (r + 1) * B : (r + 2) * B, :] = moved[r].astype(BF16)
        corners(a2[m], H, H // 2)

        def body(q, _):
            for pair in (4 * q, 4 * q + 1, 4 * q + 2, 4 * q + 3):
                got = conv_pair(a2[m], coarse_w, pair, 128)
                base = jnp.concatenate([pooled[m][2 * pair], pooled[m][2 * pair + 1]], axis=1)
                out = (base.astype(F32) + got).astype(BF16)
                coarse[m][2 * pair] = out[:, :128]
                coarse[m][2 * pair + 1] = out[:, 128:]
            return 0

        lax.fori_loop(0, 2, body, 0)

    def state(m, row, count):
        start, rows = row * B, count * B
        for pair in range(H):
            f = jnp.concatenate(
                [
                    fine[m][2 * pair, start : start + rows, :],
                    fine[m][2 * pair + 1, start : start + rows, :],
                ],
                axis=1,
            ).astype(F32)
            c = coarse[m][pair, start // 2 : (start + rows) // 2, :].astype(F32)
            c = c.reshape(count // 2, 1, B, 128)
            c = jnp.concatenate([c, c], axis=1).reshape(rows, 128)
            act_s[:rows, pair * 256 : (pair + 1) * 256] = act(f + twice(c), ones_ref[...], gain_out)
        left = dot(act_s[:rows, :2048], out_w[...])
        right = dot(act_s[:rows, 2048:], out_w[...])
        proj = jnp.concatenate([left, right], axis=1)
        cells = slice(m * 256 + start, m * 256 + start + rows)
        den = c_skip[m] * nx[cells, :].astype(F32) + c_out[m] * proj
        d_ref[m][start : start + rows, :] = den
        by_row[2 * m, start : start + rows, :] = den[:, :128]
        by_row[2 * m + 1, start : start + rows, :] = den[:, 128:]

    def route_rows(m, k):
        start = k * CHUNK
        den = d_ref[m][start : start + CHUNK, :].reshape(8, B, 256)
        below = d_ref[m][start + B : start + B + CHUNK, :].reshape(8, B, 256)
        mixed = ((1.0 - frac_p) * den + frac_p * below).reshape(CHUNK, 256)
        shifted = pltpu.roll(mixed, 248, 1)
        shifted = jnp.where(iota((CHUNK, 256), 1) >= 248, mixed, shifted)
        out = (1.0 - frac_q) * mixed.reshape(8, B, 256) + frac_q * shifted.reshape(8, B, 256)
        blocks = dot(slot_ref[...], out.reshape(CHUNK, 256).astype(BF16)).astype(BF16)
        blocks = blocks.reshape(NT, 32, 256)
        recv[2 * m + k, 0] = blocks[0]
        send[2 * m + k] = blocks
        for d in FAR:
            a_copy(2 * m + k, d).start()

    def last_stage(m):
        state(m, 0, FIRST)
        route_rows(m, 0)
        state(m, FIRST, H - FIRST)
        d_ref[m][H * B :, :] = jnp.concatenate(
            [d_ref[m][8:16, :], d_ref[m][H * B - 8 : H * B, :]], axis=0
        )
        route_rows(m, 1)

    def sum_stage(m, k):
        each(NT, lambda d: a_copy(2 * m + k, d).wait_recv())
        total = dot(sum_ref[...], recv[2 * m + k].reshape(512, 256))
        target[m, k, 0] = total.astype(BF16)
        for d in (2, 1, 3):
            y_copy(m, k, d).start()
            if m == 1 and k == 1:
                x_copy(m, k, d).start()
        x_copy(m, k, 0).start()

    def pass_stage(m, k):
        for d in (1, 3, 2):
            y_copy(m, k, d).wait_recv()
            if not (m == 1 and k == 1):
                x_copy(m, k, d).start()

    def stat_stage(k):
        for m in range(2):
            for d in range(NY):
                x_copy(m, k, d).wait_recv()
        for q in range(4):
            rows = slice(q * B, (q + 1) * B)
            values = [
                held[m, k, d, rows, :].astype(F32)
                for held in (target, other)
                for m in range(2)
                for d in range(NY)
            ]
            mean = functools.reduce(lambda a, b: a + b, values) * (1.0 / 16)
            squares = functools.reduce(lambda a, b: a + b, [(v - mean) * (v - mean) for v in values])
            spread = jnp.sqrt(squares / 15.0 + 1e-06)
            for half in range(2):
                row = half * H + k * 8
                mean_ref[q, row : row + 8, :] = mean[half * 8 : half * 8 + 8]
                spread_ref[q, row : row + 8, :] = spread[half * 8 : half * 8 + 8]

    east_west(0)
    fine_next(0, 0)
    fine_next(0, H - 1)
    finish()
    send_edges(0)
    lift(1)
    north_south(a11, N, H)
    east_west(1)
    fine_next(1, 0)
    fine_next(1, H - 1)
    fine_next(1, 1)
    send_edges(1)
    fine_run(EARLY - 1)
    finish()
    coarse_level(0)
    last_stage(0)
    fine_next(1, EARLY + 1)
    fine_run(H - 3 - EARLY)
    finish()
    coarse_level(1)
    last_stage(1)

    for m in range(2):
        for b in range(B):
            start = m * 256 + (b % 8) * N + (b // 8) * H
            for side in range(2):
                den_ref[start : start + H, side * 128 : (side + 1) * 128] = by_row[
                    2 * m + side, pl.ds(b, H, stride=B), :
                ]
    store_den = pltpu.make_async_copy(den_ref, den_hbm, o_sem.at[0])
    store_den.start()

    for m in range(2):
        for k in range(2):
            sum_stage(m, k)
    for m in range(2):
        for k in range(2):
            pass_stage(m, k)
    for k in range(2):
        stat_stage(k)
    store_mean = pltpu.make_async_copy(mean_ref, stat_hbm.at[0], o_sem.at[1])
    store_spread = pltpu.make_async_copy(spread_ref, stat_hbm.at[1], o_sem.at[2])
    store_mean.start()
    store_spread.start()
    for k in range(4):
        each(NT, lambda d: a_copy(k, d).wait_send())
    for m in range(2):
        for k in range(2):
            each(NY, lambda d: y_copy(m, k, d).wait_send())
            for d in range(NY):
                x_copy(m, k, d).wait_send()
    store_den.wait()
    store_mean.wait()
    store_spread.wait()


def on_device(
    noisy,
    timestep,
    seams,
    corner_list,
    route,
    target_block,
    frac,
    w_time,
    w_lift,
    w_fine,
    w_coarse,
    gain_fine,
    gain_coarse,
    gain_out,
    w_out,
):
    hbm = pl.BlockSpec(memory_space=pltpu.HBM)
    dma = pltpu.SemaphoreType.DMA
    den, stat = pl.pallas_call(
        kernel,
        out_shape=(
            jax.ShapeDtypeStruct((512, 256), F32),
            jax.ShapeDtypeStruct((2, 4, N, 256), F32),
        ),
        in_specs=[hbm] * 14,
        out_specs=(hbm, hbm),
        scratch_shapes=[
            pltpu.VMEM((512, 256), BF16),
            pltpu.VMEM((1, 2), jnp.int32),
            pltpu.VMEM((3, 4, 8), jnp.int32),
            pltpu.VMEM((1, 128), jnp.int32),
            pltpu.VMEM((1, 128), jnp.int32),
            pltpu.VMEM((2, 8), F32),
            pltpu.VMEM((128, 128), F32),
            pltpu.VMEM((8, 128), BF16),
            pltpu.VMEM((9, 128, 128), BF16),
            pltpu.VMEM((9, 128, 128), BF16),
            pltpu.VMEM((1, 128), F32),
            pltpu.VMEM((1, 128), F32),
            pltpu.VMEM((1, 128), F32),
            pltpu.VMEM((8, 128), BF16),
            pltpu.VMEM((512, 256), BF16),
            pltpu.VMEM((512, 256), BF16),
            pltpu.VMEM((8, 128, 256), BF16),
            pltpu.VMEM((2048, 128), BF16),
            pltpu.VMEM((1536, 256), BF16),
            pltpu.VMEM((1536, 256), BF16),
            pltpu.VMEM((256, 256), BF16),
            pltpu.VMEM((4, 256, 256), BF16),
            pltpu.VMEM((512, 128), BF16),
            pltpu.VMEM((64, 512), BF16),
            pltpu.VMEM((2, 512, 128), BF16),
        ]
        + [pltpu.VMEM((N, 256, 128), BF16)] * 2
        + [pltpu.VMEM((N + 2, 288, 128), BF16)] * 2
        + [pltpu.VMEM((N, 256, 128), BF16)] * 2
        + [pltpu.VMEM((H, 128, 128), BF16)] * 2
        + [pltpu.VMEM((H + 2, 160, 128), BF16)] * 2
        + [pltpu.VMEM((H, 128, 128), BF16)] * 2
        + [
            pltpu.VMEM((2, 2, 128, 128), BF16),
            pltpu.VMEM((2, 2, 128, 128), BF16),
            pltpu.VMEM((256, 256), F32),
            pltpu.VMEM((256, 256), F32),
            pltpu.VMEM((FIRST * B, 4096), BF16),
            pltpu.VMEM(((H + 1) * B, 256), F32),
            pltpu.VMEM(((H + 1) * B, 256), F32),
            pltpu.VMEM((4, 256, 128), F32),
            pltpu.VMEM((512, 256), F32),
            pltpu.VMEM((4, N, 256), F32),
            pltpu.VMEM((4, N, 256), F32),
            pltpu.VMEM((4, NT, 32, 256), BF16),
            pltpu.VMEM((4, NT, 32, 256), BF16),
            pltpu.VMEM((2, 2, NY, 64, 256), BF16),
            pltpu.VMEM((2, 2, NY, 64, 256), BF16),
            dma((14,)),
            dma((3,)),
            dma((2,)),
            dma((2,)),
            dma((2, 2)),
            dma((2, 2)),
            dma((4, NT)),
            dma((4, NT)),
            dma((4, NY)),
            dma((4, NY)),
            dma((4, NY)),
            dma((4, NY)),
        ],
        compiler_params=pltpu.CompilerParams(
            collective_id=0, has_side_effects=True, vmem_limit_bytes=56 * 1024 * 1024
        ),
    )(
        noisy.reshape(512, 256),
        timestep.reshape(1, 2),
        seams.transpose(2, 1, 0),
        route.reshape(1, 128),
        target_block.reshape(1, 128),
        frac.T,
        w_time,
        w_lift,
        w_fine,
        w_coarse,
        gain_fine.reshape(1, 128),
        gain_coarse.reshape(1, 128),
        gain_out.reshape(1, 128),
        w_out.T,
    )
    return (den.reshape(noisy.shape), stat[0], stat[1])


def solution(mesh):
    placed = (
        P("mem", "tile", None, None),
        P("mem"),
        P("tile", None, None),
        P("tile", None, None),
        P(),
        P(),
        P("tile", None),
        P(),
        P(),
        P(),
        P(),
        P(),
        P(),
        P(),
        P(),
    )
    return jax.shard_map(
        on_device,
        mesh=mesh,
        in_specs=placed,
        out_specs=(P("mem", "tile", None, None), P("tile", None, None), P("tile", None, None)),
        check_vma=False,
    )
```

```python
import functools
import math

import jax
import jax.numpy as jnp
from jax import lax
from jax.experimental import pallas as pl
from jax.experimental.pallas import tpu as pltpu
from jax.sharding import PartitionSpec as P

STEPS = 1000
MESH = pl.DeviceIdType.MESH
F32 = jnp.float32
BF16 = jnp.bfloat16

B = 16
N = 32
H = N // 2
NT = 16
NM = 8
NY = NM // 2
FAR = sorted(range(1, NT), key=lambda e: -min(e // 4, 4 - e // 4) - min(e % 4, 4 - e % 4))
FIRST = 10
EARLY = 9
CHUNK = 128


def dot(a, b):
    return jnp.dot(a, b, preferred_element_type=F32)


def twice(x):
    return jnp.concatenate([x, x], axis=-1)


def iota(shape, dim):
    return lax.broadcasted_iota(jnp.int32, shape, dim)


def onehot(where):
    return jnp.where(where, 1.0, 0.0).astype(BF16)


def act(x, ones, half_gain):
    short = x.astype(BF16)
    mean = dot(short * short, ones)
    h = x.astype(F32) * lax.rsqrt(mean + 1e-06) * half_gain
    return (h + h * jnp.tanh(h)).astype(BF16)


def column(row):
    spread = jnp.broadcast_to(row.astype(F32), (B, 8))
    own = iota((B, 8), 1) == (iota((B, 8), 0) & 7)
    return jnp.sum(jnp.where(own, spread, 0.0), axis=1, keepdims=True)


def from_side(perm, edge, n, flipped):
    rows = edge.shape[0]
    if rows > 256:
        edge = jnp.concatenate([edge[:256], edge[256:]], axis=1)
        got = dot(perm[...], edge)
        pieces = [
            got[c % H * B : (c % H + 1) * B, c // H * 128 : (c // H + 1) * 128] for c in range(n)
        ]
    else:
        got = dot(perm[:rows, :rows], edge)
        pieces = [got[c * B : (c + 1) * B] for c in range(n)]
    if edge.shape[1] > 128 and rows <= 256:
        flipped = twice(flipped)
    return [
        jnp.where(flipped > 0.5, pieces[n - 1 - c], pieces[c]) for c in range(n)
    ]


def conv_weights(out_ref, w_ref):
    zero = jnp.zeros((128, 128), BF16)
    for i in range(3):
        for j in range(4):
            left = w_ref[3 * i + j] if j < 3 else zero
            right = w_ref[3 * i + j - 1] if j > 0 else zero
            start = (4 * i + j) * 128
            out_ref[start : start + 128, :] = jnp.concatenate([left, right], axis=1)


def conv_pair(a_ref, w_ref, pair, rows):
    parts = []
    for i in range(3):
        for j in range(4):
            parts.append(a_ref[2 * pair + j, i * B : i * B + rows, :])
    return dot(jnp.concatenate(parts, axis=1), w_ref[...])


def each(count, what):
    def body(d, _):
        what(d)
        return 0

    lax.fori_loop(1, count, body, 0)


def kernel(
    noisy_hbm,
    step_hbm,
    seam_hbm,
    route_hbm,
    block_hbm,
    frac_hbm,
    wt_hbm,
    wl_hbm,
    wf_hbm,
    wc_hbm,
    gf_hbm,
    gc_hbm,
    go_hbm,
    wo_hbm,
    den_hbm,
    stat_hbm,
    noisy_ref,
    step_ref,
    seam_ref,
    route_ref,
    block_ref,
    frac_ref,
    wt_ref,
    wl_ref,
    wf_ref,
    wc_ref,
    gf_ref,
    gc_ref,
    go_ref,
    wo_ref,
    nx,
    sx,
    lift_w,
    out_w,
    fine_w,
    coarse_w,
    ones_ref,
    seam_w,
    slot_ref,
    sum_ref,
    halo,
    started0,
    started1,
    a10,
    a11,
    fine0,
    fine1,
    pooled0,
    pooled1,
    a20,
    a21,
    coarse0,
    coarse1,
    halo2,
    edges,
    g0,
    g1,
    act_s,
    d_ref0,
    d_ref1,
    by_row,
    den_ref,
    mean_ref,
    spread_ref,
    send,
    recv,
    target,
    other,
    w_sem,
    o_sem,
    h_send,
    h_recv,
    c_send,
    c_recv,
    a_send,
    a_recv,
    m_send,
    m_recv,
    x_send,
    x_recv,
):
    pos = lax.axis_index("tile")
    mem = lax.axis_index("mem")
    started, a1, fine = (started0, started1), (a10, a11), (fine0, fine1)
    pooled, a2, coarse = (pooled0, pooled1), (a20, a21), (coarse0, coarse1)
    d_ref = (d_ref0, d_ref1)

    def along_tile(d):
        return {"tile": lax.rem(pos + d, NT)}

    def torus(e):
        return {"tile": lax.rem(pos // 4 + e // 4, 4) * 4 + lax.rem(lax.rem(pos, 4) + e % 4, 4)}

    def along_y(d):
        return {"mem": lax.rem(mem + 2 * d, NM)}

    def across(d):
        there = lax.rem(mem + 2 * d, NM)
        return {"mem": there + 1 - 2 * lax.rem(there, 2)}

    other_core = {"mem": mem + 1 - 2 * lax.rem(mem, 2)}

    barrier = pltpu.get_barrier_semaphore()

    def greet(where):
        pl.semaphore_signal(barrier, inc=1, device_id=where, device_id_type=MESH)

    each(NT, lambda d: greet(along_tile(d)))
    each(NY, lambda d: greet(along_y(d)))
    each(NY, lambda d: greet(across(d)))
    greet(other_core)

    inputs = (
        (noisy_hbm, noisy_ref),
        (step_hbm, step_ref),
        (wt_hbm, wt_ref),
        (wl_hbm, wl_ref),
        (gf_hbm, gf_ref),
        (seam_hbm, seam_ref),
        (wf_hbm, wf_ref),
        (gc_hbm, gc_ref),
        (go_hbm, go_ref),
        (route_hbm, route_ref),
        (block_hbm, block_ref),
        (frac_hbm, frac_ref),
        (wo_hbm, wo_ref),
        (wc_hbm, wc_ref),
    )
    loads = [pltpu.make_async_copy(a, b, w_sem.at[i]) for i, (a, b) in enumerate(inputs)]
    for load in loads:
        load.start()

    ones_ref[...] = jnp.where(
        iota((256, 256), 0) // 128 == iota((256, 256), 1) // 128, 1.0 / 128, 0.0
    ).astype(BF16)
    i = iota((256, 256), 0)
    to_rows = onehot(((i & 7) * N + ((i >> 3) & 1) * H + (i >> 4)) == iota((256, 256), 1))
    lift_w[...] = jnp.zeros((8, 128, 256), BF16)
    for load in loads[:6]:
        load.wait()
    wl = wl_ref[...].astype(F32)
    wl_zero = jnp.zeros_like(wl)
    wl_pair = jnp.concatenate(
        [
            jnp.concatenate([wl, wl_zero], axis=1),
            jnp.concatenate([wl_zero, wl], axis=1),
        ],
        axis=0,
    ).astype(BF16)
    for q in range(8):
        lift_w[q, q * B : (q + 1) * B, :] = wl_pair

    level = jnp.where(iota((8, 128), 0) < 4, step_ref[0:1, 0:1], step_ref[0:1, 1:2]).astype(F32)
    fraction = level / (STEPS - 1)
    high_root = 80.0 ** (1.0 / 7.0)
    low_root = 0.002 ** (1.0 / 7.0)
    root = high_root + fraction * (low_root - high_root)
    square = root * root
    sigma = square * square * square * root
    denominator = sigma * sigma + 1.0
    scales = (lax.rsqrt(denominator), 1.0 / denominator, sigma * lax.rsqrt(denominator))
    c_in, c_skip, c_out = [[twice(x[0:1]), twice(x[4:5])] for x in scales]
    lane = iota((8, 128), 1)
    frequency = jnp.exp((lane & 63).astype(F32) * (-math.log(10000.0) / 64))
    angles = level * frequency
    features = jnp.where(lane < 64, jnp.sin(angles), jnp.cos(angles))
    embedded = jnp.dot(
        features, wt_ref[...], preferred_element_type=F32, precision=lax.Precision.HIGHEST
    )
    embedded = embedded / (1.0 + jnp.exp(-embedded))
    temb = [twice(embedded[0:1]), twice(embedded[4:5])]
    gain_fine = twice(gf_ref[...]) * 0.5

    for m in range(2):
        moved = dot(to_rows, noisy_ref[m * 256 : (m + 1) * 256, :])
        nx[m * 256 : (m + 1) * 256, :] = moved.astype(BF16)
        sx[m * 256 : (m + 1) * 256, :] = (moved * c_in[m]).astype(BF16)

    def lift(m):
        for q in range(8):
            for half in range(2):
                pair = half * 8 + q
                cells = sx[m * 256 : (m + 1) * 256, half * 128 : (half + 1) * 128]
                first = (dot(cells, lift_w[q]) + temb[m]).astype(BF16)
                started[m][2 * pair] = first[:, :128]
                started[m][2 * pair + 1] = first[:, 128:]
                normed = act(first, ones_ref[...], gain_fine)
                a1[m][2 * pair + 1, B : B + 256, :] = normed[:, :128]
                a1[m][2 * pair + 2, B : B + 256, :] = normed[:, 128:]

    lift(0)

    pl.semaphore_wait(barrier, NT - 1 + NM - 1)

    def h_copy(side):
        return pltpu.make_async_remote_copy(
            src_ref=nx.at[:, pl.ds(side * 128, 128)],
            dst_ref=halo.at[side],
            send_sem=h_send.at[side],
            recv_sem=h_recv.at[side],
            device_id=along_tile(1 if side else NT - 1),
            device_id_type=MESH,
        )

    def c_copy(m, side):
        return pltpu.make_async_remote_copy(
            src_ref=edges.at[m, side],
            dst_ref=halo2.at[m, side],
            send_sem=c_send.at[m, side],
            recv_sem=c_recv.at[m, side],
            device_id=along_tile(1 if side else NT - 1),
            device_id_type=MESH,
        )

    for side in range(2):
        h_copy(side).start()

    half = iota((B, 1), 0) >> 3
    own = iota((B, 1), 0) & 7
    flipped = []
    for side in range(4):
        tile = column(seam_ref[0, side : side + 1, :] & 7).astype(jnp.int32)
        flag = column(seam_ref[2, side : side + 1, :]).astype(jnp.int32)
        if side == 0:
            source = jnp.where(half == 0, 8 + tile, own)
            flag = jnp.where(half == 0, flag, 0)
        elif side == 2:
            source = jnp.where(half == 0, 8 + own, tile)
            flag = jnp.where(half == 0, 0, flag)
        else:
            source = ((half + flag) & 1) * 8 + tile
        flipped.append(jnp.broadcast_to(flag.astype(F32), (B, 128)))
        apart = iota((B, 256), 1) - source
        for c in range(256 // B):
            seam_w[side, c * B : (c + 1) * B, :] = onehot(apart == c * B)

    def north_south(a_ref, cols, rows):
        for side, row_from, row_to in ((0, rows, 0), (2, 1, rows + 1)):
            edge = a_ref[1 : cols + 1, row_from * B : (row_from + 1) * B, :]
            got = from_side(seam_w.at[side], edge.reshape(cols * B, 128), cols, flipped[side])
            for c in range(cols):
                a_ref[c + 1, row_to * B : (row_to + 1) * B, :] = got[c].astype(BF16)

    def corners(a_ref, cols, rows):
        for col, inner in ((0, 1), (cols + 1, cols)):
            north = a_ref[inner, 0:B, :].astype(F32)
            south = a_ref[inner, (rows + 1) * B : (rows + 2) * B, :].astype(F32)
            last = a_ref[col, rows * B : (rows + 1) * B, :].astype(F32)
            first = a_ref[col, B : 2 * B, :].astype(F32)
            a_ref[col, 0:B, :] = jnp.concatenate([north[:8], last[:8]], axis=0).astype(BF16)
            a_ref[col, (rows + 1) * B : (rows + 2) * B, :] = jnp.concatenate(
                [first[8:], south[8:]], axis=0
            ).astype(BF16)

    north_south(a10, N, H)
    loads[6].wait()
    conv_weights(fine_w, wf_ref)

    for load in loads[7:]:
        load.wait()
    gain_coarse = gc_ref[...] * 0.5
    gain_out = twice(go_ref[...]) * 0.5
    conv_weights(coarse_w, wc_ref)
    for q in range(8):
        for j in range(2):
            place = onehot(iota((8, 128), 1) == iota((8, 128), 0) + (16 * q + 8 * j))
            out_w[(2 * q + j) * 128 : (2 * q + j + 1) * 128, :] = lax.dot_general(
                wo_ref[...], place, (((0,), (0,)), ((), ())), preferred_element_type=F32
            ).astype(BF16)
    frac_p, frac_q = [
        jnp.broadcast_to(column(frac_ref[k : k + 1, :]), (B, 256)) for k in range(2)
    ]

    route = jnp.broadcast_to(route_ref[...], (8, 128))
    rank = jnp.zeros((8, 128), jnp.int32)
    for s in range(1, 8):
        again = (pltpu.roll(route, s, 1) == route) & ((lane & 7) >= s)
        rank = rank + jnp.where(again, 1, 0)
    def offset(to, start):
        return (((to >> 2) - (start >> 2)) & 3) * 4 + ((to - start) & 3)

    key = offset(route, pos) * 2 + rank
    pick = onehot(iota((128, 128), 0) == pos * 8 + (iota((128, 128), 1) & 7))
    key = dot(key.astype(F32).astype(BF16), pick)[0:1, :]
    i, j = iota((512, 128), 0), iota((512, 128), 1)
    slot_ref[...] = onehot(
        ((i >> 4).astype(F32) == key) & (((i >> 3) & 1) == ((j >> 3) & 1)) & ((i & 7) == (j >> 4))
    )
    slot = jnp.where(route == pos, offset(pos, lane >> 3) * 2 + rank, -1).astype(F32)
    diagonal = iota((128, 128), 0) == iota((128, 128), 1)
    slot = jnp.sum(jnp.where(diagonal, slot[0:1, :], 0.0), axis=1, keepdims=True)
    pick = onehot(slot == (iota((128, 512), 1) >> 4).astype(F32))
    block = jnp.broadcast_to(block_ref[...], (8, 128)).astype(F32) + 1.0
    block = dot(block.astype(BF16), pick)[0:1, :]
    i, j = iota((64, 512), 0), iota((64, 512), 1)
    sum_ref[...] = onehot(
        (((i >> 4) + 1).astype(F32) == block)
        & (((i >> 3) & 1) == ((j >> 3) & 1))
        & ((i & 7) == (j & 7))
    )

    def fine_post(m, pair, buf):
        base = jnp.concatenate([started[m][2 * pair], started[m][2 * pair + 1]], axis=1)
        out = (base.astype(F32) + buf[...]).astype(BF16)
        fine[m][2 * pair] = out[:, :128]
        fine[m][2 * pair + 1] = out[:, 128:]
        wide = out.astype(F32).reshape(H // 2, 2, B, 256)
        tall = wide[:, 0] + wide[:, 1]
        mean = ((tall[:, :, :128] + tall[:, :, 128:]) * 0.25).reshape(128, 128).astype(BF16)
        pooled[m][pair] = mean
        a2[m][pair + 1, B : B + 128, :] = act(mean, ones_ref[0:128, 0:128], gain_coarse)

    bufs = (g0, g1)
    waiting = []

    def finish():
        if waiting:
            m, pair, slot = waiting.pop()
            fine_post(m, pair, bufs[slot])

    def fine_next(m, pair):
        slot = 1 - waiting[0][2] if waiting else 0
        bufs[slot][...] = conv_pair(a1[m], fine_w, pair, 256)
        finish()
        waiting.append((m, pair, slot))

    def fine_run(count):
        for _ in range(count):
            m, pair, _ = waiting[0]
            fine_next(m, pair + 1)

    def send_edges(m):
        edges[m, 0] = a2[m][1, B : B + 128, :]
        edges[m, 1] = a2[m][H, B : B + 128, :]
        for side in range(2):
            c_copy(m, side).start()

    fine_next(0, 1)
    fine_run(H - 3)
    finish()

    for side in range(2):
        h_copy(side).wait()
    sides = []
    for side, got, w in ((3, 1, lift_w[7, :, 128:256]), (1, 0, lift_w[0, :, 0:128])):
        both = jnp.concatenate([halo[got, 0:256, :], halo[got, 256:512, :]], axis=1)
        moved = jnp.concatenate(from_side(seam_w.at[side], both, H, flipped[side]), axis=0)
        sides.append(
            [
                dot((moved[:, m * 128 : (m + 1) * 128] * c_in[m][:, :128]).astype(BF16), w)
                for m in range(2)
            ]
        )
    def east_west(m):
        first = (jnp.concatenate([sides[0][m], sides[1][m]], axis=1) + temb[m]).astype(BF16)
        normed = act(first, ones_ref[...], gain_fine)
        a1[m][0, B : B + 256, :] = normed[:, :128]
        a1[m][N + 1, B : B + 256, :] = normed[:, 128:]
        corners(a1[m], N, H)

    def a_copy(k, d):
        return pltpu.make_async_remote_copy(
            src_ref=send.at[k, d],
            dst_ref=recv.at[k, d],
            send_sem=a_send.at[k, d],
            recv_sem=a_recv.at[k, d],
            device_id=torus(d),
            device_id_type=MESH,
        )

    def y_copy(m, k, d):
        return pltpu.make_async_remote_copy(
            src_ref=target.at[m, k, 0],
            dst_ref=target.at[m, k, d],
            send_sem=m_send.at[2 * m + k, d],
            recv_sem=m_recv.at[2 * m + k, d],
            device_id=along_y(d),
            device_id_type=MESH,
        )

    def x_copy(m, k, d):
        last = m == 1 and k == 1 and d > 0
        return pltpu.make_async_remote_copy(
            src_ref=target.at[m, k, 0 if last else d],
            dst_ref=other.at[m, k, d],
            send_sem=x_send.at[2 * m + k, d],
            recv_sem=x_recv.at[2 * m + k, d],
            device_id=across(d) if last else other_core,
            device_id_type=MESH,
        )

    def coarse_level(m):
        north_south(a2[m], H, H // 2)
        for side in range(2):
            c_copy(m, side).wait()
        for side, got, col in ((1, 0, H + 1), (3, 1, 0)):
            moved = from_side(seam_w.at[side], halo2[m, got], H // 2, flipped[side])
            for r in range(H // 2):
                a2[m][col, (r + 1) * B : (r + 2) * B, :] = moved[r].astype(BF16)
        corners(a2[m], H, H // 2)

        def body(q, _):
            for pair in (4 * q, 4 * q + 1, 4 * q + 2, 4 * q + 3):
                got = conv_pair(a2[m], coarse_w, pair, 128)
                base = jnp.concatenate([pooled[m][2 * pair], pooled[m][2 * pair + 1]], axis=1)
                out = (base.astype(F32) + got).astype(BF16)
                coarse[m][2 * pair] = out[:, :128]
                coarse[m][2 * pair + 1] = out[:, 128:]
            return 0

        lax.fori_loop(0, 2, body, 0)

    def state(m, row, count):
        start, rows = row * B, count * B
        for pair in range(H):
            f = jnp.concatenate(
                [
                    fine[m][2 * pair, start : start + rows, :],
                    fine[m][2 * pair + 1, start : start + rows, :],
                ],
                axis=1,
            ).astype(F32)
            c = coarse[m][pair, start // 2 : (start + rows) // 2, :].astype(F32)
            c = c.reshape(count // 2, 1, B, 128)
            c = jnp.concatenate([c, c], axis=1).reshape(rows, 128)
            act_s[:rows, pair * 256 : (pair + 1) * 256] = act(f + twice(c), ones_ref[...], gain_out)
        left = dot(act_s[:rows, :2048], out_w[...])
        right = dot(act_s[:rows, 2048:], out_w[...])
        proj = jnp.concatenate([left, right], axis=1)
        cells = slice(m * 256 + start, m * 256 + start + rows)
        den = c_skip[m] * nx[cells, :].astype(F32) + c_out[m] * proj
        d_ref[m][start : start + rows, :] = den
        by_row[2 * m, start : start + rows, :] = den[:, :128]
        by_row[2 * m + 1, start : start + rows, :] = den[:, 128:]

    def route_rows(m, k):
        start = k * CHUNK
        den = d_ref[m][start : start + CHUNK, :].reshape(8, B, 256)
        below = d_ref[m][start + B : start + B + CHUNK, :].reshape(8, B, 256)
        mixed = ((1.0 - frac_p) * den + frac_p * below).reshape(CHUNK, 256)
        shifted = pltpu.roll(mixed, 248, 1)
        shifted = jnp.where(iota((CHUNK, 256), 1) >= 248, mixed, shifted)
        out = (1.0 - frac_q) * mixed.reshape(8, B, 256) + frac_q * shifted.reshape(8, B, 256)
        blocks = dot(slot_ref[...], out.reshape(CHUNK, 256).astype(BF16)).astype(BF16)
        blocks = blocks.reshape(NT, 32, 256)
        recv[2 * m + k, 0] = blocks[0]
        send[2 * m + k] = blocks
        for d in FAR:
            a_copy(2 * m + k, d).start()

    def last_stage(m):
        state(m, 0, FIRST)
        route_rows(m, 0)
        state(m, FIRST, H - FIRST)
        d_ref[m][H * B :, :] = jnp.concatenate(
            [d_ref[m][8:16, :], d_ref[m][H * B - 8 : H * B, :]], axis=0
        )
        route_rows(m, 1)

    def sum_stage(m, k):
        each(NT, lambda d: a_copy(2 * m + k, d).wait_recv())
        total = dot(sum_ref[...], recv[2 * m + k].reshape(512, 256))
        target[m, k, 0] = total.astype(BF16)
        for d in (2, 1, 3):
            y_copy(m, k, d).start()
            if m == 1 and k == 1:
                x_copy(m, k, d).start()
        x_copy(m, k, 0).start()

    def pass_stage(m, k):
        for d in (1, 3, 2):
            y_copy(m, k, d).wait_recv()
            if not (m == 1 and k == 1):
                x_copy(m, k, d).start()

    def stat_stage(k):
        for m in range(2):
            for d in range(NY):
                x_copy(m, k, d).wait_recv()
        for q in range(4):
            rows = slice(q * B, (q + 1) * B)
            values = [
                held[m, k, d, rows, :].astype(F32)
                for held in (target, other)
                for m in range(2)
                for d in range(NY)
            ]
            mean = functools.reduce(lambda a, b: a + b, values) * (1.0 / 16)
            squares = functools.reduce(lambda a, b: a + b, [(v - mean) * (v - mean) for v in values])
            spread = jnp.sqrt(squares / 15.0 + 1e-06)
            for half in range(2):
                row = half * H + k * 8
                mean_ref[q, row : row + 8, :] = mean[half * 8 : half * 8 + 8]
                spread_ref[q, row : row + 8, :] = spread[half * 8 : half * 8 + 8]

    east_west(0)
    fine_next(0, 0)
    fine_next(0, H - 1)
    finish()
    send_edges(0)
    lift(1)
    north_south(a11, N, H)
    east_west(1)
    fine_next(1, 0)
    fine_next(1, H - 1)
    fine_next(1, 1)
    send_edges(1)
    fine_run(EARLY - 1)
    finish()
    coarse_level(0)
    last_stage(0)
    fine_next(1, EARLY + 1)
    fine_run(H - 3 - EARLY)
    finish()
    coarse_level(1)
    last_stage(1)

    for m in range(2):
        for b in range(B):
            start = m * 256 + (b % 8) * N + (b // 8) * H
            for side in range(2):
                den_ref[start : start + H, side * 128 : (side + 1) * 128] = by_row[
                    2 * m + side, pl.ds(b, H, stride=B), :
                ]
    store_den = pltpu.make_async_copy(den_ref, den_hbm, o_sem.at[0])
    store_den.start()

    for m in range(2):
        for k in range(2):
            sum_stage(m, k)
    pass_stage(0, 0)
    pass_stage(0, 1)
    pass_stage(1, 0)
    stat_stage(0)
    pass_stage(1, 1)
    stat_stage(1)
    store_mean = pltpu.make_async_copy(mean_ref, stat_hbm.at[0], o_sem.at[1])
    store_spread = pltpu.make_async_copy(spread_ref, stat_hbm.at[1], o_sem.at[2])
    store_mean.start()
    store_spread.start()
    for k in range(4):
        each(NT, lambda d: a_copy(k, d).wait_send())
    for m in range(2):
        for k in range(2):
            each(NY, lambda d: y_copy(m, k, d).wait_send())
            for d in range(NY):
                x_copy(m, k, d).wait_send()
    store_den.wait()
    store_mean.wait()
    store_spread.wait()


def on_device(
    noisy,
    timestep,
    seams,
    corner_list,
    route,
    target_block,
    frac,
    w_time,
    w_lift,
    w_fine,
    w_coarse,
    gain_fine,
    gain_coarse,
    gain_out,
    w_out,
):
    hbm = pl.BlockSpec(memory_space=pltpu.HBM)
    dma = pltpu.SemaphoreType.DMA
    den, stat = pl.pallas_call(
        kernel,
        out_shape=(
            jax.ShapeDtypeStruct((512, 256), F32),
            jax.ShapeDtypeStruct((2, 4, N, 256), F32),
        ),
        in_specs=[hbm] * 14,
        out_specs=(hbm, hbm),
        scratch_shapes=[
            pltpu.VMEM((512, 256), BF16),
            pltpu.VMEM((1, 2), jnp.int32),
            pltpu.VMEM((3, 4, 8), jnp.int32),
            pltpu.VMEM((1, 128), jnp.int32),
            pltpu.VMEM((1, 128), jnp.int32),
            pltpu.VMEM((2, 8), F32),
            pltpu.VMEM((128, 128), F32),
            pltpu.VMEM((8, 128), BF16),
            pltpu.VMEM((9, 128, 128), BF16),
            pltpu.VMEM((9, 128, 128), BF16),
            pltpu.VMEM((1, 128), F32),
            pltpu.VMEM((1, 128), F32),
            pltpu.VMEM((1, 128), F32),
            pltpu.VMEM((8, 128), BF16),
            pltpu.VMEM((512, 256), BF16),
            pltpu.VMEM((512, 256), BF16),
            pltpu.VMEM((8, 128, 256), BF16),
            pltpu.VMEM((2048, 128), BF16),
            pltpu.VMEM((1536, 256), BF16),
            pltpu.VMEM((1536, 256), BF16),
            pltpu.VMEM((256, 256), BF16),
            pltpu.VMEM((4, 256, 256), BF16),
            pltpu.VMEM((512, 128), BF16),
            pltpu.VMEM((64, 512), BF16),
            pltpu.VMEM((2, 512, 128), BF16),
        ]
        + [pltpu.VMEM((N, 256, 128), BF16)] * 2
        + [pltpu.VMEM((N + 2, 288, 128), BF16)] * 2
        + [pltpu.VMEM((N, 256, 128), BF16)] * 2
        + [pltpu.VMEM((H, 128, 128), BF16)] * 2
        + [pltpu.VMEM((H + 2, 160, 128), BF16)] * 2
        + [pltpu.VMEM((H, 128, 128), BF16)] * 2
        + [
            pltpu.VMEM((2, 2, 128, 128), BF16),
            pltpu.VMEM((2, 2, 128, 128), BF16),
            pltpu.VMEM((256, 256), F32),
            pltpu.VMEM((256, 256), F32),
            pltpu.VMEM((FIRST * B, 4096), BF16),
            pltpu.VMEM(((H + 1) * B, 256), F32),
            pltpu.VMEM(((H + 1) * B, 256), F32),
            pltpu.VMEM((4, 256, 128), F32),
            pltpu.VMEM((512, 256), F32),
            pltpu.VMEM((4, N, 256), F32),
            pltpu.VMEM((4, N, 256), F32),
            pltpu.VMEM((4, NT, 32, 256), BF16),
            pltpu.VMEM((4, NT, 32, 256), BF16),
            pltpu.VMEM((2, 2, NY, 64, 256), BF16),
            pltpu.VMEM((2, 2, NY, 64, 256), BF16),
            dma((14,)),
            dma((3,)),
            dma((2,)),
            dma((2,)),
            dma((2, 2)),
            dma((2, 2)),
            dma((4, NT)),
            dma((4, NT)),
            dma((4, NY)),
            dma((4, NY)),
            dma((4, NY)),
            dma((4, NY)),
        ],
        compiler_params=pltpu.CompilerParams(
            collective_id=0, has_side_effects=True, vmem_limit_bytes=56 * 1024 * 1024
        ),
    )(
        noisy.reshape(512, 256),
        timestep.reshape(1, 2),
        seams.transpose(2, 1, 0),
        route.reshape(1, 128),
        target_block.reshape(1, 128),
        frac.T,
        w_time,
        w_lift,
        w_fine,
        w_coarse,
        gain_fine.reshape(1, 128),
        gain_coarse.reshape(1, 128),
        gain_out.reshape(1, 128),
        w_out.T,
    )
    return (den.reshape(noisy.shape), stat[0], stat[1])


def solution(mesh):
    placed = (
        P("mem", "tile", None, None),
        P("mem"),
        P("tile", None, None),
        P("tile", None, None),
        P(),
        P(),
        P("tile", None),
        P(),
        P(),
        P(),
        P(),
        P(),
        P(),
        P(),
        P(),
    )
    return jax.shard_map(
        on_device,
        mesh=mesh,
        in_specs=placed,
        out_specs=(P("mem", "tile", None, None), P("tile", None, None), P("tile", None, None)),
        check_vma=False,
    )
```
